256 devices in a mesh: dp: 4 (over z_hi), shard: 64 (over y, z_lo, x, core).
Axes of the slice: x: 4, y: 4, z: 8 (z_hi: 4, z_lo: 2; z = z_hi * 2 + z_lo), core: 2. Of those that a mesh axis runs over, the one named last changes fastest.
Arguments:
- block_input: bfloat16 [512, 14, 14, 1584], P(('dp', 'shard')), may hold values from -16 to 16
- upstream: bfloat16 [512, 14, 14, 1584], P(('dp', 'shard')), may hold values from -8 to 8
- kernel_tiles: bfloat16 [256, 13068], P('shard'), may hold values from -0.1875 to 0.1875
- tile_counts: int32 [64], replicated, may hold values from 1 to 4, 144 in all
- owner_order: int32 [64], replicated, may hold values from 0 to 63, each once
- gain: float32 [1584], replicated, may hold values from 0.5 to 1.5
- bias: float32 [1584], replicated, may hold values from -2.5 to 2.5
Outputs:
- block_out: bfloat16 [512, 14, 14, 1584], P(('dp', 'shard'))
- input_grad: bfloat16 [512, 14, 14, 1584], P(('dp', 'shard'))
- kernel_grad: float32 [1881792], P('shard')
- gain_grad: float32 [1584], replicated
- bias_grad: float32 [1584], replicated
The draws below stay inside these ranges and needn't reach their ends.
Inputs may be any that keep to these rules, and one draw needn't show every extreme that they name: `tile_counts`: entry k is the number of kernel tiles held by the k-th rank of the owner order; the entries sum to 144. `owner_order`: every shard index appears once.
All inputs are finite; a program needn't handle non-finite values.
Results may differ from the reference program's by a relative error of at most 0.019.
Values may be sent and summed in bfloat16 or wider, within the bound.
A program may use at most 192 MiB of HBM per device.

```python
import math
import jax
import jax.numpy as jnp
import numpy as np
from jax import lax

C = 1584
GW = 132
HH = 14
WW = 14
TILE = 13068
IMG_DEV = 2
GROUPS = 12
KSIZE = 1881792
NT = 144
CAP = 4
IMAGES = 512
N_DP = 4
N_SHARD = 64


def image_ramp(total_images):
    ramped = jnp.arange(total_images, dtype=jnp.float32) / max(total_images - 1, 1)
    return 0.6 * jnp.exp(ramped * math.log(3.0))


def draw_block_input(key, part):
    key = jax.random.fold_in(key, 11)
    key_noise, key_common, key_pixel = jax.random.split(key, 3)
    full_shape = (IMAGES, HH, WW, C)
    jitter = jnp.clip(jax.random.normal(key_noise, full_shape, jnp.float32), -4.0, 4.0)
    common = 0.5 * jnp.clip(jax.random.normal(key_common, (C,), jnp.float32), -3.0, 3.0)
    pixel_scale = jnp.exp(jax.random.uniform(key_pixel, (IMAGES, HH, WW, 1), jnp.float32, math.log(0.4), math.log(1.6)))
    ramped = image_ramp(IMAGES)[:, None, None, None]
    return (ramped * pixel_scale * (jitter + common)).astype(jnp.bfloat16)


def draw_upstream(key, part):
    key = jax.random.fold_in(key, 23)
    key_noise = jax.random.fold_in(key, 0)
    full_shape = (IMAGES, HH, WW, C)
    jitter = jnp.clip(jax.random.normal(key_noise, full_shape, jnp.float32), -4.0, 4.0)
    ramped = image_ramp(IMAGES)[:, None, None, None]
    return (ramped * jitter).astype(jnp.bfloat16)


def block_levels(rng, shape, shards, low, high):
    def one(dim, shards_of):
        steps = jax.random.uniform(jax.random.fold_in(jax.random.fold_in(rng, 6), dim), (shards_of,), jnp.float32, low / len(shards), high / len(shards))
        return jnp.repeat(jnp.exp(steps), shape[dim] // shards_of).reshape((-1,) + (1,) * (len(shape) - dim - 1))

    loudness = one(*shards[0])
    for cut in shards[1:]:
        loudness = loudness * one(*cut)
    return loudness


def split_up(count, total, limit, skew):
    portions = [(1 << 20) // math.isqrt(grade ** skew) + 1 for grade in range(2, count + 1)]
    rest, counts = total - limit - (count - 1), [1] * (count - 1)
    while rest > 0:
        candidates = [i for i in range(count - 1) if counts[i] < limit]
        whole, remaining = sum([portions[i] for i in candidates]), rest
        for i in candidates:
            extra = min(limit - counts[i], max(1, remaining * portions[i] // whole), rest)
            counts[i] = counts[i] + extra
            rest = rest - extra
    return np.array([limit] + counts)


def ragged(stream_key, amount, total, reach, slope):
    if amount == 2:
        one = jax.random.randint(stream_key, (), max(1, total - reach), min(reach, total - 1) + 1)
        return jnp.stack([one, total - one])
    tallies = jnp.asarray(split_up(amount, total, reach, slope), jnp.int32)
    couples = (amount - 1) // 2
    donor, sink = tallies[1:1 + 2 * couples:2], tallies[2:2 + 2 * couples:2]
    margin = jnp.minimum(donor - 1, reach - sink)
    moved = jax.random.randint(jax.random.fold_in(stream_key, 1), (couples,), 0, 1 << 20) % (margin + 1)
    tallies = tallies.at[1:1 + 2 * couples:2].set(donor - moved).at[2:2 + 2 * couples:2].set(sink + moved)
    return tallies[jax.random.permutation(jax.random.fold_in(stream_key, 2), amount)]


def scatter_about(own_key, shape, scale, most, pieces=(), kind=jnp.bfloat16):
    result = scale * jax.random.normal(own_key, shape, jnp.float32)
    if pieces:
        result = result * block_levels(own_key, shape, pieces, -0.22, 0.18)
    return jnp.clip(result, -most, most).astype(kind)


def setup_inputs(seed: int = 0) -> dict:
    splits = jax.random.split(jax.random.key(seed), 8)
    block_input = draw_block_input(jax.random.fold_in(splits[7], 71), 0)
    upstream = draw_upstream(jax.random.fold_in(splits[7], 71), 0)
    kernel_tiles = scatter_about(splits[2], (N_SHARD * CAP, TILE), (9 * GW) ** -0.5, 0.1875, ((0, 64),))
    tile_counts = ragged(splits[3], N_SHARD, NT, CAP, 2).astype(jnp.int32)
    owner_order = jax.random.permutation(splits[4], N_SHARD).astype(jnp.int32)
    gain = jnp.clip(1.0 + 0.1 * jax.random.normal(splits[5], (C,), jnp.float32), 0.5, 1.5)
    bias = scatter_about(splits[6], (C,), 0.5, 2.5, (), jnp.float32)
    return {"block_input": block_input, "upstream": upstream, "kernel_tiles": kernel_tiles, "tile_counts": tile_counts, "owner_order": owner_order, "gain": gain, "bias": bias}


EPSILON = 1e-05

def tile_rows(tile_counts, owner_order, capacity, total_tiles):
    ranks_total = tile_counts.shape[0]
    run_start = (jnp.cumsum(tile_counts) - tile_counts).astype(jnp.int32)
    run_end = (run_start + tile_counts).astype(jnp.int32)
    tile_ids = jnp.arange(total_tiles, dtype=jnp.int32)
    rank_of = lax.optimization_barrier(jnp.sum((run_end[None, :] <= tile_ids[:, None]).astype(jnp.int32), axis=1)).astype(jnp.int32)
    onehot = (rank_of[:, None] == jnp.arange(ranks_total, dtype=jnp.int32)[None, :]).astype(jnp.int32)
    holder = lax.optimization_barrier(jnp.sum(onehot * owner_order[None, :], axis=1)).astype(jnp.int32)
    begins = lax.optimization_barrier(jnp.sum(onehot * run_start[None, :], axis=1)).astype(jnp.int32)
    return (holder * capacity + tile_ids - begins).astype(jnp.int32)

def silu_slope(values):
    sigma = jax.nn.sigmoid(values)
    return sigma * (1.0 + values * (1.0 - sigma))

def conv_forward(images, kernel):
    number, height, breadth, channels = images.shape
    groups, group_width = (kernel.shape[0], kernel.shape[2])
    padded = jnp.pad(images.astype(jnp.float32), ((0, 0), (1, 1), (1, 1), (0, 0)))
    weights = kernel.astype(jnp.float32)
    totals = jnp.zeros((number, height, breadth, groups, group_width), jnp.float32)
    for position in range(9):
        row_off, col_off = (position // 3, position % 3)
        window = padded[:, row_off:row_off + height, col_off:col_off + breadth, :]
        window = window.reshape(number, height, breadth, groups, group_width)
        totals = totals + jnp.einsum('nhwgi,gio->nhwgo', window, weights[:, position])
    return totals.reshape(number, height, breadth, channels)

def conv_backward(grad_maps, kernel):
    number, height, breadth, channels = grad_maps.shape
    groups, group_width = (kernel.shape[0], kernel.shape[2])
    padded = jnp.pad(grad_maps.astype(jnp.float32), ((0, 0), (1, 1), (1, 1), (0, 0)))
    weights = kernel.astype(jnp.float32)
    totals = jnp.zeros((number, height, breadth, groups, group_width), jnp.float32)
    for position in range(9):
        row_off, col_off = (position // 3, position % 3)
        window = padded[:, 2 - row_off:2 - row_off + height, 2 - col_off:2 - col_off + breadth, :]
        window = window.reshape(number, height, breadth, groups, group_width)
        totals = totals + jnp.einsum('nhwgo,gio->nhwgi', window, weights[:, position])
    return totals.reshape(number, height, breadth, channels)

def kernel_term(images, grad_maps, groups):
    number, height, breadth, channels = images.shape
    group_width = channels // groups
    padded = jnp.pad(images.astype(jnp.float32), ((0, 0), (1, 1), (1, 1), (0, 0)))
    shaped = grad_maps.astype(jnp.float32).reshape(number, height, breadth, groups, group_width)
    tap_terms = []
    for position in range(9):
        row_off, col_off = (position // 3, position % 3)
        window = padded[:, row_off:row_off + height, col_off:col_off + breadth, :]
        window = window.reshape(number, height, breadth, groups, group_width)
        tap_terms.append(jnp.einsum('nhwgi,nhwgo->gio', window, shaped))
    return jnp.stack(tap_terms, axis=1)

def reference(block_input, upstream, kernel_tiles, tile_counts, owner_order, gain, bias):
    row_index = tile_rows(tile_counts, owner_order, CAP, NT)
    kernel = kernel_tiles[row_index].reshape(GROUPS, 9, GW, GW)
    blocks_total = N_DP * N_SHARD
    input_blocks = block_input.reshape(blocks_total, IMG_DEV, HH, WW, C)
    hidden = lax.map(lambda block_images: conv_forward(block_images, kernel).astype(jnp.bfloat16), input_blocks)
    hidden = hidden.reshape(IMAGES, HH, WW, C)
    values = lax.optimization_barrier(hidden).astype(jnp.float32)
    row_total = IMAGES * HH * WW
    average = lax.optimization_barrier(jnp.sum(values, axis=(0, 1, 2))) / row_total
    second = lax.optimization_barrier(jnp.sum(values * values, axis=(0, 1, 2))) / row_total
    inv_std = lax.rsqrt(second - average * average + EPSILON)
    normed = (values - average) * inv_std
    affine = gain * normed + bias
    summed = block_input.astype(jnp.float32) + jax.nn.silu(affine)
    block_out = jax.nn.silu(summed).astype(jnp.bfloat16)
    grad_sum = upstream.astype(jnp.float32) * silu_slope(summed)
    grad_affine = grad_sum * silu_slope(affine)
    gain_grad = lax.optimization_barrier(jnp.sum(grad_affine * normed, axis=(0, 1, 2)))
    bias_grad = lax.optimization_barrier(jnp.sum(grad_affine, axis=(0, 1, 2)))
    grad_hidden = (gain * inv_std * (grad_affine - bias_grad / row_total - normed * gain_grad / row_total)).astype(jnp.bfloat16)
    grad_blocks = grad_hidden.reshape(blocks_total, IMG_DEV, HH, WW, C)
    backward = lax.map(lambda block_grads: conv_backward(block_grads, kernel), grad_blocks)
    input_grad = (grad_sum + backward.reshape(IMAGES, HH, WW, C)).astype(jnp.bfloat16)

    def accumulate(running, inputs_pair):
        block_term = kernel_term(inputs_pair[0], inputs_pair[1], GROUPS).astype(jnp.bfloat16)
        return (running + lax.optimization_barrier(block_term).astype(jnp.float32), None)
    kernel_grad, unused = lax.scan(accumulate, jnp.zeros((GROUPS, 9, GW, GW), jnp.float32), (input_blocks, grad_blocks))
    return (block_out, input_grad, kernel_grad.reshape(KSIZE), gain_grad, bias_grad)
```

```python
import numpy as np
import jax
import jax.numpy as jnp
from jax import lax
from jax.experimental import pallas as pl
from jax.experimental.pallas import tpu as pltpu
from jax.sharding import PartitionSpec as P

GROUPS = 12
GW = 132
ROWS = 448
LANES = 1664
BF = jnp.bfloat16
F32 = jnp.float32
EPSILON = 1e-05
TOTAL = 100352
VLIM = 60 * 1024 * 1024


def extra_lane(g, a):
    return 16 * (g // 3) + 4 * (g % 3) + a


def constants():
    pg = np.zeros((GROUPS, 256, 256), np.float32)
    for g in range(GROUPS):
        for j in range(GW):
            a, l = j // 33, j % 33
            pg[g, 4 * g + j, 32 * a + l if l < 32 else 128 + extra_lane(g, a)] = 1
    ry = np.zeros((9, 128, 4, 128), np.float32)
    for g in range(GROUPS):
        for tap in range(9):
            for a in range(4):
                ry[tap, extra_lane(g, a), g // 3, 36 * (g % 3) + 4 * tap + a] = 1
    selm = np.zeros((GROUPS, 16, 128), np.float32)
    for g in range(GROUPS):
        for a in range(4):
            selm[g, 3 + a, extra_lane(g, a)] = 1
    sele = np.zeros((2, 3, 128, 12, 16), np.float32)
    selb = np.zeros((2, 3, 9, 16, 12, 16), np.float32)
    for gg in range(3):
        for u in range(36):
            q, j = u // 3, u % 3
            tap, a = u // 4, u % 4
            for kind, row in ((0, j), (1, 7 + j)):
                sele[kind, gg, 36 * gg + u, q, row] = 1
                selb[kind, gg, tap, 4 * gg + a, q, row] = 1
    bf = lambda v, *s: jnp.asarray(v.reshape(s), BF)
    return dict(
        pg=bf(pg, GROUPS, 256, 256),
        ry=bf(ry, 1152, 512),
        selm=bf(selm, 192, 128),
        sele=bf(sele, 2, 3, 128, 192),
        selb=bf(selb, 2, 3, 144, 192),
    )


def prep_constants():
    cs = np.zeros((GW, 128), np.float32)
    cse = np.zeros((GW, 112), np.float32)
    csee = np.zeros((GW, 128), np.float32)
    rs = np.zeros((112, 99), np.float32)
    rsm = np.zeros((99, 128), np.float32)
    rse = np.zeros((112, 99), np.float32)
    for a in range(4):
        for l in range(32):
            cs[33 * a + l, 32 * a + l] = 1
        cse[33 * a + 32, 99 + a] = 1
    for lane in range(128):
        csee[33 * (lane % 4) + 32, lane] = 1
    for j in range(3):
        for l in range(32):
            rs[32 * j + l, 33 * j + l] = 1
            rsm[33 * j + l, 32 * j + l] = 1
        rs[96 + j, 33 * j + 32] = 1
        rse[103 + j, 33 * j + 32] = 1
    return [jnp.asarray(v, BF) for v in (cs, cse, csee, rs, rsm, rse)]


def dot(a, b, dims=((1,), (0,))):
    return lax.dot_general(a, b, (dims, ((), ())), preferred_element_type=F32)


def prep_body(tile_ref, cs, cse, csee, rs, rsm, rse, out_ref):
    for s in range(4):
        t = tile_ref[s]
        u = dot(t, cs[...]).astype(BF)
        ue = dot(t, cse[...]).astype(BF)
        uee = dot(t, csee[...]).astype(BF)
        v = dot(rs[...], u) + dot(ue, rsm[...], ((0,), (0,))) + dot(rse[...], uee)
        out_ref[s] = v.astype(BF)


def prep(tiles):
    return pl.pallas_call(
        prep_body,
        out_shape=jax.ShapeDtypeStruct((4, 112, 128), BF),
        name="prep",
    )(tiles, *prep_constants())


def lanes_of(g, width=1):
    return pl.ds(pl.multiple_of(g * 128, 128), 128 * width)


def lane_iota(rows):
    return lax.broadcasted_iota(jnp.int32, (rows, 128), 1)


def load_native(src, xn):
    xn[...] = jnp.zeros_like(xn)
    for n in range(2):
        for y in range(14):
            xn[n * 14 + y, 0:14, 0:1584] = src[n, y]


def store_shifts(dst, main, lanes):
    for b in range(3):
        moved = main if b == 1 else pltpu.roll(main, (1 - b) % ROWS, 0)
        dst[b, :, 1:15, :, lanes] = moved.astype(BF).reshape(2, 14, 16, 128)


def zero_borders(dst):
    zeros = jnp.zeros((3, 2, 16, LANES), BF)
    dst[:, :, 0] = zeros
    dst[:, :, 15] = zeros


def tap_slice(src, tap, lanes, mirrored):
    a, b = tap // 3, tap % 3
    if mirrored:
        a, b = 2 - a, 2 - b
    return src[b, :, a : a + 14, :, lanes].reshape(ROWS, 128)


def tap_concat(src, lanes, mirrored, extra=None):
    pieces = [tap_slice(src, tap, lanes, mirrored) for tap in range(9)]
    if extra is not None:
        pieces.append(extra)
    return jnp.concatenate(pieces, axis=1)


def permute_in(xn, pg, sink, acc):
    acc[...] = jnp.zeros_like(acc)

    def step(g, carry):
        r = dot(xn[:, :, lanes_of(g, 2)].reshape(ROWS, 256), pg[g])
        sink(g, r[:, :128])
        acc[...] += r[:, 128:]
        return carry

    lax.fori_loop(0, GROUPS, step, 0)
    sink(GROUPS, acc[...])


def permute_out(src, pg, out_ref, on):
    def step(g, carry):
        pair = jnp.concatenate([src(g), src(GROUPS)], axis=1)
        r = dot(pair, pg[g], ((1,), (1,)))
        on[:, :, lanes_of(g)] = (carry + r[:, :128]).astype(BF).reshape(28, 16, 128)
        return r[:, 128:]

    carry = lax.fori_loop(0, GROUPS, step, jnp.zeros((ROWS, 128), F32))
    on[:, :, 1536:1664] = carry.astype(BF).reshape(28, 16, 128)
    for n in range(2):
        for y in range(14):
            out_ref[n, y] = on[n * 14 + y, 0:14, 0:1584]


def fwd_body(idx, x_ref, g_ref, pg, ry, selm, sele, xb, ex, hid, bm, ta, me, sums, xn, acc, bg):
    load_native(x_ref, xn)
    zero_borders(xb)
    permute_in(xn, pg, lambda g, v: store_shifts(xb, v, lanes_of(g)), acc)
    ex[...] = dot(tap_concat(xb, pl.ds(1536, 128), False), ry[...]).astype(BF)

    def pull(t, carry):
        g, q = t // 12, t % 12
        s = idx[t]
        bm[g, pl.ds(pl.multiple_of(q * 96, 32), 96), :] = g_ref[s, 0:96, :]
        ta[g, q] = g_ref[s, 96:112, :]
        return carry

    lax.fori_loop(0, 144, pull, 0)
    for q in range(12):
        m = dot(ta[:, q].reshape(192, 128), selm[...], ((0,), (0,)))
        me[96 * q : 96 * q + 96, :] = m[0:96].astype(BF)

    acc[...] = jnp.zeros_like(acc)
    valid = (lax.broadcasted_iota(jnp.int32, (ROWS, 128), 0) % 16) < 14

    def stat(h, lanes):
        h = jnp.where(valid, h.astype(F32), 0.0)
        sums[0:1, lanes] = jnp.sum(h, axis=0, keepdims=True)
        sums[1:2, lanes] = jnp.sum(h * h, axis=0, keepdims=True)

    def step(g, carry):
        gg = g % 3
        mine = (lane_iota(1152) // 4) == (g // 3) * 4 + gg
        bg[0:1152, 0:128] = bm[g]
        bg[0:1152, 128:256] = jnp.where(mine, me[...].astype(F32), 0.0).astype(BF)
        tails = ta[g].reshape(192, 128)
        bg[1152:1280, 0:128] = dot(sele[0, gg], tails).astype(BF)
        ee = jnp.where(mine[0:128], dot(sele[1, gg], tails), 0.0)
        bg[1152:1280, 128:256] = ee.astype(BF)
        a = tap_concat(xb, lanes_of(g), False, ex[:, lanes_of(g // 3)])
        r = dot(a, bg[...])
        h = r[:, :128].astype(BF)
        hid[:, lanes_of(g)] = h
        stat(h, lanes_of(g))
        acc[...] += r[:, 128:]
        return carry

    lax.fori_loop(0, GROUPS, step, 0)
    h = acc[...].astype(BF)
    hid[:, 1536:1664] = h
    stat(h, pl.ds(1536, 128))


SM = pltpu.SMEM
VM = pltpu.VMEM


def vspec():
    return pl.BlockSpec(memory_space=VM)


def sspec():
    return pl.BlockSpec(memory_space=SM)


def struct(shape, dtype):
    return jax.ShapeDtypeStruct(shape, dtype)


def fwd(idx, x, gathered, c):
    return pl.pallas_call(
        fwd_body,
        in_specs=[sspec()] + [vspec()] * 6,
        out_specs=[vspec()] * 7,
        out_shape=[
            struct((3, 2, 16, 16, LANES), BF),
            struct((ROWS, 512), BF),
            struct((ROWS, LANES), BF),
            struct((GROUPS, 1152, 128), BF),
            struct((GROUPS, 12, 16, 128), BF),
            struct((1152, 128), BF),
            struct((2, LANES), F32),
        ],
        scratch_shapes=[
            VM((28, 16, LANES), BF),
            VM((ROWS, 128), F32),
            VM((1280, 256), BF),
        ],
        compiler_params=pltpu.CompilerParams(vmem_limit_bytes=VLIM),
        name="fwd",
    )(idx, x, gathered, c["pg"], c["ry"], c["selm"], c["sele"])


def half_tanh(v):
    return 0.5 * jnp.tanh(0.5 * v) + 0.5


def norm_body(up_ref, xb, hid, sums, par, pg, out_ref, gs, ga, gsum, xn, on, upp, bo, acc):
    load_native(up_ref, xn)

    def keep(g, v):
        upp[:, lanes_of(g)] = v.astype(BF)

    permute_in(xn, pg, keep, acc)

    def tile(t, carry):
        lanes = lanes_of(t)
        avg = sums[0:1, lanes] / TOTAL
        inv = lax.rsqrt(sums[1:2, lanes] / TOTAL - avg * avg + EPSILON)
        gain, bias = par[0:1, lanes], par[1:2, lanes]
        s1 = jnp.zeros((8, 128), F32)
        s2 = jnp.zeros((8, 128), F32)
        for k in range(28):
            rows = pl.ds(16 * k, 16)
            n, y = k // 14, k % 14
            x = xb[1, n, y + 1, :, lanes].astype(F32)
            normed = (hid[rows, lanes].astype(F32) - avg) * inv
            aff = gain * normed + bias
            sa = half_tanh(aff)
            act = aff * sa
            summed = x + act
            ss = half_tanh(summed)
            out = summed * ss
            bo[rows, lanes] = out.astype(BF)
            gsv = upp[rows, lanes].astype(F32) * (ss + out * (1.0 - ss))
            gav = gsv * (sa + act * (1.0 - sa))
            gs[rows, lanes] = gsv
            ga[rows, lanes] = gav
            p = gav * normed
            s1 = s1 + (p[0:8] + p[8:16])
            s2 = s2 + (gav[0:8] + gav[8:16])
        gsum[0:1, lanes] = jnp.sum(s1, axis=0, keepdims=True)
        gsum[1:2, lanes] = jnp.sum(s2, axis=0, keepdims=True)
        return carry

    lax.fori_loop(0, 13, tile, 0)
    permute_out(lambda g: bo[:, lanes_of(g)], pg, out_ref, on)


def norm(up, xb, hid, sums, par, c):
    return pl.pallas_call(
        norm_body,
        in_specs=[vspec()] * 6,
        out_specs=[vspec()] * 4,
        out_shape=[
            struct((2, 14, 14, 1584), BF),
            struct((ROWS, LANES), F32),
            struct((ROWS, LANES), F32),
            struct((2, LANES), F32),
        ],
        scratch_shapes=[
            VM((28, 16, LANES), BF),
            VM((28, 16, LANES), BF),
            VM((ROWS, LANES), BF),
            VM((ROWS, LANES), BF),
            VM((ROWS, 128), F32),
        ],
        compiler_params=pltpu.CompilerParams(vmem_limit_bytes=VLIM),
        name="norm",
    )(up, xb, hid, sums, par, c["pg"])


def piece_of(b):
    one = lambda cond: jnp.where(cond, 1, 0)
    late = b >= 13
    xa = one(b >= 3) + one(b >= 7) + one(b >= 10)
    xl = one(b >= 17) + one(b >= 20) + one(b >= 24)
    sa = 3 * one(b >= 3) + 4 * one(b >= 7) + 3 * one(b >= 10)
    sl = 13 + 4 * one(b >= 17) + 3 * one(b >= 20) + 4 * one(b >= 24)
    first = jnp.where(xl == 1, 4, 3)
    x = jnp.where(late, xl, xa)
    pos = jnp.where(late, b - sl + first, b - sa)
    return x, pos


def back_body(hid, sums, gsum, par, gs, ga, xb, ex, bm, ta, me, pg, ry, selb, ig_ref, st,
              ghb, eg, tr, wt, tot, acc, on, mec):
    zero_borders(ghb)
    valid = (lax.broadcasted_iota(jnp.int32, (ROWS, 128), 0) % 16) < 14

    def tile(t, carry):
        lanes = lanes_of(t)
        avg = sums[0:1, lanes] / TOTAL
        inv = lax.rsqrt(sums[1:2, lanes] / TOTAL - avg * avg + EPSILON)
        scale = par[0:1, lanes] * inv
        c1 = gsum[1:2, lanes] / TOTAL
        c2 = gsum[0:1, lanes] / TOTAL
        normed = (hid[:, lanes].astype(F32) - avg) * inv
        gh = scale * (ga[:, lanes] - c1 - normed * c2)
        gh = jnp.where(valid, gh, 0.0)
        store_shifts(ghb, gh, lanes)
        return carry

    lax.fori_loop(0, 13, tile, 0)
    eg[...] = dot(tap_concat(ghb, pl.ds(1536, 128), True), ry[...]).astype(BF)
    g12 = ghb[1, :, 1:15, :, pl.ds(1536, 128)].reshape(ROWS, 128)
    g12t = g12.astype(F32).T.astype(BF)

    for yy in range(4):
        acc[...] = jnp.zeros_like(acc)
        mec[...] = jnp.zeros_like(mec)
        lhs12 = g12t[16 * yy : 16 * yy + 16]

        def wstep(gg, carry):
            g = 3 * yy + gg
            main = ghb[1, :, 1:15, :, lanes_of(g)].reshape(ROWS, 128)
            lhs = jnp.concatenate([main.astype(F32).T.astype(BF), lhs12], axis=0)
            a = tap_concat(xb, lanes_of(g), False, ex[:, pl.ds(128 * yy, 128)])
            r = dot(lhs, a)
            for tap in range(9):
                x, pos = piece_of(gg * 9 + tap)
                blk = r[0:128, tap * 128 : tap * 128 + 128].astype(BF)
                at = pl.ds(pl.multiple_of(pos * 64, 64), 64)
                st[0, yy, x, at, :] = blk[0:64]
                st[1, x, yy, at, :] = blk[64:128]
            rowsel = (lax.broadcasted_iota(jnp.int32, (16, 1152), 0) // 4) == gg
            mec[...] += jnp.where(rowsel, r[128:144, 0:1152], 0.0)
            lane = lane_iota(144)
            lanesel = (lane >= 36 * gg) & (lane < 36 * gg + 36)
            rowsel2 = lax.broadcasted_iota(jnp.int32, (144, 128), 0)
            rowsel2 = (rowsel2 < 128) | (rowsel2 // 4 == 32 + gg)
            acc[0:144, :] += jnp.where(lanesel & rowsel2, r[:, 1152:1280], 0.0)
            return carry

        lax.fori_loop(0, 3, wstep, 0)
        blocks = [mec[:, 128 * tap : 128 * tap + 128].astype(BF) for tap in range(9)]
        eb = acc[0:144, :].astype(BF)
        zeros = jnp.zeros((64, 128), BF)
        for x in range(3):
            for k in range(3):
                st[0, yy, x, 448 + 16 * k : 464 + 16 * k, :] = blocks[3 * x + k]
            st[1, x, yy, 448:496, :] = eb[48 * x : 48 * x + 48]
            st[0, yy, x, 496:512, :] = zeros[0:16]
            st[1, x, yy, 496:512, :] = zeros[0:16]
        for h in range(2):
            st[h, (3 if h else yy), (yy if h else 3), 384:448, :] = zeros
            st[h, (3 if h else yy), (yy if h else 3), 448:512, :] = zeros

    tr_in = jnp.concatenate([me[128 * tap : 128 * tap + 128] for tap in range(9)], axis=1)
    tr[...] = dot(tr_in, ry[...]).astype(BF)
    tot[:, 1536:1664] = gs[:, 1536:1664]

    for yy in range(4):
        wt[128:256, :] = jnp.zeros((128, 1280), BF)

        def bstep(gg, carry):
            g = 3 * yy + gg
            for tap in range(9):
                wt[0:128, 128 * tap : 128 * tap + 128] = bm[g, 128 * tap : 128 * tap + 128, :]
            lane = lane_iota(128)
            lanesel = (lane >= 36 * gg) & (lane < 36 * gg + 36)
            wt[0:128, 1152:1280] = jnp.where(lanesel, tr[:, 128 * yy : 128 * yy + 128].astype(F32), 0.0).astype(BF)
            tails = ta[g].reshape(192, 128)
            bl = dot(selb[0, gg], tails).astype(BF)
            be = dot(selb[1, gg], tails)
            low = jnp.zeros((16, 128), F32)
            lane = lane_iota(16)
            for tap in range(9):
                wt[128 + 16 * yy : 144 + 16 * yy, 128 * tap : 128 * tap + 128] = bl[16 * tap : 16 * tap + 16]
                low = jnp.where((lane // 4) == 9 * gg + tap, be[16 * tap : 16 * tap + 16], low)
            wt[128 + 16 * yy : 144 + 16 * yy, 1152:1280] = low.astype(BF)
            a = tap_concat(ghb, lanes_of(g), True, eg[:, pl.ds(128 * yy, 128)])
            r = dot(a, wt[...], ((1,), (1,)))
            tot[:, lanes_of(g)] = gs[:, lanes_of(g)] + r[:, :128]
            tot[:, 1536:1664] += r[:, 128:]
            return carry

        lax.fori_loop(0, 3, bstep, 0)
    permute_out(lambda g: tot[:, lanes_of(g)].astype(BF), pg, ig_ref, on)


def back(hid, sums, gsum, par, gs, ga, xb, ex, bm, ta, me, c):
    return pl.pallas_call(
        back_body,
        in_specs=[vspec()] * 14,
        out_specs=[vspec()] * 2,
        out_shape=[
            struct((2, 14, 14, 1584), BF),
            struct((2, 4, 4, 512, 128), BF),
        ],
        scratch_shapes=[
            VM((3, 2, 16, 16, LANES), BF),
            VM((ROWS, 512), BF),
            VM((128, 512), BF),
            VM((256, 1280), BF),
            VM((ROWS, LANES), F32),
            VM((ROWS, 128), F32),
            VM((28, 16, LANES), BF),
            VM((16, 1152), F32),
        ],
        compiler_params=pltpu.CompilerParams(vmem_limit_bytes=VLIM),
        name="back",
    )(hid, sums, gsum, par, gs, ga, xb, ex, bm, ta, me, c["pg"], c["ry"], c["selb"])


def fin_constants():
    q_i = np.zeros((27, 256, 136), np.float32)
    q_o = np.zeros((3, 144, GW), np.float32)
    for gg in range(3):
        for a in range(4):
            for l in range(32):
                q_o[gg, 32 * a + l, 33 * a + l] = 1
                for tap in range(9):
                    q_i[gg * 9 + tap, 32 * a + l, 33 * a + l] = 1
            q_o[gg, 128 + 4 * gg + a, 33 * a + 32] = 1
            for tap in range(9):
                q_i[gg * 9 + tap, 128 + 36 * gg + 4 * tap + a, 33 * a + 32] = 1
    return jnp.asarray(q_i, BF), jnp.asarray(q_o, BF)


def fin_body(pos, h_ref, q_i, q_o, out_ref):
    b0 = pos[0]
    for k in range(3):
        b = b0 + k
        x, p = piece_of(b)
        tap = b % 9
        gg = b // 9
        at = pl.ds(pl.multiple_of(p * 64, 64), 64)
        main = jnp.concatenate([h_ref[0, x, at, :], h_ref[1, x, at, :]], axis=0)
        mrow = pl.ds(pl.multiple_of(448 + 16 * (tap % 3), 16), 16)
        me = h_ref[0, tap // 3, mrow, :]
        em = jnp.concatenate([h_ref[1, j, 448:496, :] for j in range(3)], axis=0)
        left = jnp.concatenate([main, me], axis=0)
        full = jnp.concatenate([left, em], axis=1)
        t1 = dot(full, q_i[b]).astype(BF)
        t2 = dot(t1, q_o[gg], ((0,), (0,)))
        out_ref[pl.ds(132 * k, 132), :] = t2[0:132]


def fin(pos, h):
    q_i, q_o = fin_constants()
    return pl.pallas_call(
        fin_body,
        in_specs=[sspec()] + [vspec()] * 3,
        out_specs=vspec(),
        out_shape=struct((396, GW), F32),
        compiler_params=pltpu.CompilerParams(vmem_limit_bytes=VLIM),
        name="fin",
    )(pos, h, q_i, q_o)


def channels_in(v):
    r = v.reshape(4, 3, 4, 33)
    main = r[..., :32].reshape(1536)
    extra = jnp.pad(r[..., 32].reshape(4, 12), ((0, 0), (0, 4))).reshape(64)
    return jnp.concatenate([main, extra, jnp.zeros((64,), v.dtype)])


def channels_out(v):
    main = v[:1536].reshape(4, 3, 4, 32)
    extra = v[1536:1600].reshape(4, 16)[:, :12].reshape(4, 3, 4, 1)
    return jnp.concatenate([main, extra], axis=-1).reshape(1584)
MESH = pl.DeviceIdType.MESH


def place():
    dp = lax.axis_index("dp")
    s = lax.axis_index("shard")
    return (s // 2) % 4, s // 16, dp * 2 + (s // 8) % 2, s % 2


def device(x, y, z, c):
    return (z // 2, y * 16 + (z % 2) * 8 + x * 2 + c)


def greet(devices):
    barrier = pltpu.get_barrier_semaphore()
    for d in devices:
        pl.semaphore_signal(barrier, inc=1, device_id=d, device_id_type=MESH)
    pl.semaphore_wait(barrier, len(devices))


def send(src, dst, send_sem, recv_sem, to):
    copy = pltpu.make_async_remote_copy(
        src_ref=src, dst_ref=dst, send_sem=send_sem, recv_sem=recv_sem,
        device_id=to, device_id_type=MESH,
    )
    copy.start()
    return copy


def remote_params(number):
    return pltpu.CompilerParams(
        collective_id=number, has_side_effects=True, vmem_limit_bytes=VLIM
    )


DMA = pltpu.SemaphoreType.DMA


def gather_body(pay, out, s_sib, r_sib, s_z, r_z, s_u, r_u, s_v, r_v, s_d, r_d):
    x, y, z, c = place()
    zl = z % 2
    oz = 1 - zl
    u = x * (1 - c) + y * c
    v = y * (1 - c) + x * c

    def at_u(k):
        k = (u + k) % 4
        return device(k * (1 - c) + x * c, y * (1 - c) + k * c, z, c)

    def at_v(k):
        k = (v + k) % 4
        return device(x * (1 - c) + k * c, k * (1 - c) + y * c, z, c)

    sib = device(x, y, z, 1 - c)
    zp, zm = device(x, y, (z + 1) % 8, c), device(x, y, (z + 7) % 8, c)
    greet([sib, zp, zm, at_u(1), at_u(3), at_v(1), at_v(3)])
    sends = []

    mine = out.at[c, v, u, zl, c]
    other = out.at[1 - c, u, v, zl, c]
    mine[...] = pay[pl.ds(2 * c, 2)]
    other[...] = pay[pl.ds(2 - 2 * c, 2)]
    sib_copy = send(other, other, s_sib.at[0], r_sib.at[0], sib)
    sends.append(sib_copy)
    sends.append(send(mine, mine, s_d.at[32], r_d.at[32], sib))
    sib_copy.wait_recv()

    a, b = out.at[c, v, u, zl, 0], out.at[c, v, u, zl, 1]
    z0 = send(a, a, s_z.at[0], r_z.at[0], zp)
    z1 = send(b, b, s_z.at[1], r_z.at[1], zm)
    sends += [z0, z1]

    def chunk(i, j, zz):
        return out.at[c, (v + i) % 4, (u + j) % 4, zz]

    def spread_u(n, zz):
        k = chunk(0, 0, zz)
        return [send(k, k, s_u.at[n, 0], r_u.at[n, 0], at_u(1)),
                send(k, k, s_u.at[n, 1], r_u.at[n, 1], at_u(3))]

    def spread_v(n, k):
        return [send(k, k, s_v.at[n, 0], r_v.at[n, 0], at_v(1)),
                send(k, k, s_v.at[n, 1], r_v.at[n, 1], at_v(3))]

    def pass_on(n, k):
        sends.append(send(k, k, s_d.at[n], r_d.at[n], sib))

    order = [(0, zl), (0, oz), (3, zl), (1, zl), (3, oz), (1, oz), (2, zl), (2, oz)]
    ring_u, ring_v = {}, {}

    ring_u[0] = spread_u(0, zl)
    ring_v[0] = spread_v(0, chunk(0, 0, zl))
    z0.wait_recv()
    z1.wait_recv()
    ring_u[1] = spread_u(1, oz)
    ring_v[1] = spread_v(1, chunk(0, 0, oz))
    pass_on(1, chunk(0, 0, oz))
    sends += ring_u[0] + ring_u[1] + ring_v[0] + ring_v[1]
    half_u = {}
    for n, zz in ((0, zl), (1, oz)):
        ring_u[n][0].wait_recv()
        k = chunk(0, 3, zz)
        h0 = send(k.at[0], k.at[0], s_u.at[n, 2], r_u.at[n, 2], at_u(1))
        ring_v[2 + 2 * n] = spread_v(2 + 2 * n, k)
        pass_on(2 + 2 * n, k)
        ring_u[n][1].wait_recv()
        k = chunk(0, 1, zz)
        h1 = send(k.at[1], k.at[1], s_u.at[n, 3], r_u.at[n, 3], at_u(3))
        ring_v[3 + 2 * n] = spread_v(3 + 2 * n, k)
        pass_on(3 + 2 * n, k)
        sends += [h0, h1] + ring_v[2 + 2 * n] + ring_v[3 + 2 * n]
        half_u[n] = (h0, h1)
    for n, zz in ((0, zl), (1, oz)):
        half_u[n][0].wait_recv()
        half_u[n][1].wait_recv()
        k = chunk(0, 2, zz)
        ring_v[6 + n] = spread_v(6 + n, k)
        pass_on(6 + n, k)
        sends += ring_v[6 + n]
    half_v = {}
    for n, (j, zz) in enumerate(order):
        ring_v[n][0].wait_recv()
        k = chunk(3, j, zz)
        h0 = send(k.at[0], k.at[0], s_v.at[n, 2], r_v.at[n, 2], at_v(1))
        pass_on(8 + n, k)
        ring_v[n][1].wait_recv()
        k = chunk(1, j, zz)
        h1 = send(k.at[1], k.at[1], s_v.at[n, 3], r_v.at[n, 3], at_v(3))
        pass_on(16 + n, k)
        sends += [h0, h1]
        half_v[n] = (h0, h1)
    for n, (j, zz) in enumerate(order):
        half_v[n][0].wait_recv()
        half_v[n][1].wait_recv()
        pass_on(24 + n, chunk(2, j, zz))
    for copy in sends:
        copy.wait_send()
    for n in list(range(1, 32)):
        k = out.at[1 - c, 0, 0, 0]
        pltpu.make_async_remote_copy(
            src_ref=k, dst_ref=k, send_sem=s_d.at[n], recv_sem=r_d.at[n],
            device_id=sib, device_id_type=MESH,
        ).wait_recv()
    sends[1].wait_recv()


def gather_tiles(pay):
    return pl.pallas_call(
        gather_body,
        in_specs=[vspec()],
        out_specs=vspec(),
        out_shape=struct((2, 4, 4, 2, 2, 2, 112, 128), BF),
        scratch_shapes=[
            DMA((1,)), DMA((1,)), DMA((2,)), DMA((2,)), DMA((2, 4)), DMA((2, 4)),
            DMA((8, 4)), DMA((8, 4)), DMA((33,)), DMA((33,)),
        ],
        compiler_params=remote_params(1),
        name="gather_tiles",
    )(pay)


def partners(x, y, z, c):
    out = [device(x, y, z, 1 - c)]
    out += [device((x + r) % 4, y, z, c) for r in range(1, 4)]
    out += [device(x, (y + r) % 4, z, c) for r in range(1, 4)]
    out += [device(x, y, (z + r) % 8, c) for r in range(1, 8)]
    return out


def reduce_body(v_ref, out_ref, b0, b1, b2, b3, ssem, rsem):
    x, y, z, c = place()
    greet(partners(x, y, z, c))
    stages = [
        (b0, 2, c, lambda q: device(x, y, z, q)),
        (b1, 4, x, lambda q: device(q, y, z, c)),
        (b2, 4, y, lambda q: device(x, q, z, c)),
        (b3, 8, z, lambda q: device(x, y, q, c)),
    ]
    value = v_ref[...]
    base = 0
    sends = []
    for buf, n, p, dev in stages:
        buf[p] = value
        copies = [
            send(buf.at[p], buf.at[p], ssem.at[base + r], rsem.at[base + r], dev((p + r) % n))
            for r in range(1, n)
        ]
        for copy in copies:
            copy.wait_recv()
        value = buf[0]
        for k in range(1, n):
            value = value + buf[k]
        base += n
        sends += copies
    out_ref[...] = value
    for copy in sends:
        copy.wait_send()


def reduce_sums(v, number):
    return pl.pallas_call(
        reduce_body,
        in_specs=[vspec()],
        out_specs=vspec(),
        out_shape=struct((2, LANES), F32),
        scratch_shapes=[VM((n, 2, LANES), F32) for n in (2, 4, 4, 8)]
        + [DMA((18,)), DMA((18,))],
        compiler_params=remote_params(number),
        name="reduce_sums",
    )(v)


def scatter_body(st, out, r0, cur, r1, cur2, r2, cur3, r3, ss, rs):
    x, y, z, c = place()
    greet(partners(x, y, z, c))
    u = x * (1 - c) + y * c
    v = y * (1 - c) + x * c
    sib = device(x, y, z, 1 - c)

    def at_u(k):
        return device(k * (1 - c) + x * c, y * (1 - c) + k * c, z, c)

    def at_v(k):
        return device(x * (1 - c) + k * c, k * (1 - c) + y * c, z, c)

    sends = []
    first = []
    for r in range(4):
        q = (v + 1 + r) % 4
        first.append(send(st.at[1 - c, r], r0.at[r], ss.at[r], rs.at[r], sib))
    sends += first
    for r in range(4):
        first[r].wait_recv()

        def add(k, carry, r=r):
            row = pl.ds(pl.multiple_of(k * 64, 64), 64)
            for j in range(4):
                cur[r, j, row, :] = (st[c, r, j, row, :].astype(F32) + r0[r, j, row, :].astype(F32)).astype(BF)
            return carry

        lax.fori_loop(0, 8, add, 0)
    second = []
    for r in range(1, 4):
        q = (v + r) % 4
        second.append(send(cur.at[q], r1.at[r - 1], ss.at[3 + r], rs.at[3 + r], at_v(q)))
    sends += second
    for copy in second:
        copy.wait_recv()

    def add1(k, carry):
        row = pl.ds(pl.multiple_of(k * 64, 64), 64)
        for j in range(4):
            total = cur[v, j, row, :].astype(F32)
            for r in range(3):
                total = total + r1[r, j, row, :].astype(F32)
            cur2[j, row, :] = total.astype(BF)
        return carry

    lax.fori_loop(0, 8, add1, 0)
    third = []
    for r in range(1, 4):
        q = (u + r) % 4
        third.append(send(cur2.at[q], r2.at[r - 1], ss.at[6 + r], rs.at[6 + r], at_u(q)))
    sends += third
    for copy in third:
        copy.wait_recv()

    def add2(k, carry):
        row = pl.ds(pl.multiple_of(k * 64, 64), 64)
        total = cur2[u, row, :].astype(F32)
        for r in range(3):
            total = total + r2[r, row, :].astype(F32)
        cur3[k] = total.astype(BF)
        return carry

    lax.fori_loop(0, 8, add2, 0)
    fourth = []
    for r in range(1, 8):
        q = (z + r) % 8
        fourth.append(send(cur3.at[q], r3.at[r - 1], ss.at[9 + r], rs.at[9 + r], device(x, y, q, c)))
    sends += fourth
    for copy in fourth:
        copy.wait_recv()
    total = cur3[z].astype(F32)
    for r in range(7):
        total = total + r3[r].astype(F32)
    out[c, x, z] = total.astype(BF)
    fifth = []
    here = out.at[c, x, z]
    for r in range(1, 8):
        q = (z + r) % 8
        fifth.append(send(here, here, ss.at[16 + r], rs.at[16 + r], device(x, y, q, c)))
    sends += fifth
    for copy in fifth:
        copy.wait_recv()
    sixth = []
    here = out.at[c, x]
    for r in range(1, 4):
        q = (x + r) % 4
        sixth.append(send(here, here, ss.at[23 + r], rs.at[23 + r], device(q, y, z, c)))
    sends += sixth
    for copy in sixth:
        copy.wait_recv()
    here = out.at[c]
    last = send(here, here, ss.at[27], rs.at[27], sib)
    last.wait_recv()
    sends.append(last)
    for copy in sends:
        copy.wait_send()


def scatter_grad(st):
    return pl.pallas_call(
        scatter_body,
        in_specs=[vspec()],
        out_specs=vspec(),
        out_shape=struct((2, 4, 8, 64, 128), BF),
        scratch_shapes=[
            VM((4, 4, 512, 128), BF), VM((4, 4, 512, 128), BF),
            VM((3, 4, 512, 128), BF), VM((4, 512, 128), BF),
            VM((3, 512, 128), BF), VM((8, 64, 128), BF), VM((7, 64, 128), BF),
            DMA((28,)), DMA((28,)),
        ],
        compiler_params=remote_params(4),
        name="scatter_grad",
    )(st)


def tile_rows(tile_counts, owner_order):
    run_end = jnp.cumsum(tile_counts)
    run_start = run_end - tile_counts
    tile_ids = jnp.arange(144, dtype=jnp.int32)
    rank_of = jnp.sum((run_end[None, :] <= tile_ids[:, None]).astype(jnp.int32), axis=1)
    onehot = (rank_of[:, None] == jnp.arange(64, dtype=jnp.int32)[None, :]).astype(jnp.int32)
    s = jnp.sum(onehot * owner_order[None, :], axis=1)
    j = tile_ids - jnp.sum(onehot * run_start[None, :], axis=1)
    y, zl, x, core = s // 16, (s // 8) % 2, (s // 2) % 4, s % 2
    vu = jnp.where(j < 2, y * 4 + x, x * 4 + y)
    return (j // 2) * 128 + vu * 8 + zl * 4 + core * 2 + j % 2


def local(block_input, upstream, kernel_tiles, tile_counts, owner_order, gain, bias):
    c = constants()
    idx = tile_rows(tile_counts, owner_order)
    par = jnp.stack([channels_in(gain), channels_in(bias)])
    gathered = gather_tiles(prep(kernel_tiles.reshape(4, 99, 132))).reshape(256, 112, 128)
    xb, ex, hid, bm, ta, me, sums = fwd(idx, block_input, gathered, c)
    sums = reduce_sums(sums, 2)
    block_out, gs, ga, gsum = norm(upstream, xb, hid, sums, par, c)
    gsum = reduce_sums(gsum, 3)
    input_grad, st = back(hid, sums, gsum, par, gs, ga, xb, ex, bm, ta, me, c)
    h = scatter_grad(st).reshape(2, 4, 512, 128)
    sp = lax.axis_index("shard") % 16
    b0 = jnp.minimum((sp * 29403) // 17424, 24)
    flat = fin(b0.reshape(1), h).reshape(-1)
    kernel_grad = lax.dynamic_slice(flat, (sp * 29403 - b0 * 17424,), (29403,))
    return (block_out, input_grad, kernel_grad, channels_out(gsum[0]), channels_out(gsum[1]))


def solution(mesh):
    return jax.shard_map(
        local,
        mesh=mesh,
        in_specs=(
            P(("dp", "shard"), None, None, None),
            P(("dp", "shard"), None, None, None),
            P("shard", None),
            P(),
            P(),
            P(),
            P(),
        ),
        out_specs=(
            P(("dp", "shard"), None, None, None),
            P(("dp", "shard"), None, None, None),
            P("shard"),
            P(),
            P(),
        ),
        check_vma=False,
    )
```

```python
import numpy as np
import jax
import jax.numpy as jnp
from jax import lax
from jax.experimental import pallas as pl
from jax.experimental.pallas import tpu as pltpu
from jax.sharding import PartitionSpec as P

GROUPS = 12
GW = 132
ROWS = 448
LANES = 1664
BF = jnp.bfloat16
F32 = jnp.float32
EPSILON = 1e-05
TOTAL = 100352
VLIM = 60 * 1024 * 1024


def extra_lane(g, a):
    return 16 * (g // 3) + 4 * (g % 3) + a


def constants():
    pg = np.zeros((GROUPS, 256, 256), np.float32)
    for g in range(GROUPS):
        for j in range(GW):
            a, l = j // 33, j % 33
            pg[g, 4 * g + j, 32 * a + l if l < 32 else 128 + extra_lane(g, a)] = 1
    ry = np.zeros((9, 128, 4, 128), np.float32)
    for g in range(GROUPS):
        for tap in range(9):
            for a in range(4):
                ry[tap, extra_lane(g, a), g // 3, 36 * (g % 3) + 4 * tap + a] = 1
    selm = np.zeros((GROUPS, 16, 128), np.float32)
    for g in range(GROUPS):
        for a in range(4):
            selm[g, 3 + a, extra_lane(g, a)] = 1
    sele = np.zeros((2, 3, 128, 12, 16), np.float32)
    selb = np.zeros((2, 3, 9, 16, 12, 16), np.float32)
    for gg in range(3):
        for u in range(36):
            q, j = u // 3, u % 3
            tap, a = u // 4, u % 4
            for kind, row in ((0, j), (1, 7 + j)):
                sele[kind, gg, 36 * gg + u, q, row] = 1
                selb[kind, gg, tap, 4 * gg + a, q, row] = 1
    bf = lambda v, *s: jnp.asarray(v.reshape(s), BF)
    return dict(
        pg=bf(pg, GROUPS, 256, 256),
        ry=bf(ry, 1152, 512),
        selm=bf(selm, 192, 128),
        sele=bf(sele, 2, 3, 128, 192),
        selb=bf(selb, 2, 3, 144, 192),
    )


def prep_constants():
    cs = np.zeros((GW, 128), np.float32)
    cse = np.zeros((GW, 112), np.float32)
    csee = np.zeros((GW, 128), np.float32)
    rs = np.zeros((112, 99), np.float32)
    rsm = np.zeros((99, 128), np.float32)
    rse = np.zeros((112, 99), np.float32)
    for a in range(4):
        for l in range(32):
            cs[33 * a + l, 32 * a + l] = 1
        cse[33 * a + 32, 99 + a] = 1
    for lane in range(128):
        csee[33 * (lane % 4) + 32, lane] = 1
    for j in range(3):
        for l in range(32):
            rs[32 * j + l, 33 * j + l] = 1
            rsm[33 * j + l, 32 * j + l] = 1
        rs[96 + j, 33 * j + 32] = 1
        rse[103 + j, 33 * j + 32] = 1
    return [jnp.asarray(v, BF) for v in (cs, cse, csee, rs, rsm, rse)]


def dot(a, b, dims=((1,), (0,))):
    return lax.dot_general(a, b, (dims, ((), ())), preferred_element_type=F32)


MESH = pl.DeviceIdType.MESH
DMA = pltpu.SemaphoreType.DMA
VM = pltpu.VMEM


def vspec():
    return pl.BlockSpec(memory_space=VM)


def struct(shape, dtype):
    return jax.ShapeDtypeStruct(shape, dtype)


def lanes_of(g, width=1):
    if isinstance(g, int):
        return pl.ds(g * 128, 128 * width)
    return pl.ds(pl.multiple_of(g * 128, 128), 128 * width)


def rows_at(start, size):
    if isinstance(start, int):
        return pl.ds(start, size)
    return pl.ds(pl.multiple_of(start, 16), size)


def lane_iota(rows):
    return lax.broadcasted_iota(jnp.int32, (rows, 128), 1)


def half_tanh(v):
    return 0.5 * jnp.tanh(0.5 * v) + 0.5


def place():
    dp = lax.axis_index("dp")
    s = lax.axis_index("shard")
    return (s // 2) % 4, s // 16, dp * 2 + (s // 8) % 2, s % 2


def device(x, y, z, c):
    return (z // 2, y * 16 + (z % 2) * 8 + x * 2 + c)


def send(src, dst, send_sem, recv_sem, to):
    copy = pltpu.make_async_remote_copy(
        src_ref=src, dst_ref=dst, send_sem=send_sem, recv_sem=recv_sem,
        device_id=to, device_id_type=MESH,
    )
    copy.start()
    return copy


def load_native(raw, xn):
    xn[...] = jnp.zeros_like(xn)
    for y in range(14):
        xn[y, 0:28, 0:1584] = raw[y].reshape(28, 1584)


def store_shifts(dst, main, lanes):
    for b in range(3):
        moved = main if b == 1 else pltpu.roll(main, (2 - 2 * b) % ROWS, 0)
        dst[b, 1:15, :, lanes] = moved.astype(BF).reshape(14, 32, 128)


def zero_borders(dst):
    zeros = jnp.zeros((3, 32, LANES), BF)
    dst[:, 0] = zeros
    dst[:, 15] = zeros


def tap_slice(src, tap, lanes, mirrored):
    a, b = tap // 3, tap % 3
    if mirrored:
        a, b = 2 - a, 2 - b
    return src[b, a : a + 14, :, lanes].reshape(ROWS, 128)


def tap_concat(src, lanes, mirrored, extra=None):
    pieces = [tap_slice(src, tap, lanes, mirrored) for tap in range(9)]
    if extra is not None:
        pieces.append(extra)
    return jnp.concatenate(pieces, axis=1)


def piece_of(b):
    s = {t: (b + 27 - t) // 27 for t in (3, 7, 10, 13, 17, 20, 24)}
    x = s[3] + s[7] + s[10] - 3 * s[13] + s[17] + s[20] + s[24]
    pos = b - 3 * s[3] - 4 * s[7] - 3 * s[10] - 3 * s[17] - 4 * s[20] - 4 * s[24]
    return x, pos


def fin_constants():
    q_m = np.zeros((128, 136), np.float32)
    q_o = np.zeros((3, 144, GW), np.float32)
    for a in range(4):
        for l in range(32):
            q_m[32 * a + l, 33 * a + l] = 1
            q_o[:, 32 * a + l, 33 * a + l] = 1
        for gg in range(3):
            q_o[gg, 128 + 4 * gg + a, 33 * a + 32] = 1
    return jnp.asarray(q_m, BF), jnp.asarray(q_o, BF)


IN_NAMES = (
    "idx", "tile", "cs", "cse", "csee", "rs", "rsm", "rse", "par",
    "pg", "ry", "selm", "sele", "selb", "qm", "qo", "x_hbm", "up_hbm",
)
OUT_NAMES = ("out_hbm", "ig_hbm", "kg", "gsum")


def scratch_list():
    sets = dict(
        pay=VM((4, 112, 128), BF),
        gat=VM((256, 112, 128), BF),
        xb=VM((3, 16, 32, LANES), BF),
        ghb=VM((3, 16, 32, LANES), BF),
        ex=VM((ROWS, 512), BF),
        eg=VM((ROWS, 512), BF),
        bm=VM((GROUPS, 1152, 128), BF),
        ta=VM((GROUPS, 12, 16, 128), BF),
        me=VM((1152, 128), BF),
        hid=VM((ROWS, LANES), BF),
        gs=VM((ROWS, LANES), F32),
        ga=VM((ROWS, LANES), F32),
        upp=VM((ROWS, LANES), BF),
        bo=VM((ROWS, LANES), BF),
        raw=VM((14, 14, 2, 1584), BF),
        raw2=VM((14, 14, 2, 1584), BF),
        xn=VM((14, 32, LANES), BF),
        acc=VM((ROWS, 128), F32),
        mec=VM((16, 1152), F32),
        bg=VM((1280, 256), BF),
        wt=VM((256, 1280), BF),
        tr=VM((128, 512), BF),
        g12t=VM((128, ROWS), BF),
        st=VM((2, 4, 4, 512, 128), BF),
        r0=VM((4, 4, 512, 128), BF),
        r1=VM((3, 4, 512, 128), BF),
        cur2=VM((4, 512, 128), BF),
        r2=VM((3, 512, 128), BF),
        cur3=VM((8, 64, 128), BF),
        r3=VM((7, 64, 128), BF),
        hh=VM((2, 4, 8, 64, 128), BF),
        sums=VM((2, LANES), F32),
        lsum=VM((2, LANES), F32),
        s_in=DMA((2,)),
        s_out=DMA((2,)),
        s_sib=DMA((1,)), r_sib=DMA((1,)),
        s_z=DMA((2,)), r_z=DMA((2,)),
        s_u=DMA((2, 4)), r_u=DMA((2, 4)),
        s_v=DMA((8, 4)), r_v=DMA((8, 4)),
        s_d=DMA((33,)), r_d=DMA((33,)),
        s_c=DMA((16,)), r_c=DMA((16,)),
        s_1=DMA((12,)), r_1=DMA((12,)),
        s_2=DMA((3,)), r_2=DMA((3,)),
        s_3=DMA((7,)), r_3=DMA((7,)),
        s_4=DMA((7,)), r_4=DMA((7,)),
        s_5=DMA((11,)), r_5=DMA((11,)),
        s_a=DMA((2, 18)), r_a=DMA((2, 18)),
    )
    for k in range(2):
        for n, name in ((2, "c"), (4, "x"), (4, "y"), (8, "z")):
            sets["b%d%s" % (k, name)] = VM((n, 2, LANES), F32)
    return sets


class Refs:
    pass


def mega_body(*refs):
    r = Refs()
    names = list(IN_NAMES) + list(OUT_NAMES) + list(scratch_list())
    for name, ref in zip(names, refs, strict=True):
        setattr(r, name, ref)
    x, y, z, c = place()
    u = x * (1 - c) + y * c
    v = y * (1 - c) + x * c
    zl = z % 2
    oz = 1 - zl
    sib = device(x, y, z, 1 - c)

    def at_u(k):
        return device(k * (1 - c) + x * c, y * (1 - c) + k * c, z, c)

    def at_v(k):
        return device(x * (1 - c) + k * c, k * (1 - c) + y * c, z, c)

    others = [sib]
    others += [device((x + k) % 4, y, z, c) for k in range(1, 4)]
    others += [device((x + k) % 4, y, z, 1 - c) for k in range(1, 4)]
    others += [device(x, (y + k) % 4, z, c) for k in range(1, 4)]
    others += [device(x, y, (z + k) % 8, c) for k in range(1, 8)]
    barrier = pltpu.get_barrier_semaphore()
    for d in others:
        pl.semaphore_signal(barrier, inc=1, device_id=d, device_id_type=MESH)
    in_x = pltpu.make_async_copy(r.x_hbm, r.raw, r.s_in.at[0])
    in_x.start()
    in_up = pltpu.make_async_copy(r.up_hbm, r.raw2, r.s_in.at[1])
    in_up.start()
    for s in range(4):
        t = r.tile[s]
        w = dot(t, r.cs[...]).astype(BF)
        we = dot(t, r.cse[...]).astype(BF)
        wee = dot(t, r.csee[...]).astype(BF)
        full = dot(r.rs[...], w) + dot(we, r.rsm[...], ((0,), (0,))) + dot(r.rse[...], wee)
        r.pay[s] = full.astype(BF)
    pl.semaphore_wait(barrier, len(others))
    sends = []

    acc = r.acc

    def first_x():
        in_x.wait()
        load_native(r.raw, r.xn)
        zero_borders(r.xb)
        acc[...] = jnp.zeros_like(acc)

    def permute(lo, hi, sink):
        def step(g, carry):
            p = dot(r.xn[:, :, lanes_of(g, 2)].reshape(ROWS, 256), r.pg[g])
            sink(g, p[:, :128])
            acc[...] += p[:, 128:]
            return carry

        lax.fori_loop(lo, hi, step, 0)

    def keep_x(g, val):
        store_shifts(r.xb, val, lanes_of(g))

    def keep_up(g, val):
        r.upp[:, lanes_of(g)] = val.astype(BF)

    def last_x():
        keep_x(GROUPS, acc[...])
        r.ex[...] = dot(tap_concat(r.xb, lanes_of(12), False), r.ry[...]).astype(BF)

    def first_up():
        in_up.wait()
        load_native(r.raw2, r.xn)
        zero_borders(r.ghb)
        acc[...] = jnp.zeros_like(acc)

    thunks = [first_x]
    thunks += [lambda k=k: permute(3 * k, 3 * k + 3, keep_x) for k in range(4)]
    thunks += [last_x, first_up]
    thunks += [lambda k=k: permute(3 * k, 3 * k + 3, keep_up) for k in range(4)]
    thunks += [lambda: keep_up(GROUPS, acc[...])]

    def work():
        if thunks:
            thunks.pop(0)()

    gat = r.gat

    def chunk(i, j, zz):
        lin = c * 128 + ((v + i) % 4) * 32 + ((u + j) % 4) * 8 + zz * 4
        return lambda h=None: gat.at[pl.ds(lin, 4)] if h is None else gat.at[pl.ds(lin + 2 * h, 2)]

    mine = c * 128 + v * 32 + u * 8 + zl * 4 + c * 2
    other = (1 - c) * 128 + u * 32 + v * 8 + zl * 4 + c * 2
    gat[pl.ds(mine, 2)] = r.pay[pl.ds(2 * c, 2)]
    gat[pl.ds(other, 2)] = r.pay[pl.ds(2 - 2 * c, 2)]
    mine, other = gat.at[pl.ds(mine, 2)], gat.at[pl.ds(other, 2)]
    sib_copy = send(other, other, r.s_sib.at[0], r.r_sib.at[0], sib)
    own_copy = send(mine, mine, r.s_d.at[32], r.r_d.at[32], sib)
    sends += [sib_copy, own_copy]
    sib_copy.wait_recv()

    k = chunk(0, 0, zl)
    z0 = send(k(0), k(0), r.s_z.at[0], r.r_z.at[0], device(x, y, (z + 1) % 8, c))
    z1 = send(k(1), k(1), r.s_z.at[1], r.r_z.at[1], device(x, y, (z + 7) % 8, c))
    sends += [z0, z1]

    def spread(n, k, ss, rs, at, p):
        pair = [send(k(), k(), ss.at[n, 0], rs.at[n, 0], at((p + 1) % 4)),
                send(k(), k(), ss.at[n, 1], rs.at[n, 1], at((p + 3) % 4))]
        sends.extend(pair)
        return pair

    def spread_u(n, zz):
        return spread(n, chunk(0, 0, zz), r.s_u, r.r_u, at_u, u)

    def spread_v(n, k):
        return spread(n, k, r.s_v, r.r_v, at_v, v)

    def pass_on(n, k):
        sends.append(send(k(), k(), r.s_d.at[n], r.r_d.at[n], sib))

    order = [(0, zl), (0, oz), (3, zl), (1, zl), (3, oz), (1, oz), (2, zl), (2, oz)]
    ring_u, ring_v = {}, {}
    ring_u[0] = spread_u(0, zl)
    ring_v[0] = spread_v(0, chunk(0, 0, zl))
    work()
    z0.wait_recv()
    z1.wait_recv()
    ring_u[1] = spread_u(1, oz)
    ring_v[1] = spread_v(1, chunk(0, 0, oz))
    pass_on(1, chunk(0, 0, oz))
    half_u = {}
    for n, zz in ((0, zl), (1, oz)):
        work()
        ring_u[n][0].wait_recv()
        k = chunk(0, 3, zz)
        h0 = send(k(0), k(0), r.s_u.at[n, 2], r.r_u.at[n, 2], at_u((u + 1) % 4))
        ring_v[2 + 2 * n] = spread_v(2 + 2 * n, k)
        pass_on(2 + 2 * n, k)
        ring_u[n][1].wait_recv()
        k = chunk(0, 1, zz)
        h1 = send(k(1), k(1), r.s_u.at[n, 3], r.r_u.at[n, 3], at_u((u + 3) % 4))
        ring_v[3 + 2 * n] = spread_v(3 + 2 * n, k)
        pass_on(3 + 2 * n, k)
        sends += [h0, h1]
        half_u[n] = (h0, h1)
    for n, zz in ((0, zl), (1, oz)):
        work()
        half_u[n][0].wait_recv()
        half_u[n][1].wait_recv()
        k = chunk(0, 2, zz)
        ring_v[6 + n] = spread_v(6 + n, k)
        pass_on(6 + n, k)
    half_v = {}
    for n, (j, zz) in enumerate(order):
        work()
        ring_v[n][0].wait_recv()
        k = chunk(3, j, zz)
        h0 = send(k(0), k(0), r.s_v.at[n, 2], r.r_v.at[n, 2], at_v((v + 1) % 4))
        pass_on(8 + n, k)
        ring_v[n][1].wait_recv()
        k = chunk(1, j, zz)
        h1 = send(k(1), k(1), r.s_v.at[n, 3], r.r_v.at[n, 3], at_v((v + 3) % 4))
        pass_on(16 + n, k)
        sends += [h0, h1]
        half_v[n] = (h0, h1)
    for n, (j, zz) in enumerate(order):
        half_v[n][0].wait_recv()
        half_v[n][1].wait_recv()
        pass_on(24 + n, chunk(2, j, zz))
    while thunks:
        work()
    for n in range(1, 32):
        k = gat.at[pl.ds((1 - c) * 128, 4)]
        pltpu.make_async_remote_copy(
            src_ref=k, dst_ref=k, send_sem=r.s_d.at[n], recv_sem=r.r_d.at[n],
            device_id=sib, device_id_type=MESH,
        ).wait_recv()
    own_copy.wait_recv()
    for copy in sends:
        copy.wait_send()
    sends = []

    def pull(t, carry):
        g, q = t // 12, t % 12
        s = r.idx[t]
        r.bm[g, pl.ds(pl.multiple_of(q * 96, 32), 96), :] = gat[s, 0:96, :]
        r.ta[g, q] = gat[s, 96:112, :]
        return carry

    lax.fori_loop(0, 144, pull, 0)
    for q in range(12):
        m = dot(r.ta[:, q].reshape(192, 128), r.selm[...], ((0,), (0,)))
        r.me[96 * q : 96 * q + 96, :] = m[0:96].astype(BF)
    acc[...] = jnp.zeros_like(acc)
    valid = (lax.broadcasted_iota(jnp.int32, (ROWS, 128), 0) % 32) < 28

    def stat(h, lanes):
        h = jnp.where(valid, h.astype(F32), 0.0)
        r.lsum[0:1, lanes] = jnp.sum(h, axis=0, keepdims=True)
        r.lsum[1:2, lanes] = jnp.sum(h * h, axis=0, keepdims=True)

    def fstep(yy, carry):
        for gg in range(3):
            g = 3 * yy + gg
            here = (lane_iota(1152) // 4) == yy * 4 + gg
            bg = r.bg
            bg[0:1152, 0:128] = r.bm[g]
            bg[0:1152, 128:256] = jnp.where(here, r.me[...].astype(F32), 0.0).astype(BF)
            tails = r.ta[g].reshape(192, 128)
            bg[1152:1280, 0:128] = dot(r.sele[0, gg], tails).astype(BF)
            ee = jnp.where(here[0:128], dot(r.sele[1, gg], tails), 0.0)
            bg[1152:1280, 128:256] = ee.astype(BF)
            a = tap_concat(r.xb, lanes_of(g), False, r.ex[:, lanes_of(yy)])
            p = dot(a, bg[...])
            h = p[:, :128].astype(BF)
            r.hid[:, lanes_of(g)] = h
            stat(h, lanes_of(g))
            acc[...] += p[:, 128:]
        return carry

    lax.fori_loop(0, 4, fstep, 0)
    h = acc[...].astype(BF)
    r.hid[:, 1536:1664] = h
    stat(h, lanes_of(12))

    def all_sum(k, src, dst, fill):
        value = src[...]
        base = 0
        stages = [
            ("c", 2, c, lambda q: device(x, y, z, q)),
            ("x", 4, x, lambda q: device(q, y, z, c)),
            ("y", 4, y, lambda q: device(x, q, z, c)),
            ("z", 8, z, lambda q: device(x, y, q, c)),
        ]
        for name, n, p, dev in stages:
            buf = getattr(r, "b%d%s" % (k, name))
            buf[p] = value
            copies = [
                send(buf.at[p], buf.at[p], r.s_a.at[k, base + i], r.r_a.at[k, base + i], dev((p + i) % n))
                for i in range(1, n)
            ]
            sends.extend(copies)
            if fill:
                fill.pop(0)()
            for copy in copies:
                copy.wait_recv()
            value = buf[0]
            for i in range(1, n):
                value = value + buf[i]
            base += n
        dst[...] = value

    def make_tr():
        tr_in = jnp.concatenate([r.me[128 * tap : 128 * tap + 128] for tap in range(9)], axis=1)
        r.tr[...] = dot(tr_in, r.ry[...]).astype(BF)
        r.wt[128:256, :] = jnp.zeros((128, 1280), BF)

    all_sum(0, r.lsum, r.sums, [make_tr])

    def tile(t, carry):
        lanes = lanes_of(t)
        avg = r.sums[0:1, lanes] / TOTAL
        inv = lax.rsqrt(r.sums[1:2, lanes] / TOTAL - avg * avg + EPSILON)
        gain, bias = r.par[0:1, lanes], r.par[1:2, lanes]
        s1 = jnp.zeros((8, 128), F32)
        s2 = jnp.zeros((8, 128), F32)
        for k in range(28):
            rows = pl.ds(16 * k, 16)
            xv = r.xb[1, 1 + k // 2, 16 * (k % 2) : 16 * (k % 2) + 16, lanes].astype(F32)
            normed = (r.hid[rows, lanes].astype(F32) - avg) * inv
            aff = gain * normed + bias
            sa = half_tanh(aff)
            act = aff * sa
            summed = xv + act
            ss = half_tanh(summed)
            out = summed * ss
            r.bo[rows, lanes] = out.astype(BF)
            gsv = r.upp[rows, lanes].astype(F32) * (ss + out * (1.0 - ss))
            gav = gsv * (sa + act * (1.0 - sa))
            r.gs[rows, lanes] = gsv
            r.ga[rows, lanes] = gav
            p = gav * normed
            s1 = s1 + (p[0:8] + p[8:16])
            s2 = s2 + (gav[0:8] + gav[8:16])
        r.lsum[0:1, lanes] = jnp.sum(s1, axis=0, keepdims=True)
        r.lsum[1:2, lanes] = jnp.sum(s2, axis=0, keepdims=True)
        return carry

    lax.fori_loop(0, 13, tile, 0)

    def unpermute(lo, hi, src):
        def step(g, carry):
            pair = jnp.concatenate([src(g), src(GROUPS)], axis=1)
            p = dot(pair, r.pg[g], ((1,), (1,)))
            r.xn[:, :, lanes_of(g)] = (acc[...] + p[:, :128]).astype(BF).reshape(14, 32, 128)
            acc[...] = p[:, 128:]
            return carry

        if lo == 0:
            acc[...] = jnp.zeros_like(acc)
        lax.fori_loop(lo, hi, step, 0)

    def write_out(raw, hbm, n):
        r.xn[:, :, 1536:1664] = acc[...].astype(BF).reshape(14, 32, 128)
        for yy in range(14):
            raw[yy] = r.xn[yy, 0:28, 0:1584].reshape(14, 2, 1584)
        copy = pltpu.make_async_copy(raw, hbm, r.s_out.at[n])
        copy.start()
        return copy

    outs = []
    from_bo = lambda g: r.bo[:, lanes_of(g)]
    all_sum(1, r.lsum, r.gsum, [
        lambda: unpermute(0, 4, from_bo),
        lambda: unpermute(4, 8, from_bo),
        lambda: unpermute(8, 12, from_bo),
        lambda: outs.append(write_out(r.raw, r.out_hbm, 0)),
    ])

    def gtile(t, carry):
        lanes = lanes_of(t)
        avg = r.sums[0:1, lanes] / TOTAL
        inv = lax.rsqrt(r.sums[1:2, lanes] / TOTAL - avg * avg + EPSILON)
        scale = r.par[0:1, lanes] * inv
        c1 = r.gsum[1:2, lanes] / TOTAL
        c2 = r.gsum[0:1, lanes] / TOTAL
        normed = (r.hid[:, lanes].astype(F32) - avg) * inv
        gh = scale * (r.ga[:, lanes] - c1 - normed * c2)
        store_shifts(r.ghb, jnp.where(valid, gh, 0.0), lanes)
        return carry

    lax.fori_loop(0, 13, gtile, 0)
    r.eg[...] = dot(tap_concat(r.ghb, lanes_of(12), True), r.ry[...]).astype(BF)
    g12 = r.ghb[1, 1:15, :, 1536:1664].reshape(ROWS, 128)
    r.g12t[...] = g12.astype(F32).T.astype(BF)

    st, r0 = r.st, r.r0

    def place_of(k, i, half):
        yy, xx = (y + 1 + k) % 4, (x + 1 + i) % 4
        return yy * (1 - half) + xx * half, xx * (1 - half) + yy * half

    def core_copy(k, i):
        pv, pu = place_of(k, i, 1 - c)
        return pltpu.make_async_remote_copy(
            src_ref=st.at[1 - c, pv, pu], dst_ref=r0.at[pv, pu],
            send_sem=r.s_c.at[4 * k + i], recv_sem=r.r_c.at[4 * k + i],
            device_id=sib, device_id_type=MESH,
        )

    def v_copy(rel, ju):
        q = (v + 1 + rel) % 4
        return pltpu.make_async_remote_copy(
            src_ref=r0.at[q, (u + 1 + ju) % 4], dst_ref=r.r1.at[rel, ju],
            send_sem=r.s_1.at[4 * rel + ju], recv_sem=r.r_1.at[4 * rel + ju],
            device_id=at_v(q), device_id_type=MESH,
        )

    def add_core(k):
        for i in range(4):
            core_copy(k, i).wait_recv()
            pv, pu = place_of(k, i, c)

            def add(n, carry):
                row = pl.ds(pl.multiple_of(n * 128, 128), 128)
                total = st[c, pv, pu, row, :].astype(F32) + r0[pv, pu, row, :].astype(F32)
                r0[pv, pu, row, :] = total.astype(BF)
                return carry

            lax.fori_loop(0, 4, add, 0)
            if i < 3:
                @pl.when(c == 1)
                def _():
                    v_copy(i, k).start()

            @pl.when((c == 0) & (k < 3))
            def _():
                v_copy(k, i).start()

    def wstep(k, carry):
        yy = (y + 1 + k) % 4
        acc[0:144, :] = jnp.zeros((144, 128), F32)
        r.mec[...] = jnp.zeros_like(r.mec)
        lhs12 = r.g12t[rows_at(16 * yy, 16), :]
        for gg in range(3):
            g = 3 * yy + gg
            main = r.ghb[1, 1:15, :, lanes_of(g)].reshape(ROWS, 128)
            lhs = jnp.concatenate([main.astype(F32).T.astype(BF), lhs12], axis=0)
            a = tap_concat(r.xb, lanes_of(g), False, r.ex[:, lanes_of(yy)])
            p = dot(lhs, a)
            for tap in range(9):
                px, pos = piece_of(gg * 9 + tap)
                blk = p[0:128, tap * 128 : tap * 128 + 128].astype(BF)
                st[0, yy, px, pos * 64 : pos * 64 + 64, :] = blk[0:64]
                st[1, px, yy, pos * 64 : pos * 64 + 64, :] = blk[64:128]
            rowsel = (lax.broadcasted_iota(jnp.int32, (16, 1152), 0) // 4) == gg
            r.mec[...] += jnp.where(rowsel, p[128:144, 0:1152], 0.0)
            lane = lane_iota(144)
            lanesel = (lane >= 36 * gg) & (lane < 36 * gg + 36)
            row = lax.broadcasted_iota(jnp.int32, (144, 128), 0)
            rowsel = (row < 128) | (row // 4 == 32 + gg)
            acc[0:144, :] += jnp.where(lanesel & rowsel, p[:, 1152:1280], 0.0)
        zeros = jnp.zeros((128, 128), BF)
        for px in range(3):
            for j in range(3):
                tap = 3 * px + j
                st[0, yy, px, 448 + 16 * j : 464 + 16 * j, :] = r.mec[:, 128 * tap : 128 * tap + 128].astype(BF)
            st[1, px, yy, 448:496, :] = acc[48 * px : 48 * px + 48, :].astype(BF)
            st[0, yy, px, 496:512, :] = zeros[0:16]
            st[1, px, yy, 496:512, :] = zeros[0:16]
        st[0, yy, 3, 384:512, :] = zeros
        st[1, 3, yy, 384:512, :] = zeros
        for i in range(4):
            core_copy(k, i).start()

        @pl.when(k > 0)
        def _():
            add_core(k - 1)

        return carry

    lax.fori_loop(0, 4, wstep, 0)

    def back_set(yy):
        block = pl.ds(128 + 16 * yy, 16)
        wt = r.wt

        def bstep(gg, carry):
            g = 3 * yy + gg
            for tap in range(9):
                wt[0:128, 128 * tap : 128 * tap + 128] = r.bm[g, 128 * tap : 128 * tap + 128, :]
            lane = lane_iota(128)
            lanesel = (lane >= 36 * gg) & (lane < 36 * gg + 36)
            wt[0:128, 1152:1280] = jnp.where(lanesel, r.tr[:, lanes_of(yy)].astype(F32), 0.0).astype(BF)
            tails = r.ta[g].reshape(192, 128)
            bl = dot(r.selb[0, gg], tails).astype(BF)
            be = dot(r.selb[1, gg], tails)
            low = jnp.zeros((16, 128), F32)
            lane = lane_iota(16)
            for tap in range(9):
                wt[block, 128 * tap : 128 * tap + 128] = bl[16 * tap : 16 * tap + 16]
                low = jnp.where((lane // 4) == 9 * gg + tap, be[16 * tap : 16 * tap + 16], low)
            wt[block, 1152:1280] = low.astype(BF)
            a = tap_concat(r.ghb, lanes_of(g), True, r.eg[:, lanes_of(yy)])
            p = dot(a, wt[...], ((1,), (1,)))
            r.gs[:, lanes_of(g)] += p[:, :128]
            r.gs[:, 1536:1664] += p[:, 128:]
            return carry

        lax.fori_loop(0, 3, bstep, 0)
        wt[block, :] = jnp.zeros((16, 1280), BF)

    def sum_v(ju):
        for rel in range(3):
            v_copy(rel, ju).wait_recv()
        pu = (u + 1 + ju) % 4

        def add(n, carry):
            row = pl.ds(pl.multiple_of(n * 128, 128), 128)
            total = r0[v, pu, row, :].astype(F32)
            for rel in range(3):
                total = total + r.r1[rel, ju, row, :].astype(F32)
            r.cur2[ju, row, :] = total.astype(BF)
            return carry

        lax.fori_loop(0, 4, add, 0)
        if ju < 3:
            send_u = send(r.cur2.at[ju], r.r2.at[ju], r.s_2.at[ju], r.r_2.at[ju], at_u(pu))
            u_copies.append(send_u)

    u_copies = []
    back_set(0)
    add_core(3)
    back_set(1)
    back_set(2)
    sum_v(0)
    sum_v(1)
    back_set(3)
    sum_v(2)
    sum_v(3)
    from_gs = lambda g: r.gs[:, lanes_of(g)].astype(BF)
    unpermute(0, 4, from_gs)
    for copy in u_copies:
        copy.wait_recv()
    sends += u_copies
    for n in range(8):
        row = pl.ds(64 * n, 64)
        total = r.cur2[3, row, :].astype(F32)
        for rel in range(3):
            total = total + r.r2[rel, row, :].astype(F32)
        r.cur3[n] = total.astype(BF)
    copies = []
    for k in range(1, 8):
        q = (z + k) % 8
        copies.append(send(r.cur3.at[q], r.r3.at[k - 1], r.s_3.at[k - 1], r.r_3.at[k - 1], device(x, y, q, c)))
    sends += copies
    unpermute(4, 8, from_gs)
    for copy in copies:
        copy.wait_recv()
    total = r.cur3[z].astype(F32)
    for k in range(7):
        total = total + r.r3[k].astype(F32)
    hh = r.hh
    hh[c, x, z] = total.astype(BF)
    here = hh.at[c, x, z]
    copies = []
    for k in range(1, 8):
        q = (z + k) % 8
        copies.append(send(here, here, r.s_4.at[k - 1], r.r_4.at[k - 1], device(x, y, q, c)))
    sends += copies
    unpermute(8, 12, from_gs)
    outs.append(write_out(r.raw2, r.ig_hbm, 1))
    for copy in copies:
        copy.wait_recv()
    near = [(1, 6 - 3 * (x % 2) - 3 * (x // 3)), (3, 3 - 3 * (x % 2))]
    copies = [send(hh.at[c, x], hh.at[c, x], r.s_5.at[0], r.r_5.at[0], sib)]
    n = 1
    for cc in (c, 1 - c):
        for rel, pos in near:
            to = device((x + rel) % 4, y, z, cc)
            copies.append(send(hh.at[c, x, pos], hh.at[c, x, pos], r.s_5.at[n], r.r_5.at[n], to))
            copies.append(send(hh.at[c, x, 7], hh.at[c, x, 7], r.s_5.at[n + 1], r.r_5.at[n + 1], to))
            n += 2
        to = device((x + 2) % 4, y, z, cc)
        copies.append(send(hh.at[c, x, 7], hh.at[c, x, 7], r.s_5.at[n], r.r_5.at[n], to))
        n += 1
    for copy in copies:
        copy.wait_recv()
    sends += copies
    sp = (z % 2) * 8 + x * 2 + c
    b0 = (sp * 29403) // 17424 - sp // 15
    em = jnp.concatenate([hh[1, j, 7, 0:48, :] for j in range(3)], axis=0)
    for k in range(3):
        b = b0 + k
        px, pos = piece_of(b)
        tap = b % 9
        gg = b // 9
        main = jnp.concatenate([hh[0, px, pos], hh[1, px, pos]], axis=0)
        mrow = hh[0, tap // 3, 7, rows_at(16 * (tap % 3), 16), :]
        left = jnp.concatenate([main, mrow], axis=0)
        line = lax.broadcasted_iota(jnp.int32, (128, 136), 0) - (36 * gg + 4 * tap)
        unit = lax.broadcasted_iota(jnp.int32, (128, 136), 1)
        qe = jnp.where((line >= 0) & (line < 4) & (unit == 33 * line + 32), 1.0, 0.0).astype(BF)
        t1 = (dot(left, r.qm[...]) + dot(em, qe)).astype(BF)
        t2 = dot(t1, r.qo[gg], ((0,), (0,)))
        r.kg[pl.ds(132 * k, 132), :] = t2[0:132]

    for copy in sends:
        copy.wait_send()
    for k in range(4):
        for i in range(4):
            core_copy(k, i).wait_send()
    for rel in range(3):
        for ju in range(4):
            v_copy(rel, ju).wait_send()
    for copy in outs:
        copy.wait()


def mega(idx, tiles, par, xt, upt):
    k = constants()
    operands = [idx, tiles, *prep_constants(), par, k["pg"], k["ry"], k["selm"], k["sele"], k["selb"], *fin_constants(), xt, upt]
    anywhere = pl.BlockSpec(memory_space=pl.ANY)
    return pl.pallas_call(
        mega_body,
        in_specs=[pl.BlockSpec(memory_space=pltpu.SMEM)] + [vspec()] * 15 + [anywhere] * 2,
        out_specs=[anywhere, anywhere, vspec(), vspec()],
        out_shape=[
            struct((14, 14, 2, 1584), BF),
            struct((14, 14, 2, 1584), BF),
            struct((396, GW), F32),
            struct((2, LANES), F32),
        ],
        scratch_shapes=list(scratch_list().values()),
        compiler_params=pltpu.CompilerParams(
            collective_id=1, has_side_effects=True, vmem_limit_bytes=VLIM
        ),
        name="block",
    )(*operands)


def channels_in(v):
    p = v.reshape(4, 3, 4, 33)
    main = p[..., :32].reshape(1536)
    extra = jnp.pad(p[..., 32].reshape(4, 12), ((0, 0), (0, 4))).reshape(64)
    return jnp.concatenate([main, extra, jnp.zeros((64,), v.dtype)])


def channels_out(v):
    main = v[:1536].reshape(4, 3, 4, 32)
    extra = v[1536:1600].reshape(4, 16)[:, :12].reshape(4, 3, 4, 1)
    return jnp.concatenate([main, extra], axis=-1).reshape(1584)


def tile_rows(tile_counts, owner_order):
    run_end = jnp.cumsum(tile_counts)
    run_start = run_end - tile_counts
    tile_ids = jnp.arange(144, dtype=jnp.int32)
    rank_of = jnp.sum((run_end[None, :] <= tile_ids[:, None]).astype(jnp.int32), axis=1)
    onehot = (rank_of[:, None] == jnp.arange(64, dtype=jnp.int32)[None, :]).astype(jnp.int32)
    s = jnp.sum(onehot * owner_order[None, :], axis=1)
    j = tile_ids - jnp.sum(onehot * run_start[None, :], axis=1)
    y, zl, x, core = s // 16, (s // 8) % 2, (s // 2) % 4, s % 2
    vu = jnp.where(j < 2, y * 4 + x, x * 4 + y)
    return (j // 2) * 128 + vu * 8 + zl * 4 + core * 2 + j % 2


def local(block_input, upstream, kernel_tiles, tile_counts, owner_order, gain, bias):
    idx = tile_rows(tile_counts, owner_order)
    par = jnp.stack([channels_in(gain), channels_in(bias)])
    turn = lambda a: jnp.transpose(a, (1, 2, 0, 3))
    back = lambda a: jnp.transpose(a, (2, 0, 1, 3))
    out, ig, kg, gsum = mega(
        idx, kernel_tiles.reshape(4, 99, GW), par, turn(block_input), turn(upstream)
    )
    sp = lax.axis_index("shard") % 16
    b0 = (sp * 29403) // 17424 - sp // 15
    kernel_grad = lax.dynamic_slice(kg.reshape(-1), (sp * 29403 - b0 * 17424,), (29403,))
    return (back(out), back(ig), kernel_grad, channels_out(gsum[0]), channels_out(gsum[1]))


def solution(mesh):
    return jax.shard_map(
        local,
        mesh=mesh,
        in_specs=(
            P(("dp", "shard"), None, None, None),
            P(("dp", "shard"), None, None, None),
            P("shard", None),
            P(),
            P(),
            P(),
            P(),
        ),
        out_specs=(
            P(("dp", "shard"), None, None, None),
            P(("dp", "shard"), None, None, None),
            P("shard"),
            P(),
            P(),
        ),
        check_vma=False,
    )
```

```python
import numpy as np
import jax
import jax.numpy as jnp
from jax import lax
from jax.experimental import pallas as pl
from jax.experimental.pallas import tpu as pltpu
from jax.sharding import PartitionSpec as P

GROUPS = 12
GW = 132
ROWS = 448
LANES = 1664
BF = jnp.bfloat16
F32 = jnp.float32
EPSILON = 1e-05
TOTAL = 100352
VLIM = 60 * 1024 * 1024


def extra_lane(g, a):
    return 16 * (g // 3) + 4 * (g % 3) + a


def constants():
    pg = np.zeros((GROUPS, 256, 256), np.float32)
    for g in range(GROUPS):
        for j in range(GW):
            a, l = j // 33, j % 33
            pg[g, 4 * g + j, 32 * a + l if l < 32 else 128 + extra_lane(g, a)] = 1
    ry = np.zeros((9, 128, 4, 128), np.float32)
    for g in range(GROUPS):
        for tap in range(9):
            for a in range(4):
                ry[tap, extra_lane(g, a), g // 3, 36 * (g % 3) + 4 * tap + a] = 1
    selm = np.zeros((GROUPS, 16, 128), np.float32)
    for g in range(GROUPS):
        for a in range(4):
            selm[g, 3 + a, extra_lane(g, a)] = 1
    sele = np.zeros((2, 3, 128, 12, 16), np.float32)
    selb = np.zeros((2, 3, 9, 16, 12, 16), np.float32)
    for gg in range(3):
        for u in range(36):
            q, j = u // 3, u % 3
            tap, a = u // 4, u % 4
            for kind, row in ((0, j), (1, 7 + j)):
                sele[kind, gg, 36 * gg + u, q, row] = 1
                selb[kind, gg, tap, 4 * gg + a, q, row] = 1
    bf = lambda v, *s: jnp.asarray(v.reshape(s), BF)
    return dict(
        pg=bf(pg, GROUPS, 256, 256),
        ry=bf(ry, 1152, 512),
        selm=bf(selm, 192, 128),
        sele=bf(sele, 2, 3, 128, 192),
        selb=bf(selb, 2, 3, 144, 192),
    )


def prep_constants():
    cs = np.zeros((GW, 128), np.float32)
    cse = np.zeros((GW, 112), np.float32)
    csee = np.zeros((GW, 128), np.float32)
    rs = np.zeros((112, 99), np.float32)
    rsm = np.zeros((99, 128), np.float32)
    rse = np.zeros((112, 99), np.float32)
    for a in range(4):
        for l in range(32):
            cs[33 * a + l, 32 * a + l] = 1
        cse[33 * a + 32, 99 + a] = 1
    for lane in range(128):
        csee[33 * (lane % 4) + 32, lane] = 1
    for j in range(3):
        for l in range(32):
            rs[32 * j + l, 33 * j + l] = 1
            rsm[33 * j + l, 32 * j + l] = 1
        rs[96 + j, 33 * j + 32] = 1
        rse[103 + j, 33 * j + 32] = 1
    return [jnp.asarray(v, BF) for v in (cs, cse, csee, rs, rsm, rse)]


def dot(a, b, dims=((1,), (0,))):
    return lax.dot_general(a, b, (dims, ((), ())), preferred_element_type=F32)


MESH = pl.DeviceIdType.MESH
DMA = pltpu.SemaphoreType.DMA
VM = pltpu.VMEM


def vspec():
    return pl.BlockSpec(memory_space=VM)


def struct(shape, dtype):
    return jax.ShapeDtypeStruct(shape, dtype)


def lanes_of(g, width=1):
    if isinstance(g, int):
        return pl.ds(g * 128, 128 * width)
    return pl.ds(pl.multiple_of(g * 128, 128), 128 * width)


def rows_at(start, size):
    if isinstance(start, int):
        return pl.ds(start, size)
    return pl.ds(pl.multiple_of(start, 16), size)


def lane_iota(rows):
    return lax.broadcasted_iota(jnp.int32, (rows, 128), 1)


def half_tanh(v):
    return 0.5 * jnp.tanh(0.5 * v) + 0.5


def place():
    dp = lax.axis_index("dp")
    s = lax.axis_index("shard")
    return (s // 2) % 4, s // 16, dp * 2 + (s // 8) % 2, s % 2


def device(x, y, z, c):
    return (z // 2, y * 16 + (z % 2) * 8 + x * 2 + c)


def send(src, dst, send_sem, recv_sem, to):
    copy = pltpu.make_async_remote_copy(
        src_ref=src, dst_ref=dst, send_sem=send_sem, recv_sem=recv_sem,
        device_id=to, device_id_type=MESH,
    )
    copy.start()
    return copy


def load_native(raw, xn):
    xn[...] = jnp.zeros_like(xn)
    for y in range(14):
        xn[y, 0:28, 0:1584] = raw[y].reshape(28, 1584)


def store_shifts(dst, main, lanes):
    for b in range(3):
        moved = main if b == 1 else pltpu.roll(main, (2 - 2 * b) % ROWS, 0)
        dst[b, 1:15, :, lanes] = moved.astype(BF).reshape(14, 32, 128)


def zero_borders(dst):
    zeros = jnp.zeros((3, 32, LANES), BF)
    dst[:, 0] = zeros
    dst[:, 15] = zeros


def tap_slice(src, tap, lanes, mirrored):
    a, b = tap // 3, tap % 3
    if mirrored:
        a, b = 2 - a, 2 - b
    return src[b, a : a + 14, :, lanes].reshape(ROWS, 128)


def tap_concat(src, lanes, mirrored, extra=None):
    pieces = [tap_slice(src, tap, lanes, mirrored) for tap in range(9)]
    if extra is not None:
        pieces.append(extra)
    return jnp.concatenate(pieces, axis=1)


def piece_of(b):
    s = {t: (b + 27 - t) // 27 for t in (3, 7, 10, 13, 17, 20, 24)}
    x = s[3] + s[7] + s[10] - 3 * s[13] + s[17] + s[20] + s[24]
    pos = b - 3 * s[3] - 4 * s[7] - 3 * s[10] - 3 * s[17] - 4 * s[20] - 4 * s[24]
    return x, pos


def fin_constants():
    q_m = np.zeros((128, 136), np.float32)
    q_o = np.zeros((3, 144, GW), np.float32)
    for a in range(4):
        for l in range(32):
            q_m[32 * a + l, 33 * a + l] = 1
            q_o[:, 32 * a + l, 33 * a + l] = 1
        for gg in range(3):
            q_o[gg, 128 + 4 * gg + a, 33 * a + 32] = 1
    return jnp.asarray(q_m, BF), jnp.asarray(q_o, BF)


IN_NAMES = (
    "idx", "tile", "cs", "cse", "csee", "rs", "rsm", "rse", "gain", "bias",
    "pg_h", "ry_h", "selm_h", "sele_h", "selb_h", "qm_h", "qo_h", "x_hbm", "up_hbm",
)
LOADED = ("pg", "ry", "selm", "sele", "selb", "qm", "qo")
OUT_NAMES = ("out_hbm", "ig_hbm", "kg", "gg_out", "bg_out")


def scratch_list():
    sets = dict(
        pay=VM((4, 112, 128), BF),
        gat=VM((256, 112, 128), BF),
        xb=VM((3, 16, 32, LANES), BF),
        ghb=VM((3, 16, 32, LANES), BF),
        ex=VM((ROWS, 512), BF),
        eg=VM((ROWS, 512), BF),
        bm=VM((GROUPS, 1152, 128), BF),
        ta=VM((GROUPS, 12, 16, 128), BF),
        me=VM((1152, 128), BF),
        hid=VM((ROWS, LANES), BF),
        gs=VM((ROWS, LANES), F32),
        ga=VM((ROWS, LANES), F32),
        upp=VM((ROWS, LANES), BF),
        bo=VM((ROWS, LANES), BF),
        raw=VM((14, 14, 2, 1584), BF),
        raw2=VM((14, 14, 2, 1584), BF),
        xn=VM((14, 32, LANES), BF),
        acc=VM((ROWS + 16, 128), F32),
        mec=VM((16, 1152), F32),
        bg=VM((1280, 256), BF),
        wt=VM((256, 1280), BF),
        tr=VM((128, 512), BF),
        g12t=VM((128, ROWS), BF),
        st=VM((2, 4, 4, 512, 128), BF),
        r0=VM((4, 4, 512, 128), BF),
        ra=VM((4, 256, 128), BF),
        rb=VM((4, 256, 128), BF),
        rp=VM((4, 512, 128), BF),
        rm=VM((4, 512, 128), BF),
        cur2=VM((4, 512, 128), BF),
        r2=VM((3, 512, 128), BF),
        cur3=VM((8, 64, 128), BF),
        r3=VM((7, 64, 128), BF),
        hh=VM((2, 4, 8, 64, 128), BF),
        sums=VM((2, 16, 128), F32),
        gsum=VM((2, 16, 128), F32),
        lsum=VM((2, 16, 128), F32),
        par=VM((2, 16, 128), F32),
        pf=VM((16, LANES), F32),
        pn=VM((16, LANES), BF),
        og=VM((2, LANES), F32),
        pg=VM((GROUPS, 256, 256), BF),
        ry=VM((1152, 512), BF),
        selm=VM((192, 128), BF),
        sele=VM((2, 3, 128, 192), BF),
        selb=VM((2, 3, 144, 192), BF),
        qm=VM((128, 136), BF),
        qo=VM((3, 144, GW), BF),
        s_in=DMA((2,)),
        s_k=DMA((7,)),
        s_out=DMA((2,)),
        s_sib=DMA((1,)), r_sib=DMA((1,)),
        s_z=DMA((11, 2)), r_z=DMA((11, 2)),
        s_u=DMA((2, 4)), r_u=DMA((2, 4)),
        s_v=DMA((8, 4)), r_v=DMA((8, 4)),
        s_d=DMA((33,)), r_d=DMA((33,)),
        s_c=DMA((16,)), r_c=DMA((16,)),
        s_1=DMA((6, 4)), r_1=DMA((6, 4)),
        s_2=DMA((3,)), r_2=DMA((3,)),
        s_3=DMA((7,)), r_3=DMA((7,)),
        s_4=DMA((7,)), r_4=DMA((7,)),
        s_5=DMA((11,)), r_5=DMA((11,)),
        s_a=DMA((2, 25)), r_a=DMA((2, 25)),
        buf_c=VM((2, 16, 128), F32),
        buf_p=VM((2, 16, 16, 128), F32),
        buf_z=VM((2, 8, 16, 128), F32),
    )
    return sets


class Refs:
    pass


def mega_body(*refs):
    r = Refs()
    names = list(IN_NAMES) + list(OUT_NAMES) + list(scratch_list())
    for name, ref in zip(names, refs, strict=True):
        setattr(r, name, ref)
    x, y, z, c = place()
    u = x * (1 - c) + y * c
    v = y * (1 - c) + x * c
    zl = z % 2
    oz = 1 - zl
    sib = device(x, y, z, 1 - c)

    def at_u(k):
        return device(k * (1 - c) + x * c, y * (1 - c) + k * c, z, c)

    def at_v(k):
        return device(x * (1 - c) + k * c, k * (1 - c) + y * c, z, c)

    others = [sib]
    others += [device((x + k % 4) % 4, (y + k // 4) % 4, z, c) for k in range(1, 16)]
    others += [device((x + k) % 4, y, z, 1 - c) for k in range(1, 4)]
    others += [device(x, y, (z + k) % 8, c) for k in range(1, 8)]
    barrier = pltpu.get_barrier_semaphore()
    for d in others:
        pl.semaphore_signal(barrier, inc=1, device_id=d, device_id_type=MESH)
    in_x = pltpu.make_async_copy(r.x_hbm, r.raw, r.s_in.at[0])
    in_x.start()
    in_up = pltpu.make_async_copy(r.up_hbm, r.raw2, r.s_in.at[1])
    in_up.start()
    loads = [
        pltpu.make_async_copy(getattr(r, name + "_h"), getattr(r, name), r.s_k.at[n])
        for n, name in enumerate(LOADED)
    ]
    for load in loads:
        load.start()

    def split3(val):
        hi = val.astype(BF).astype(F32)
        mid = (val - hi).astype(BF).astype(F32)
        return hi, mid, val - hi - mid

    r.pf[...] = jnp.zeros_like(r.pf)
    for n, ref in ((0, r.gain), (3, r.bias)):
        for k, part in enumerate(split3(ref[...].reshape(1, 1584))):
            r.pf[n + k : n + k + 1, 0:1584] = part
    r.pn[...] = r.pf[...].astype(BF)
    r.lsum[...] = jnp.zeros_like(r.lsum)
    for s in range(4):
        t = r.tile[s]
        w = dot(t, r.cs[...]).astype(BF)
        we = dot(t, r.cse[...]).astype(BF)
        wee = dot(t, r.csee[...]).astype(BF)
        full = dot(r.rs[...], w) + dot(we, r.rsm[...], ((0,), (0,))) + dot(r.rse[...], wee)
        r.pay[s] = full.astype(BF)
    pl.semaphore_wait(barrier, len(others))
    sends = []

    acc = r.acc

    def first_x():
        for load in loads:
            load.wait()
        in_x.wait()
        load_native(r.raw, r.xn)
        zero_borders(r.xb)
        acc[...] = jnp.zeros_like(acc)

    def permute(lo, hi, sink):
        def step(g, carry):
            rows = jnp.concatenate(
                [r.xn[:, :, lanes_of(g, 2)].reshape(ROWS, 256), r.pn[:, lanes_of(g, 2)]], axis=0
            )
            p = dot(rows, r.pg[g])
            sink(g, p[:, :128])
            acc[...] += p[:, 128:]
            return carry

        lax.fori_loop(lo, hi, step, 0)

    def row_of(k, t):
        return (k, pl.ds(t, 1), slice(None))

    def keep_x(g, val):
        store_shifts(r.xb, val[0:ROWS], lanes_of(g))
        p = val[ROWS:]
        r.par[row_of(0, g)] = p[0:1] + p[1:2] + p[2:3]
        r.par[row_of(1, g)] = p[3:4] + p[4:5] + p[5:6]

    def keep_up(g, val):
        r.upp[:, lanes_of(g)] = val[0:ROWS].astype(BF)

    def last_x():
        keep_x(GROUPS, acc[...])
        r.ex[...] = dot(tap_concat(r.xb, lanes_of(12), False), r.ry[...]).astype(BF)

    def first_up():
        in_up.wait()
        load_native(r.raw2, r.xn)
        zero_borders(r.ghb)
        acc[...] = jnp.zeros_like(acc)

    thunks = [first_x]
    thunks += [lambda k=k: permute(3 * k, 3 * k + 3, keep_x) for k in range(4)]
    thunks += [last_x, first_up]
    thunks += [lambda k=k: permute(3 * k, 3 * k + 3, keep_up) for k in range(4)]
    thunks += [lambda: keep_up(GROUPS, acc[...])]

    def work():
        if thunks:
            thunks.pop(0)()

    gat = r.gat

    def chunk(i, j, zz):
        lin = c * 128 + ((v + i) % 4) * 32 + ((u + j) % 4) * 8 + zz * 4
        return lambda h=None: gat.at[pl.ds(lin, 4)] if h is None else gat.at[pl.ds(lin + 2 * h, 2)]

    mine = c * 128 + v * 32 + u * 8 + zl * 4 + c * 2
    other = (1 - c) * 128 + u * 32 + v * 8 + zl * 4 + c * 2
    gat[pl.ds(mine, 2)] = r.pay[pl.ds(2 * c, 2)]
    gat[pl.ds(other, 2)] = r.pay[pl.ds(2 - 2 * c, 2)]
    mine, other = gat.at[pl.ds(mine, 2)], gat.at[pl.ds(other, 2)]
    sib_copy = send(other, other, r.s_sib.at[0], r.r_sib.at[0], sib)
    own_copy = send(mine, mine, r.s_d.at[32], r.r_d.at[32], sib)
    sends += [sib_copy, own_copy]
    sib_copy.wait_recv()

    k = chunk(0, 0, zl)
    def spread_z(m, k):
        pair = [send(k(0), k(0), r.s_z.at[m, 0], r.r_z.at[m, 0], device(x, y, (z + 1) % 8, c)),
                send(k(1), k(1), r.s_z.at[m, 1], r.r_z.at[m, 1], device(x, y, (z + 7) % 8, c))]
        sends.extend(pair)
        return pair

    z0, z1 = spread_z(0, k)

    def spread(n, k, ss, rs, at, p):
        pair = [send(k(), k(), ss.at[n, 0], rs.at[n, 0], at((p + 1) % 4)),
                send(k(), k(), ss.at[n, 1], rs.at[n, 1], at((p + 3) % 4))]
        sends.extend(pair)
        return pair

    def spread_u(n, zz):
        return spread(n, chunk(0, 0, zz), r.s_u, r.r_u, at_u, u)

    def spread_v(n, k):
        return spread(n, k, r.s_v, r.r_v, at_v, v)

    def pass_on(n, k):
        sends.append(send(k(), k(), r.s_d.at[n], r.r_d.at[n], sib))

    order = [(0, zl), (0, oz), (3, zl), (1, zl), (3, oz), (1, oz), (2, zl), (2, oz)]
    ring_u, ring_v = {}, {}
    ring_u[0] = spread_u(0, zl)
    ring_v[0] = spread_v(0, chunk(0, 0, zl))
    work()
    z0.wait_recv()
    z1.wait_recv()
    ring_u[1] = spread_u(1, oz)
    ring_v[1] = spread_v(1, chunk(0, 0, oz))
    pass_on(1, chunk(0, 0, oz))
    half_u = {}
    for n, zz in ((0, zl), (1, oz)):
        work()
        ring_u[n][0].wait_recv()
        k = chunk(0, 3, zz)
        h0 = send(k(0), k(0), r.s_u.at[n, 2], r.r_u.at[n, 2], at_u((u + 1) % 4))
        ring_v[2 + 2 * n] = spread_v(2 + 2 * n, k)
        pass_on(2 + 2 * n, k)
        ring_u[n][1].wait_recv()
        k = chunk(0, 1, zz)
        h1 = send(k(1), k(1), r.s_u.at[n, 3], r.r_u.at[n, 3], at_u((u + 3) % 4))
        ring_v[3 + 2 * n] = spread_v(3 + 2 * n, k)
        pass_on(3 + 2 * n, k)
        sends += [h0, h1]
        half_u[n] = (h0, h1)
    for n, zz in ((0, zl), (1, oz)):
        work()
        half_u[n][0].wait_recv()
        half_u[n][1].wait_recv()
        k = chunk(0, 2, zz)
        ring_v[6 + n] = spread_v(6 + n, k)
        pass_on(6 + n, k)
    half_v = {}
    for n, (j, zz) in enumerate(order):
        work()
        ring_v[n][0].wait_recv()
        k = chunk(3, j, zz)
        h0 = send(k(0), k(0), r.s_v.at[n, 2], r.r_v.at[n, 2], at_v((v + 1) % 4))
        pass_on(8 + n, k)
        ring_v[n][1].wait_recv()
        k = chunk(1, j, zz)
        h1 = send(k(1), k(1), r.s_v.at[n, 3], r.r_v.at[n, 3], at_v((v + 3) % 4))
        pass_on(16 + n, k)
        sends += [h0, h1]
        half_v[n] = (h0, h1)
    for n, (j, zz) in enumerate(order):
        half_v[n][0].wait_recv()
        half_v[n][1].wait_recv()
        pass_on(24 + n, chunk(2, j, zz))
    while thunks:
        work()
    for n in range(1, 32):
        k = gat.at[pl.ds((1 - c) * 128, 4)]
        pltpu.make_async_remote_copy(
            src_ref=k, dst_ref=k, send_sem=r.s_d.at[n], recv_sem=r.r_d.at[n],
            device_id=sib, device_id_type=MESH,
        ).wait_recv()
    own_copy.wait_recv()
    for copy in sends:
        copy.wait_send()
    sends = []

    def pull(t, carry):
        g, q = t // 12, t % 12
        s = r.idx[t]
        r.bm[g, pl.ds(pl.multiple_of(q * 96, 32), 96), :] = gat[s, 0:96, :]
        r.ta[g, q] = gat[s, 96:112, :]
        return carry

    lax.fori_loop(0, 144, pull, 0)
    for q in range(12):
        m = dot(r.ta[:, q].reshape(192, 128), r.selm[...], ((0,), (0,)))
        r.me[96 * q : 96 * q + 96, :] = m[0:96].astype(BF)
    acc[...] = jnp.zeros_like(acc)
    valid = (lax.broadcasted_iota(jnp.int32, (ROWS, 128), 0) % 32) < 28

    def stat(h, t):
        h = jnp.where(valid, h.astype(F32), 0.0)
        r.lsum[row_of(0, t)] = jnp.sum(h, axis=0, keepdims=True)
        r.lsum[row_of(1, t)] = jnp.sum(h * h, axis=0, keepdims=True)

    def fstep(yy, carry):
        for gg in range(3):
            g = 3 * yy + gg
            here = (lane_iota(1152) // 4) == yy * 4 + gg
            bg = r.bg
            bg[0:1152, 0:128] = r.bm[g]
            bg[0:1152, 128:256] = jnp.where(here, r.me[...].astype(F32), 0.0).astype(BF)
            tails = r.ta[g].reshape(192, 128)
            bg[1152:1280, 0:128] = dot(r.sele[0, gg], tails).astype(BF)
            ee = jnp.where(here[0:128], dot(r.sele[1, gg], tails), 0.0)
            bg[1152:1280, 128:256] = ee.astype(BF)
            a = tap_concat(r.xb, lanes_of(g), False, r.ex[:, lanes_of(yy)])
            p = dot(a, bg[...])
            h = p[:, :128].astype(BF)
            r.hid[:, lanes_of(g)] = h
            stat(h, g)
            acc[0:ROWS, :] += p[:, 128:]
        return carry

    lax.fori_loop(0, 4, fstep, 0)
    h = acc[0:ROWS, :].astype(BF)
    r.hid[:, 1536:1664] = h
    stat(h, 12)

    def all_sum(k, src, dst, fill):
        def share(buf, n, p, base, dev):
            copies = [
                send(buf.at[p], buf.at[p], r.s_a.at[k, base + i], r.r_a.at[k, base + i], dev((p + i) % n))
                for i in range(1, n)
            ]
            sends.extend(copies)
            if fill:
                fill.pop(0)()
            for copy in copies:
                copy.wait_recv()
            total = buf[0]
            for i in range(1, n):
                total = total + buf[i]
            return total

        half = send(src.at[1 - c], r.buf_c.at[k], r.s_a.at[k, 0], r.r_a.at[k, 0], sib)
        half.wait_recv()
        plane, line = r.buf_p.at[k], r.buf_z.at[k]
        p = y * 4 + x
        plane[p] = src[c] + r.buf_c[k]
        line[z] = share(plane, 16, p, 0, lambda q: device(q % 4, q // 4, z, c))
        dst[c] = share(line, 8, z, 16, lambda q: device(x, y, q, c))
        rest = send(dst.at[c], dst.at[c], r.s_a.at[k, 24], r.r_a.at[k, 24], sib)
        rest.wait_recv()
        half.wait_send()
        sends.append(rest)

    def make_tr():
        tr_in = jnp.concatenate([r.me[128 * tap : 128 * tap + 128] for tap in range(9)], axis=1)
        r.tr[...] = dot(tr_in, r.ry[...]).astype(BF)
        r.wt[128:256, :] = jnp.zeros((128, 1280), BF)

    all_sum(0, r.lsum, r.sums, [make_tr])

    def tile(t, carry):
        lanes = lanes_of(t)
        avg = r.sums[row_of(0, t)] / TOTAL
        inv = lax.rsqrt(r.sums[row_of(1, t)] / TOTAL - avg * avg + EPSILON)
        gain, bias = r.par[row_of(0, t)], r.par[row_of(1, t)]
        s1 = jnp.zeros((8, 128), F32)
        s2 = jnp.zeros((8, 128), F32)
        for k in range(28):
            rows = pl.ds(16 * k, 16)
            xv = r.xb[1, 1 + k // 2, 16 * (k % 2) : 16 * (k % 2) + 16, lanes].astype(F32)
            normed = (r.hid[rows, lanes].astype(F32) - avg) * inv
            aff = gain * normed + bias
            sa = half_tanh(aff)
            act = aff * sa
            summed = xv + act
            ss = half_tanh(summed)
            out = summed * ss
            r.bo[rows, lanes] = out.astype(BF)
            gsv = r.upp[rows, lanes].astype(F32) * (ss + out * (1.0 - ss))
            gav = gsv * (sa + act * (1.0 - sa))
            r.gs[rows, lanes] = gsv
            r.ga[rows, lanes] = gav
            p = gav * normed
            s1 = s1 + (p[0:8] + p[8:16])
            s2 = s2 + (gav[0:8] + gav[8:16])
        r.lsum[row_of(0, t)] = jnp.sum(s1, axis=0, keepdims=True)
        r.lsum[row_of(1, t)] = jnp.sum(s2, axis=0, keepdims=True)
        return carry

    lax.fori_loop(0, 13, tile, 0)

    def keep_sums(lanes, whole):
        q = whole[ROWS:]
        r.og[0:1, lanes] = q[0:1] + q[1:2] + q[2:3]
        r.og[1:2, lanes] = q[3:4] + q[4:5] + q[5:6]

    def unpermute(lo, hi, src):
        def step(g, carry):
            pair = jnp.concatenate([src(g), src(GROUPS)], axis=1)
            rows = jnp.concatenate([r.pn[:, lanes_of(g)], r.pn[:, 1536:1664]], axis=1)
            p = dot(jnp.concatenate([pair, rows], axis=0), r.pg[g], ((1,), (1,)))
            whole = acc[...] + p[:, :128]
            acc[...] = p[:, 128:]
            r.xn[:, :, lanes_of(g)] = whole[0:ROWS].astype(BF).reshape(14, 32, 128)
            keep_sums(lanes_of(g), whole)
            return carry

        if lo == 0:
            acc[...] = jnp.zeros_like(acc)
        lax.fori_loop(lo, hi, step, 0)

    def write_out(raw, hbm, n):
        r.xn[:, :, 1536:1664] = acc[0:ROWS, :].astype(BF).reshape(14, 32, 128)
        keep_sums(lanes_of(12), acc[...])
        for yy in range(14):
            raw[yy] = r.xn[yy, 0:28, 0:1584].reshape(14, 2, 1584)
        copy = pltpu.make_async_copy(raw, hbm, r.s_out.at[n])
        copy.start()
        return copy

    outs = []
    from_bo = lambda g: r.bo[:, lanes_of(g)]
    all_sum(1, r.lsum, r.gsum, [
        lambda: unpermute(0, 8, from_bo),
        lambda: (unpermute(8, 12, from_bo), outs.append(write_out(r.raw, r.out_hbm, 0))),
    ])

    def gtile(t, carry):
        lanes = lanes_of(t)
        avg = r.sums[row_of(0, t)] / TOTAL
        inv = lax.rsqrt(r.sums[row_of(1, t)] / TOTAL - avg * avg + EPSILON)
        scale = r.par[row_of(0, t)] * inv
        c1 = r.gsum[row_of(1, t)] / TOTAL
        c2 = r.gsum[row_of(0, t)] / TOTAL
        normed = (r.hid[:, lanes].astype(F32) - avg) * inv
        gh = scale * (r.ga[:, lanes] - c1 - normed * c2)
        store_shifts(r.ghb, jnp.where(valid, gh, 0.0), lanes)
        return carry

    lax.fori_loop(0, 13, gtile, 0)
    r.eg[...] = dot(tap_concat(r.ghb, lanes_of(12), True), r.ry[...]).astype(BF)
    g12 = r.ghb[1, 1:15, :, 1536:1664].reshape(ROWS, 128)
    r.g12t[...] = g12.astype(F32).T.astype(BF)

    st, r0 = r.st, r.r0

    turns = (2, 1, 3, 0)
    low, high = pl.ds(0, 256), pl.ds(256, 256)

    def place_of(ay, ax, half):
        yy, xx = (y + ay) % 4, (x + ax) % 4
        return yy * (1 - half) + xx * half, xx * (1 - half) + yy * half

    def core_copy(ay, ax):
        pv, pu = place_of(ay, ax, 1 - c)
        return pltpu.make_async_remote_copy(
            src_ref=st.at[1 - c, pv, pu], dst_ref=r0.at[pv, pu],
            send_sem=r.s_c.at[4 * ay + ax], recv_sem=r.r_c.at[4 * ay + ax],
            device_id=sib, device_id_type=MESH,
        )

    def ring(m, ru):
        rv, rows, dst, way = (
            (2, low, r.ra.at[ru], 1),
            (2, high, r.rb.at[ru], 3),
            (1, high, r.rp.at[ru, high], 1),
            (1, low, r.rp.at[ru, low], 1),
            (3, low, r.rm.at[ru, low], 3),
            (3, high, r.rm.at[ru, high], 3),
        )[m]
        return pltpu.make_async_remote_copy(
            src_ref=r0.at[(v + rv) % 4, (u + ru) % 4, rows], dst_ref=dst,
            send_sem=r.s_1.at[m, ru], recv_sem=r.r_1.at[m, ru],
            device_id=at_v((v + way) % 4), device_id_type=MESH,
        )

    def launch(rv, ru):
        for m in {2: (0, 1), 1: (2,), 3: (4,), 0: ()}[rv]:
            ring(m, ru).start()

    def add_core(ay):
        for ax in turns:
            core_copy(ay, ax).wait_recv()
            pv, pu = place_of(ay, ax, c)

            def add(n, carry):
                row = pl.ds(pl.multiple_of(n * 128, 128), 128)
                total = st[c, pv, pu, row, :].astype(F32) + r0[pv, pu, row, :].astype(F32)
                r0[pv, pu, row, :] = total.astype(BF)
                return carry

            lax.fori_loop(0, 4, add, 0)
            if ax == ay:
                launch(ay, ax)
            else:
                @pl.when(c == 0)
                def _():
                    launch(ay, ax)

                @pl.when(c == 1)
                def _():
                    launch(ax, ay)

    def add_half(ru, m, buf, rv, start):
        ring(m, ru).wait_recv()
        pv, pu = (v + rv) % 4, (u + ru) % 4
        for n in range(2):
            row, own = pl.ds(128 * n, 128), pl.ds(start + 128 * n, 128)
            total = r0[pv, pu, own, :].astype(F32) + buf[ru, row, :].astype(F32)
            r0[pv, pu, own, :] = total.astype(BF)

    def relay(ru):
        add_half(ru, 0, r.ra, 1, 0)
        ring(3, ru).start()
        add_half(ru, 1, r.rb, 3, 256)
        ring(5, ru).start()

    def wstep(k):
        yy = (y + turns[k]) % 4
        acc[0:144, :] = jnp.zeros((144, 128), F32)
        r.mec[...] = jnp.zeros_like(r.mec)
        lhs12 = r.g12t[rows_at(16 * yy, 16), :]
        for gg in range(3):
            g = 3 * yy + gg
            main = r.ghb[1, 1:15, :, lanes_of(g)].reshape(ROWS, 128)
            lhs = jnp.concatenate([main.astype(F32).T.astype(BF), lhs12], axis=0)
            a = tap_concat(r.xb, lanes_of(g), False, r.ex[:, lanes_of(yy)])
            p = dot(lhs, a)
            for tap in range(9):
                px, pos = piece_of(gg * 9 + tap)
                blk = p[0:128, tap * 128 : tap * 128 + 128].astype(BF)
                st[0, yy, px, pos * 64 : pos * 64 + 64, :] = blk[0:64]
                st[1, px, yy, pos * 64 : pos * 64 + 64, :] = blk[64:128]
            rowsel = (lax.broadcasted_iota(jnp.int32, (16, 1152), 0) // 4) == gg
            r.mec[...] += jnp.where(rowsel, p[128:144, 0:1152], 0.0)
            lane = lane_iota(144)
            lanesel = (lane >= 36 * gg) & (lane < 36 * gg + 36)
            row = lax.broadcasted_iota(jnp.int32, (144, 128), 0)
            rowsel = (row < 128) | (row // 4 == 32 + gg)
            acc[0:144, :] += jnp.where(lanesel & rowsel, p[:, 1152:1280], 0.0)
        zeros = jnp.zeros((128, 128), BF)
        for px in range(3):
            for j in range(3):
                tap = 3 * px + j
                st[0, yy, px, 448 + 16 * j : 464 + 16 * j, :] = r.mec[:, 128 * tap : 128 * tap + 128].astype(BF)
            st[1, px, yy, 448:496, :] = acc[48 * px : 48 * px + 48, :].astype(BF)
            st[0, yy, px, 496:512, :] = zeros[0:16]
            st[1, px, yy, 496:512, :] = zeros[0:16]
        st[0, yy, 3, 384:512, :] = zeros
        st[1, 3, yy, 384:512, :] = zeros
        for ax in turns:
            core_copy(turns[k], ax).start()
        if k > 0:
            add_core(turns[k - 1])

    for k in range(4):
        wstep(k)
    add_core(turns[3])

    def back_part(yy, lo, hi):
        block = pl.ds(128 + 16 * yy, 16)
        wt = r.wt

        def bstep(gg, carry):
            g = 3 * yy + gg
            for tap in range(9):
                wt[0:128, 128 * tap : 128 * tap + 128] = r.bm[g, 128 * tap : 128 * tap + 128, :]
            lane = lane_iota(128)
            lanesel = (lane >= 36 * gg) & (lane < 36 * gg + 36)
            wt[0:128, 1152:1280] = jnp.where(lanesel, r.tr[:, lanes_of(yy)].astype(F32), 0.0).astype(BF)
            tails = r.ta[g].reshape(192, 128)
            bl = dot(r.selb[0, gg], tails).astype(BF)
            be = dot(r.selb[1, gg], tails)
            low = jnp.zeros((16, 128), F32)
            lane = lane_iota(16)
            for tap in range(9):
                wt[block, 128 * tap : 128 * tap + 128] = bl[16 * tap : 16 * tap + 16]
                low = jnp.where((lane // 4) == 9 * gg + tap, be[16 * tap : 16 * tap + 16], low)
            wt[block, 1152:1280] = low.astype(BF)
            a = tap_concat(r.ghb, lanes_of(g), True, r.eg[:, lanes_of(yy)])
            p = dot(a, wt[...], ((1,), (1,)))
            r.gs[:, lanes_of(g)] += p[:, :128]
            r.gs[:, 1536:1664] += p[:, 128:]
            return carry

        lax.fori_loop(lo, hi, bstep, 0)
        if hi == 3:
            wt[block, :] = jnp.zeros((16, 1280), BF)

    u_copies = []

    def sum_v(ru):
        for m in range(2, 6):
            ring(m, ru).wait_recv()
        pu = (u + ru) % 4
        for n in range(4):
            row = pl.ds(128 * n, 128)
            total = r0[v, pu, row, :].astype(F32) + r.rp[ru, row, :].astype(F32)
            r.cur2[ru, row, :] = (total + r.rm[ru, row, :].astype(F32)).astype(BF)
        if ru:
            u_copies.append(
                send(r.cur2.at[ru], r.r2.at[ru - 1], r.s_2.at[ru - 1], r.r_2.at[ru - 1], at_u(pu))
            )

    parts = [(yy, lo, hi) for yy in range(4) for lo, hi in ((0, 1), (1, 2), (2, 3))]

    def back_next(n=1):
        for _ in range(n):
            if parts:
                back_part(*parts.pop(0))

    for ru in turns:
        back_next()
        relay(ru)
    back_next()
    for ru in turns:
        back_next()
        sum_v(ru)
    back_next(12)
    from_gs = lambda g: r.gs[:, lanes_of(g)].astype(BF)
    for t in range(13):
        for n in range(2):
            for k, part in enumerate(split3(r.gsum[n, t : t + 1, :])):
                r.pf[3 * n + k : 3 * n + k + 1, lanes_of(t)] = part
    r.pn[...] = r.pf[...].astype(BF)
    unpermute(0, 4, from_gs)
    for copy in u_copies:
        copy.wait_recv()
    sends += u_copies
    for n in range(8):
        row = pl.ds(64 * n, 64)
        total = r.cur2[0, row, :].astype(F32)
        for rel in range(3):
            total = total + r.r2[rel, row, :].astype(F32)
        r.cur3[n] = total.astype(BF)
    copies = []
    for k in range(1, 8):
        q = (z + k) % 8
        copies.append(send(r.cur3.at[q], r.r3.at[k - 1], r.s_3.at[k - 1], r.r_3.at[k - 1], device(x, y, q, c)))
    sends += copies
    unpermute(4, 8, from_gs)
    for copy in copies:
        copy.wait_recv()
    total = r.cur3[z].astype(F32)
    for k in range(7):
        total = total + r.r3[k].astype(F32)
    hh = r.hh
    hh[c, x, z] = total.astype(BF)
    here = hh.at[c, x, z]
    copies = []
    for k in range(1, 8):
        q = (z + k) % 8
        copies.append(send(here, here, r.s_4.at[k - 1], r.r_4.at[k - 1], device(x, y, q, c)))
    sends += copies
    unpermute(8, 12, from_gs)
    outs.append(write_out(r.raw2, r.ig_hbm, 1))
    r.gg_out[...] = r.og[0:1, 0:1584].reshape(1584)
    r.bg_out[...] = r.og[1:2, 0:1584].reshape(1584)
    for copy in copies:
        copy.wait_recv()
    near = [(1, 6 - 3 * (x % 2) - 3 * (x // 3)), (3, 3 - 3 * (x % 2))]
    copies = [send(hh.at[c, x], hh.at[c, x], r.s_5.at[0], r.r_5.at[0], sib)]
    n = 1
    for cc in (c, 1 - c):
        for rel, pos in near:
            to = device((x + rel) % 4, y, z, cc)
            copies.append(send(hh.at[c, x, pos], hh.at[c, x, pos], r.s_5.at[n], r.r_5.at[n], to))
            copies.append(send(hh.at[c, x, 7], hh.at[c, x, 7], r.s_5.at[n + 1], r.r_5.at[n + 1], to))
            n += 2
        to = device((x + 2) % 4, y, z, cc)
        copies.append(send(hh.at[c, x, 7], hh.at[c, x, 7], r.s_5.at[n], r.r_5.at[n], to))
        n += 1
    for copy in copies:
        copy.wait_recv()
    sends += copies
    sp = (z % 2) * 8 + x * 2 + c
    b0 = (sp * 29403) // 17424 - sp // 15
    em = jnp.concatenate([hh[1, j, 7, 0:48, :] for j in range(3)], axis=0)
    for k in range(3):
        b = b0 + k
        px, pos = piece_of(b)
        tap = b % 9
        gg = b // 9
        main = jnp.concatenate([hh[0, px, pos], hh[1, px, pos]], axis=0)
        mrow = hh[0, tap // 3, 7, rows_at(16 * (tap % 3), 16), :]
        left = jnp.concatenate([main, mrow], axis=0)
        line = lax.broadcasted_iota(jnp.int32, (128, 136), 0) - (36 * gg + 4 * tap)
        unit = lax.broadcasted_iota(jnp.int32, (128, 136), 1)
        qe = jnp.where((line >= 0) & (line < 4) & (unit == 33 * line + 32), 1.0, 0.0).astype(BF)
        t1 = (dot(left, r.qm[...]) + dot(em, qe)).astype(BF)
        t2 = dot(t1, r.qo[gg], ((0,), (0,)))
        r.kg[pl.ds(132 * k, 132), :] = t2[0:132]

    for copy in sends:
        copy.wait_send()
    for ay in range(4):
        for ax in range(4):
            core_copy(ay, ax).wait_send()
    for m in range(6):
        for ru in range(4):
            ring(m, ru).wait_send()
    for copy in outs:
        copy.wait()


def mega(idx, tiles, gain, bias, xt, upt):
    k = constants()
    operands = [idx, tiles, *prep_constants(), gain, bias]
    operands += [k["pg"], k["ry"], k["selm"], k["sele"], k["selb"], *fin_constants(), xt, upt]
    anywhere = pl.BlockSpec(memory_space=pl.ANY)
    return pl.pallas_call(
        mega_body,
        in_specs=[pl.BlockSpec(memory_space=pltpu.SMEM)] + [vspec()] * 9 + [anywhere] * 9,
        out_specs=[anywhere, anywhere, vspec(), vspec(), vspec()],
        out_shape=[
            struct((14, 14, 2, 1584), BF),
            struct((14, 14, 2, 1584), BF),
            struct((396, GW), F32),
            struct((1584,), F32),
            struct((1584,), F32),
        ],
        scratch_shapes=list(scratch_list().values()),
        compiler_params=pltpu.CompilerParams(
            collective_id=1, has_side_effects=True, vmem_limit_bytes=VLIM
        ),
        name="block",
    )(*operands)


def finish_body(out_a, ig_a, out_b, ig_b, one, two, sem):
    pairs = [(out_a, one, out_b), (ig_a, two, ig_b)]
    loads = [pltpu.make_async_copy(src, mid, sem.at[n]) for n, (src, mid, _) in enumerate(pairs)]
    saves = [pltpu.make_async_copy(mid, dst, sem.at[2 + n]) for n, (_, mid, dst) in enumerate(pairs)]
    for load in loads:
        load.start()
    for load, save in zip(loads, saves):
        load.wait()
        save.start()
    for save in saves:
        save.wait()


def finish(out, ig):
    anywhere = pl.BlockSpec(memory_space=pl.ANY)
    return pl.pallas_call(
        finish_body,
        in_specs=[anywhere] * 2,
        out_specs=[anywhere] * 2,
        out_shape=[struct((14, 14, 2, 1584), BF)] * 2,
        scratch_shapes=[VM((14, 14, 2, 1584), BF)] * 2 + [DMA((4,))],
        name="finish",
    )(out, ig)


def tile_rows(tile_counts, owner_order):
    ranks = jnp.arange(64, dtype=jnp.int32)
    upto = (ranks[None, :] <= ranks[:, None]).astype(jnp.int32)
    run_end = jnp.sum(upto * tile_counts[None, :], axis=1)
    run_start = run_end - tile_counts
    t = jnp.arange(144, dtype=jnp.int32)[:, None]
    j = t - run_start[None, :]
    s = owner_order[None, :]
    y, zl, x, core = s // 16, (s // 8) % 2, (s // 2) % 4, s % 2
    vu = jnp.where(j < 2, y * 4 + x, x * 4 + y)
    spot = (j // 2) * 128 + vu * 8 + zl * 4 + core * 2 + j % 2
    held = (j >= 0) & (t < run_end[None, :])
    return jnp.sum(jnp.where(held, spot, 0), axis=1)


def local(block_input, upstream, kernel_tiles, tile_counts, owner_order, gain, bias):
    idx = tile_rows(tile_counts, owner_order)
    turn = lambda a: jnp.transpose(a, (1, 2, 0, 3))
    back = lambda a: jnp.transpose(a, (2, 0, 1, 3))
    out, ig, kg, gg, bg = mega(
        idx, kernel_tiles.reshape(4, 99, GW), gain, bias,
        turn(block_input), turn(upstream),
    )
    out, ig = finish(out, ig)
    sp = lax.axis_index("shard") % 16
    b0 = (sp * 29403) // 17424 - sp // 15
    kernel_grad = lax.dynamic_slice(kg.reshape(-1), (sp * 29403 - b0 * 17424,), (29403,))
    return (back(out), back(ig), kernel_grad, gg, bg)


def solution(mesh):
    return jax.shard_map(
        local,
        mesh=mesh,
        in_specs=(
            P(("dp", "shard"), None, None, None),
            P(("dp", "shard"), None, None, None),
            P("shard", None),
            P(),
            P(),
            P(),
            P(),
        ),
        out_specs=(
            P(("dp", "shard"), None, None, None),
            P(("dp", "shard"), None, None, None),
            P("shard"),
            P(),
            P(),
        ),
        check_vma=False,
    )
```

```python
import numpy as np
import jax
import jax.numpy as jnp
from jax import lax
from jax.experimental import pallas as pl
from jax.experimental.pallas import tpu as pltpu
from jax.sharding import PartitionSpec as P

GROUPS = 12
GW = 132
ROWS = 448
LANES = 1664
BF = jnp.bfloat16
F32 = jnp.float32
EPSILON = 1e-05
TOTAL = 100352
VLIM = 60 * 1024 * 1024


def extra_lane(g, a):
    return 16 * (g // 3) + 4 * (g % 3) + a


def constants():
    pg = np.zeros((GROUPS, 256, 256), np.float32)
    for g in range(GROUPS):
        for j in range(GW):
            a, l = j // 33, j % 33
            pg[g, 4 * g + j, 32 * a + l if l < 32 else 128 + extra_lane(g, a)] = 1
    ry = np.zeros((9, 128, 4, 128), np.float32)
    for g in range(GROUPS):
        for tap in range(9):
            for a in range(4):
                ry[tap, extra_lane(g, a), g // 3, 36 * (g % 3) + 4 * tap + a] = 1
    selm = np.zeros((GROUPS, 16, 128), np.float32)
    for g in range(GROUPS):
        for a in range(4):
            selm[g, 3 + a, extra_lane(g, a)] = 1
    sele = np.zeros((2, 3, 128, 12, 16), np.float32)
    selb = np.zeros((2, 3, 9, 16, 12, 16), np.float32)
    for gg in range(3):
        for u in range(36):
            q, j = u // 3, u % 3
            tap, a = u // 4, u % 4
            for kind, row in ((0, j), (1, 7 + j)):
                sele[kind, gg, 36 * gg + u, q, row] = 1
                selb[kind, gg, tap, 4 * gg + a, q, row] = 1
    bf = lambda v, *s: jnp.asarray(v.reshape(s), BF)
    return dict(
        pg=bf(pg, GROUPS, 256, 256),
        ry=bf(ry, 1152, 512),
        selm=bf(selm, 192, 128),
        sele=bf(sele, 2, 3, 128, 192),
        selb=bf(selb, 2, 3, 144, 192),
    )


def prep_constants():
    cs = np.zeros((GW, 128), np.float32)
    cse = np.zeros((GW, 112), np.float32)
    csee = np.zeros((GW, 128), np.float32)
    rs = np.zeros((112, 99), np.float32)
    rsm = np.zeros((99, 128), np.float32)
    rse = np.zeros((112, 99), np.float32)
    for a in range(4):
        for l in range(32):
            cs[33 * a + l, 32 * a + l] = 1
        cse[33 * a + 32, 99 + a] = 1
    for lane in range(128):
        csee[33 * (lane % 4) + 32, lane] = 1
    for j in range(3):
        for l in range(32):
            rs[32 * j + l, 33 * j + l] = 1
            rsm[33 * j + l, 32 * j + l] = 1
        rs[96 + j, 33 * j + 32] = 1
        rse[103 + j, 33 * j + 32] = 1
    return [jnp.asarray(v, BF) for v in (cs, cse, csee, rs, rsm, rse)]


def dot(a, b, dims=((1,), (0,))):
    return lax.dot_general(a, b, (dims, ((), ())), preferred_element_type=F32)


MESH = pl.DeviceIdType.MESH
DMA = pltpu.SemaphoreType.DMA
VM = pltpu.VMEM


def vspec():
    return pl.BlockSpec(memory_space=VM)


def struct(shape, dtype):
    return jax.ShapeDtypeStruct(shape, dtype)


def lanes_of(g, width=1):
    if isinstance(g, int):
        return pl.ds(g * 128, 128 * width)
    return pl.ds(pl.multiple_of(g * 128, 128), 128 * width)


def rows_at(start, size):
    if isinstance(start, int):
        return pl.ds(start, size)
    return pl.ds(pl.multiple_of(start, 16), size)


def lane_iota(rows):
    return lax.broadcasted_iota(jnp.int32, (rows, 128), 1)


def half_tanh(v):
    return 0.5 * jnp.tanh(0.5 * v) + 0.5


def place():
    dp = lax.axis_index("dp")
    s = lax.axis_index("shard")
    return (s // 2) % 4, s // 16, dp * 2 + (s // 8) % 2, s % 2


def device(x, y, z, c):
    return (z // 2, y * 16 + (z % 2) * 8 + x * 2 + c)


def send(src, dst, send_sem, recv_sem, to):
    copy = pltpu.make_async_remote_copy(
        src_ref=src, dst_ref=dst, send_sem=send_sem, recv_sem=recv_sem,
        device_id=to, device_id_type=MESH,
    )
    copy.start()
    return copy


def load_native(raw, xn):
    xn[...] = jnp.zeros_like(xn)
    for y in range(14):
        xn[y, 0:28, 0:1584] = raw[y].reshape(28, 1584)


def store_shifts(dst, main, lanes):
    for b in range(3):
        moved = main if b == 1 else pltpu.roll(main, (2 - 2 * b) % ROWS, 0)
        dst[b, 1:15, :, lanes] = moved.astype(BF).reshape(14, 32, 128)


def zero_borders(dst):
    zeros = jnp.zeros((3, 32, LANES), BF)
    dst[:, 0] = zeros
    dst[:, 15] = zeros


def tap_slice(src, tap, lanes, mirrored):
    a, b = tap // 3, tap % 3
    if mirrored:
        a, b = 2 - a, 2 - b
    return src[b, a : a + 14, :, lanes].reshape(ROWS, 128)


def tap_concat(src, lanes, mirrored, extra=None):
    pieces = [tap_slice(src, tap, lanes, mirrored) for tap in range(9)]
    if extra is not None:
        pieces.append(extra)
    return jnp.concatenate(pieces, axis=1)


def piece_of(b):
    s = {t: (b + 27 - t) // 27 for t in (3, 7, 10, 13, 17, 20, 24)}
    x = s[3] + s[7] + s[10] - 3 * s[13] + s[17] + s[20] + s[24]
    pos = b - 3 * s[3] - 4 * s[7] - 3 * s[10] - 3 * s[17] - 4 * s[20] - 4 * s[24]
    return x, pos


def fin_constants():
    q_m = np.zeros((128, 136), np.float32)
    q_o = np.zeros((3, 144, GW), np.float32)
    for a in range(4):
        for l in range(32):
            q_m[32 * a + l, 33 * a + l] = 1
            q_o[:, 32 * a + l, 33 * a + l] = 1
        for gg in range(3):
            q_o[gg, 128 + 4 * gg + a, 33 * a + 32] = 1
    return jnp.asarray(q_m, BF), jnp.asarray(q_o, BF)


IN_NAMES = (
    "idx", "tile", "cs", "cse", "csee", "rs", "rsm", "rse", "gain", "bias",
    "pg_h", "ry_h", "selm_h", "sele_h", "selb_h", "qm_h", "qo_h", "x_hbm", "up_hbm",
)
LOADED = ("pg", "ry", "selm", "sele", "selb", "qm", "qo")
OUT_NAMES = ("out_hbm", "ig_hbm", "kg", "gg_out", "bg_out")


def scratch_list():
    sets = dict(
        pay=VM((4, 112, 128), BF),
        gat=VM((256, 112, 128), BF),
        xb=VM((3, 16, 32, LANES), BF),
        ghb=VM((3, 16, 32, LANES), BF),
        ex=VM((ROWS, 512), BF),
        eg=VM((ROWS, 512), BF),
        bm=VM((GROUPS, 1152, 128), BF),
        ta=VM((GROUPS, 12, 16, 128), BF),
        me=VM((1152, 128), BF),
        hid=VM((ROWS, LANES), BF),
        gs=VM((ROWS, LANES), F32),
        ga=VM((ROWS, LANES), F32),
        upp=VM((ROWS, LANES), BF),
        bo=VM((ROWS, LANES), BF),
        raw=VM((14, 14, 2, 1584), BF),
        raw2=VM((14, 14, 2, 1584), BF),
        xn=VM((14, 32, LANES), BF),
        acc=VM((ROWS + 16, 128), F32),
        mec=VM((16, 1152), F32),
        bg=VM((3, 1280, 256), BF),
        kgs=VM((416, 256), F32),
        wt=VM((256, 1280), BF),
        tr=VM((128, 512), BF),
        g12t=VM((128, ROWS), BF),
        st=VM((2, 4, 4, 512, 128), BF),
        r0=VM((4, 4, 512, 128), BF),
        ra=VM((4, 256, 128), BF),
        rb=VM((4, 256, 128), BF),
        rp=VM((4, 512, 128), BF),
        rm=VM((4, 512, 128), BF),
        cur2=VM((4, 512, 128), BF),
        r2=VM((3, 512, 128), BF),
        cur3=VM((8, 64, 128), BF),
        r3=VM((7, 64, 128), BF),
        hh=VM((2, 4, 8, 64, 128), BF),
        sums=VM((2, 16, 128), F32),
        gsum=VM((2, 16, 128), F32),
        lsum=VM((2, 16, 128), F32),
        par=VM((2, 16, 128), F32),
        pf=VM((16, LANES), F32),
        pn=VM((16, LANES), BF),
        og=VM((2, LANES), F32),
        pg=VM((GROUPS, 256, 256), BF),
        ry=VM((1152, 512), BF),
        selm=VM((192, 128), BF),
        sele=VM((2, 3, 128, 192), BF),
        selb=VM((2, 3, 144, 192), BF),
        qm=VM((128, 136), BF),
        qo=VM((3, 144, GW), BF),
        s_in=DMA((2,)),
        s_k=DMA((7,)),
        s_out=DMA((2,)),
        s_sib=DMA((1,)), r_sib=DMA((1,)),
        s_z=DMA((11, 2)), r_z=DMA((11, 2)),
        s_u=DMA((2, 4)), r_u=DMA((2, 4)),
        s_v=DMA((8, 4)), r_v=DMA((8, 4)),
        s_d=DMA((33,)), r_d=DMA((33,)),
        s_c=DMA((16,)), r_c=DMA((16,)),
        s_1=DMA((6, 4)), r_1=DMA((6, 4)),
        s_2=DMA((3,)), r_2=DMA((3,)),
        s_3=DMA((7,)), r_3=DMA((7,)),
        s_4=DMA((7,)), r_4=DMA((7,)),
        s_5=DMA((11,)), r_5=DMA((11,)),
        s_a=DMA((2, 33)), r_a=DMA((2, 33)),
        buf_c=VM((2, 16, 128), F32),
        buf_p=VM((2, 16, 16, 128), F32),
        buf_z=VM((2, 2, 8, 16, 128), F32),
    )
    return sets


class Refs:
    pass


def mega_body(*refs):
    r = Refs()
    names = list(IN_NAMES) + list(OUT_NAMES) + list(scratch_list())
    for name, ref in zip(names, refs, strict=True):
        setattr(r, name, ref)
    x, y, z, c = place()
    u = x * (1 - c) + y * c
    v = y * (1 - c) + x * c
    zl = z % 2
    oz = 1 - zl
    sib = device(x, y, z, 1 - c)

    def at_u(k):
        return device(k * (1 - c) + x * c, y * (1 - c) + k * c, z, c)

    def at_v(k):
        return device(x * (1 - c) + k * c, k * (1 - c) + y * c, z, c)

    others = [sib]
    others += [device((x + k % 4) % 4, (y + k // 4) % 4, z, c) for k in range(1, 16)]
    others += [device((x + k) % 4, y, z, 1 - c) for k in range(1, 4)]
    others += [device(x, y, (z + k) % 8, cc) for k in range(1, 8) for cc in (c, 1 - c)]
    barrier = pltpu.get_barrier_semaphore()
    for d in others:
        pl.semaphore_signal(barrier, inc=1, device_id=d, device_id_type=MESH)
    in_x = pltpu.make_async_copy(r.x_hbm, r.raw, r.s_in.at[0])
    in_x.start()
    in_up = pltpu.make_async_copy(r.up_hbm, r.raw2, r.s_in.at[1])
    in_up.start()
    loads = [
        pltpu.make_async_copy(getattr(r, name + "_h"), getattr(r, name), r.s_k.at[n])
        for n, name in enumerate(LOADED)
    ]
    for load in loads:
        load.start()

    def split3(val):
        hi = val.astype(BF).astype(F32)
        mid = (val - hi).astype(BF).astype(F32)
        return hi, mid, val - hi - mid

    r.pf[...] = jnp.zeros_like(r.pf)
    for n, ref in ((0, r.gain), (3, r.bias)):
        for k, part in enumerate(split3(ref[...].reshape(1, 1584))):
            r.pf[n + k : n + k + 1, 0:1584] = part
    r.pn[...] = r.pf[...].astype(BF)
    r.lsum[...] = jnp.zeros_like(r.lsum)
    for s in range(4):
        t = r.tile[s]
        w = dot(t, r.cs[...]).astype(BF)
        we = dot(t, r.cse[...]).astype(BF)
        wee = dot(t, r.csee[...]).astype(BF)
        full = dot(r.rs[...], w) + dot(we, r.rsm[...], ((0,), (0,))) + dot(r.rse[...], wee)
        r.pay[s] = full.astype(BF)
    pl.semaphore_wait(barrier, len(others))
    sends = []

    acc = r.acc

    def first_x():
        for load in loads:
            load.wait()
        in_x.wait()
        load_native(r.raw, r.xn)
        zero_borders(r.xb)
        acc[...] = jnp.zeros_like(acc)

    def permute(lo, hi, sink):
        def step(g, carry):
            rows = jnp.concatenate(
                [r.xn[:, :, lanes_of(g, 2)].reshape(ROWS, 256), r.pn[:, lanes_of(g, 2)]], axis=0
            )
            p = dot(rows, r.pg[g])
            sink(g, p[:, :128])
            acc[...] += p[:, 128:]
            return carry

        lax.fori_loop(lo, hi, step, 0)

    def row_of(k, t):
        return (k, pl.ds(t, 1), slice(None))

    def keep_x(g, val):
        store_shifts(r.xb, val[0:ROWS], lanes_of(g))
        p = val[ROWS:]
        r.par[row_of(0, g)] = p[0:1] + p[1:2] + p[2:3]
        r.par[row_of(1, g)] = p[3:4] + p[4:5] + p[5:6]

    def keep_up(g, val):
        r.upp[:, lanes_of(g)] = val[0:ROWS].astype(BF)

    def last_x():
        keep_x(GROUPS, acc[...])
        r.ex[...] = dot(tap_concat(r.xb, lanes_of(12), False), r.ry[...]).astype(BF)

    def first_up():
        in_up.wait()
        load_native(r.raw2, r.xn)
        zero_borders(r.ghb)
        acc[...] = jnp.zeros_like(acc)

    thunks = [first_x]
    thunks += [lambda k=k: permute(3 * k, 3 * k + 3, keep_x) for k in range(4)]
    thunks += [last_x, first_up]
    thunks += [lambda k=k: permute(3 * k, 3 * k + 3, keep_up) for k in range(4)]
    thunks += [lambda: keep_up(GROUPS, acc[...])]

    def work():
        if thunks:
            thunks.pop(0)()

    gat = r.gat

    def chunk(i, j, zz):
        lin = c * 128 + ((v + i) % 4) * 32 + ((u + j) % 4) * 8 + zz * 4
        return lambda h=None: gat.at[pl.ds(lin, 4)] if h is None else gat.at[pl.ds(lin + 2 * h, 2)]

    mine = c * 128 + v * 32 + u * 8 + zl * 4 + c * 2
    other = (1 - c) * 128 + u * 32 + v * 8 + zl * 4 + c * 2
    gat[pl.ds(mine, 2)] = r.pay[pl.ds(2 * c, 2)]
    gat[pl.ds(other, 2)] = r.pay[pl.ds(2 - 2 * c, 2)]
    mine, other = gat.at[pl.ds(mine, 2)], gat.at[pl.ds(other, 2)]
    sib_copy = send(other, other, r.s_sib.at[0], r.r_sib.at[0], sib)
    own_copy = send(mine, mine, r.s_d.at[32], r.r_d.at[32], sib)
    sends += [sib_copy, own_copy]
    sib_copy.wait_recv()

    k = chunk(0, 0, zl)
    def spread_z(m, k):
        pair = [send(k(0), k(0), r.s_z.at[m, 0], r.r_z.at[m, 0], device(x, y, (z + 1) % 8, c)),
                send(k(1), k(1), r.s_z.at[m, 1], r.r_z.at[m, 1], device(x, y, (z + 7) % 8, c))]
        sends.extend(pair)
        return pair

    z0, z1 = spread_z(0, k)

    def spread(n, k, ss, rs, at, p):
        pair = [send(k(), k(), ss.at[n, 0], rs.at[n, 0], at((p + 1) % 4)),
                send(k(), k(), ss.at[n, 1], rs.at[n, 1], at((p + 3) % 4))]
        sends.extend(pair)
        return pair

    def spread_u(n, zz):
        return spread(n, chunk(0, 0, zz), r.s_u, r.r_u, at_u, u)

    def spread_v(n, k):
        return spread(n, k, r.s_v, r.r_v, at_v, v)

    def pass_on(n, k):
        sends.append(send(k(), k(), r.s_d.at[n], r.r_d.at[n], sib))

    order = [(0, zl), (0, oz), (3, zl), (1, zl), (3, oz), (1, oz), (2, zl), (2, oz)]
    ring_u, ring_v = {}, {}
    ring_u[0] = spread_u(0, zl)
    ring_v[0] = spread_v(0, chunk(0, 0, zl))
    work()
    z0.wait_recv()
    z1.wait_recv()
    ring_u[1] = spread_u(1, oz)
    ring_v[1] = spread_v(1, chunk(0, 0, oz))
    pass_on(1, chunk(0, 0, oz))
    half_u = {}
    for n, zz in ((0, zl), (1, oz)):
        work()
        ring_u[n][0].wait_recv()
        k = chunk(0, 3, zz)
        h0 = send(k(0), k(0), r.s_u.at[n, 2], r.r_u.at[n, 2], at_u((u + 1) % 4))
        ring_v[2 + 2 * n] = spread_v(2 + 2 * n, k)
        pass_on(2 + 2 * n, k)
        ring_u[n][1].wait_recv()
        k = chunk(0, 1, zz)
        h1 = send(k(1), k(1), r.s_u.at[n, 3], r.r_u.at[n, 3], at_u((u + 3) % 4))
        ring_v[3 + 2 * n] = spread_v(3 + 2 * n, k)
        pass_on(3 + 2 * n, k)
        sends += [h0, h1]
        half_u[n] = (h0, h1)
    for n, zz in ((0, zl), (1, oz)):
        work()
        half_u[n][0].wait_recv()
        half_u[n][1].wait_recv()
        k = chunk(0, 2, zz)
        ring_v[6 + n] = spread_v(6 + n, k)
        pass_on(6 + n, k)
    half_v = {}
    for n, (j, zz) in enumerate(order):
        work()
        ring_v[n][0].wait_recv()
        k = chunk(3, j, zz)
        h0 = send(k(0), k(0), r.s_v.at[n, 2], r.r_v.at[n, 2], at_v((v + 1) % 4))
        pass_on(8 + n, k)
        ring_v[n][1].wait_recv()
        k = chunk(1, j, zz)
        h1 = send(k(1), k(1), r.s_v.at[n, 3], r.r_v.at[n, 3], at_v((v + 3) % 4))
        pass_on(16 + n, k)
        sends += [h0, h1]
        half_v[n] = (h0, h1)
    for n, (j, zz) in enumerate(order):
        half_v[n][0].wait_recv()
        half_v[n][1].wait_recv()
        pass_on(24 + n, chunk(2, j, zz))
    while thunks:
        work()
    for n in range(1, 32):
        k = gat.at[pl.ds((1 - c) * 128, 4)]
        pltpu.make_async_remote_copy(
            src_ref=k, dst_ref=k, send_sem=r.s_d.at[n], recv_sem=r.r_d.at[n],
            device_id=sib, device_id_type=MESH,
        ).wait_recv()
    own_copy.wait_recv()
    for copy in sends:
        copy.wait_send()
    sends = []

    def pull(t, carry):
        g, q = t // 12, t % 12
        s = r.idx[t]
        r.bm[g, pl.ds(pl.multiple_of(q * 96, 32), 96), :] = gat[s, 0:96, :]
        r.ta[g, q] = gat[s, 96:112, :]
        return carry

    lax.fori_loop(0, 144, pull, 0)
    for q in range(12):
        m = dot(r.ta[:, q].reshape(192, 128), r.selm[...], ((0,), (0,)))
        r.me[96 * q : 96 * q + 96, :] = m[0:96].astype(BF)
    acc[...] = jnp.zeros_like(acc)
    valid = (lax.broadcasted_iota(jnp.int32, (ROWS, 128), 0) % 32) < 28

    def stat(h, t):
        h = jnp.where(valid, h.astype(F32), 0.0)
        r.lsum[row_of(0, t)] = jnp.sum(h, axis=0, keepdims=True)
        r.lsum[row_of(1, t)] = jnp.sum(h * h, axis=0, keepdims=True)

    def fstep(yy, carry):
        for gg in range(3):
            g = 3 * yy + gg
            here = (lane_iota(1152) // 4) == yy * 4 + gg
            bg = r.bg.at[gg]
            bg[0:1152, 0:128] = r.bm[g]
            bg[0:1152, 128:256] = jnp.where(here, r.me[...].astype(F32), 0.0).astype(BF)
            tails = r.ta[g].reshape(192, 128)
            bg[1152:1280, 0:128] = dot(r.sele[0, gg], tails).astype(BF)
            ee = jnp.where(here[0:128], dot(r.sele[1, gg], tails), 0.0)
            bg[1152:1280, 128:256] = ee.astype(BF)
            a = tap_concat(r.xb, lanes_of(g), False, r.ex[:, lanes_of(yy)])
            p = dot(a, bg[...])
            h = p[:, :128].astype(BF)
            r.hid[:, lanes_of(g)] = h
            stat(h, g)
            acc[0:ROWS, :] += p[:, 128:]
        return carry

    lax.fori_loop(0, 4, fstep, 0)
    h = acc[0:ROWS, :].astype(BF)
    r.hid[:, 1536:1664] = h
    stat(h, 12)

    def all_sum(k, src, dst, fill):
        def share(buf, p, base, partners):
            copies = [
                send(buf.at[p], buf.at[p], r.s_a.at[k, base + i], r.r_a.at[k, base + i], to)
                for i, to in enumerate(partners)
            ]
            sends.extend(copies)
            if fill:
                fill.pop(0)()
            for copy in copies:
                copy.wait_recv()

        def total(buf, n):
            out = buf[0]
            for i in range(1, n):
                out = out + buf[i]
            return out

        half = send(src.at[1 - c], r.buf_c.at[k], r.s_a.at[k, 0], r.r_a.at[k, 0], sib)
        half.wait_recv()
        plane, line = r.buf_p.at[k], r.buf_z.at[k]
        p = y * 4 + x
        plane[p] = src[c] + r.buf_c[k]
        over = [(p + i) % 16 for i in range(1, 16)]
        share(plane, p, 1, [device(q % 4, q // 4, z, c) for q in over])
        mine = line.at[c]
        mine[z] = total(plane, 16)
        along = [device(x, y, (z + i) % 8, c) for i in range(1, 8)]
        along += [device(x, y, (z + i) % 8, 1 - c) for i in range(8)]
        share(mine, z, 16, along)
        for n in range(2):
            dst[n] = total(line.at[n], 8)
        half.wait_send()

    def make_tr():
        tr_in = jnp.concatenate([r.me[128 * tap : 128 * tap + 128] for tap in range(9)], axis=1)
        r.tr[...] = dot(tr_in, r.ry[...]).astype(BF)
        r.wt[128:256, :] = jnp.zeros((128, 1280), BF)

    all_sum(0, r.lsum, r.sums, [make_tr])

    def tile(t, carry):
        lanes = lanes_of(t)
        avg = r.sums[row_of(0, t)] / TOTAL
        inv = lax.rsqrt(r.sums[row_of(1, t)] / TOTAL - avg * avg + EPSILON)
        gain, bias = r.par[row_of(0, t)], r.par[row_of(1, t)]
        s1 = jnp.zeros((8, 128), F32)
        s2 = jnp.zeros((8, 128), F32)
        for k in range(28):
            rows = pl.ds(16 * k, 16)
            xv = r.xb[1, 1 + k // 2, 16 * (k % 2) : 16 * (k % 2) + 16, lanes].astype(F32)
            normed = (r.hid[rows, lanes].astype(F32) - avg) * inv
            aff = gain * normed + bias
            sa = half_tanh(aff)
            act = aff * sa
            summed = xv + act
            ss = half_tanh(summed)
            out = summed * ss
            r.bo[rows, lanes] = out.astype(BF)
            gsv = r.upp[rows, lanes].astype(F32) * (ss + out * (1.0 - ss))
            gav = gsv * (sa + act * (1.0 - sa))
            r.gs[rows, lanes] = gsv
            r.ga[rows, lanes] = gav
            p = gav * normed
            s1 = s1 + (p[0:8] + p[8:16])
            s2 = s2 + (gav[0:8] + gav[8:16])
        r.lsum[row_of(0, t)] = jnp.sum(s1, axis=0, keepdims=True)
        r.lsum[row_of(1, t)] = jnp.sum(s2, axis=0, keepdims=True)
        return carry

    lax.fori_loop(0, 13, tile, 0)

    def keep_sums(lanes, whole):
        q = whole[ROWS:]
        r.og[0:1, lanes] = q[0:1] + q[1:2] + q[2:3]
        r.og[1:2, lanes] = q[3:4] + q[4:5] + q[5:6]

    def unpermute(lo, hi, src):
        def step(g, carry):
            pair = jnp.concatenate([src(g), src(GROUPS)], axis=1)
            rows = jnp.concatenate([r.pn[:, lanes_of(g)], r.pn[:, 1536:1664]], axis=1)
            p = dot(jnp.concatenate([pair, rows], axis=0), r.pg[g], ((1,), (1,)))
            whole = acc[...] + p[:, :128]
            acc[...] = p[:, 128:]
            r.xn[:, :, lanes_of(g)] = whole[0:ROWS].astype(BF).reshape(14, 32, 128)
            keep_sums(lanes_of(g), whole)
            return carry

        if lo == 0:
            acc[...] = jnp.zeros_like(acc)
        lax.fori_loop(lo, hi, step, 0)

    def write_out(raw, hbm, n):
        r.xn[:, :, 1536:1664] = acc[0:ROWS, :].astype(BF).reshape(14, 32, 128)
        keep_sums(lanes_of(12), acc[...])
        for yy in range(14):
            raw[yy] = r.xn[yy, 0:28, 0:1584].reshape(14, 2, 1584)
        copy = pltpu.make_async_copy(raw, hbm, r.s_out.at[n])
        copy.start()
        return copy

    outs = []
    from_bo = lambda g: r.bo[:, lanes_of(g)]
    all_sum(1, r.lsum, r.gsum, [
        lambda: unpermute(0, 8, from_bo),
        lambda: (unpermute(8, 12, from_bo), outs.append(write_out(r.raw, r.out_hbm, 0))),
    ])

    def gtile(t, carry):
        lanes = lanes_of(t)
        avg = r.sums[row_of(0, t)] / TOTAL
        inv = lax.rsqrt(r.sums[row_of(1, t)] / TOTAL - avg * avg + EPSILON)
        scale = r.par[row_of(0, t)] * inv
        c1 = r.gsum[row_of(1, t)] / TOTAL
        c2 = r.gsum[row_of(0, t)] / TOTAL
        normed = (r.hid[:, lanes].astype(F32) - avg) * inv
        gh = scale * (r.ga[:, lanes] - c1 - normed * c2)
        store_shifts(r.ghb, jnp.where(valid, gh, 0.0), lanes)
        return carry

    lax.fori_loop(0, 13, gtile, 0)
    r.eg[...] = dot(tap_concat(r.ghb, lanes_of(12), True), r.ry[...]).astype(BF)
    g12 = r.ghb[1, 1:15, :, 1536:1664].reshape(ROWS, 128)
    r.g12t[...] = g12.astype(F32).T.astype(BF)

    st, r0 = r.st, r.r0

    turns = (2, 1, 3, 0)
    low, high = pl.ds(0, 256), pl.ds(256, 256)

    def place_of(ay, ax, half):
        yy, xx = (y + ay) % 4, (x + ax) % 4
        return yy * (1 - half) + xx * half, xx * (1 - half) + yy * half

    def core_copy(ay, ax):
        pv, pu = place_of(ay, ax, 1 - c)
        return pltpu.make_async_remote_copy(
            src_ref=st.at[1 - c, pv, pu], dst_ref=r0.at[pv, pu],
            send_sem=r.s_c.at[4 * ay + ax], recv_sem=r.r_c.at[4 * ay + ax],
            device_id=sib, device_id_type=MESH,
        )

    def ring(m, ru):
        rv, rows, dst, way = (
            (2, low, r.ra.at[ru], 1),
            (2, high, r.rb.at[ru], 3),
            (1, high, r.rp.at[ru, high], 1),
            (1, low, r.rp.at[ru, low], 1),
            (3, low, r.rm.at[ru, low], 3),
            (3, high, r.rm.at[ru, high], 3),
        )[m]
        return pltpu.make_async_remote_copy(
            src_ref=r0.at[(v + rv) % 4, (u + ru) % 4, rows], dst_ref=dst,
            send_sem=r.s_1.at[m, ru], recv_sem=r.r_1.at[m, ru],
            device_id=at_v((v + way) % 4), device_id_type=MESH,
        )

    def launch(rv, ru):
        for m in {2: (0, 1), 1: (2,), 3: (4,), 0: ()}[rv]:
            ring(m, ru).start()

    def add_core(ay):
        for ax in turns:
            core_copy(ay, ax).wait_recv()
            pv, pu = place_of(ay, ax, c)

            def add(n, carry):
                row = pl.ds(pl.multiple_of(n * 128, 128), 128)
                total = st[c, pv, pu, row, :].astype(F32) + r0[pv, pu, row, :].astype(F32)
                r0[pv, pu, row, :] = total.astype(BF)
                return carry

            lax.fori_loop(0, 4, add, 0)
            if ax == ay:
                launch(ay, ax)
            else:
                @pl.when(c == 0)
                def _():
                    launch(ay, ax)

                @pl.when(c == 1)
                def _():
                    launch(ax, ay)

    def add_half(ru, m, buf, rv, start):
        ring(m, ru).wait_recv()
        pv, pu = (v + rv) % 4, (u + ru) % 4
        for n in range(2):
            row, own = pl.ds(128 * n, 128), pl.ds(start + 128 * n, 128)
            total = r0[pv, pu, own, :].astype(F32) + buf[ru, row, :].astype(F32)
            r0[pv, pu, own, :] = total.astype(BF)

    def relay(ru):
        add_half(ru, 0, r.ra, 1, 0)
        ring(3, ru).start()
        add_half(ru, 1, r.rb, 3, 256)
        ring(5, ru).start()

    def wstep(k):
        yy = (y + turns[k]) % 4
        acc[0:144, :] = jnp.zeros((144, 128), F32)
        r.mec[...] = jnp.zeros_like(r.mec)
        lhs12 = r.g12t[rows_at(16 * yy, 16), :]
        for gg in range(3):
            g = 3 * yy + gg
            main = r.ghb[1, 1:15, :, lanes_of(g)].reshape(ROWS, 128)
            lhs = jnp.concatenate([main.astype(F32).T.astype(BF), lhs12], axis=0)
            a = tap_concat(r.xb, lanes_of(g), False, r.ex[:, lanes_of(yy)])
            p = dot(lhs, a)
            for tap in range(9):
                px, pos = piece_of(gg * 9 + tap)
                blk = p[0:128, tap * 128 : tap * 128 + 128].astype(BF)
                st[0, yy, px, pos * 64 : pos * 64 + 64, :] = blk[0:64]
                st[1, px, yy, pos * 64 : pos * 64 + 64, :] = blk[64:128]
            rowsel = (lax.broadcasted_iota(jnp.int32, (16, 1152), 0) // 4) == gg
            r.mec[...] += jnp.where(rowsel, p[128:144, 0:1152], 0.0)
            lane = lane_iota(144)
            lanesel = (lane >= 36 * gg) & (lane < 36 * gg + 36)
            row = lax.broadcasted_iota(jnp.int32, (144, 128), 0)
            rowsel = (row < 128) | (row // 4 == 32 + gg)
            acc[0:144, :] += jnp.where(lanesel & rowsel, p[:, 1152:1280], 0.0)
        zeros = jnp.zeros((128, 128), BF)
        for px in range(3):
            for j in range(3):
                tap = 3 * px + j
                st[0, yy, px, 448 + 16 * j : 464 + 16 * j, :] = r.mec[:, 128 * tap : 128 * tap + 128].astype(BF)
            st[1, px, yy, 448:496, :] = acc[48 * px : 48 * px + 48, :].astype(BF)
            st[0, yy, px, 496:512, :] = zeros[0:16]
            st[1, px, yy, 496:512, :] = zeros[0:16]
        st[0, yy, 3, 384:512, :] = zeros
        st[1, 3, yy, 384:512, :] = zeros
        for ax in turns:
            core_copy(turns[k], ax).start()
        if k > 0:
            add_core(turns[k - 1])

    for k in range(4):
        wstep(k)
    add_core(turns[3])

    def back_part(yy, lo, hi):
        block = pl.ds(128 + 16 * yy, 16)
        wt = r.wt

        def bstep(gg, carry):
            g = 3 * yy + gg
            for tap in range(9):
                wt[0:128, 128 * tap : 128 * tap + 128] = r.bm[g, 128 * tap : 128 * tap + 128, :]
            lane = lane_iota(128)
            lanesel = (lane >= 36 * gg) & (lane < 36 * gg + 36)
            wt[0:128, 1152:1280] = jnp.where(lanesel, r.tr[:, lanes_of(yy)].astype(F32), 0.0).astype(BF)
            tails = r.ta[g].reshape(192, 128)
            bl = dot(r.selb[0, gg], tails).astype(BF)
            be = dot(r.selb[1, gg], tails)
            low = jnp.zeros((16, 128), F32)
            lane = lane_iota(16)
            for tap in range(9):
                wt[block, 128 * tap : 128 * tap + 128] = bl[16 * tap : 16 * tap + 16]
                low = jnp.where((lane // 4) == 9 * gg + tap, be[16 * tap : 16 * tap + 16], low)
            wt[block, 1152:1280] = low.astype(BF)
            a = tap_concat(r.ghb, lanes_of(g), True, r.eg[:, lanes_of(yy)])
            p = dot(a, wt[...], ((1,), (1,)))
            r.gs[:, lanes_of(g)] += p[:, :128]
            r.gs[:, 1536:1664] += p[:, 128:]
            return carry

        lax.fori_loop(lo, hi, bstep, 0)
        if hi == 3:
            wt[block, :] = jnp.zeros((16, 1280), BF)

    u_copies = []

    def sum_v(ru):
        for m in range(2, 6):
            ring(m, ru).wait_recv()
        pu = (u + ru) % 4
        for n in range(4):
            row = pl.ds(128 * n, 128)
            total = r0[v, pu, row, :].astype(F32) + r.rp[ru, row, :].astype(F32)
            r.cur2[ru, row, :] = (total + r.rm[ru, row, :].astype(F32)).astype(BF)
        if ru:
            u_copies.append(
                send(r.cur2.at[ru], r.r2.at[ru - 1], r.s_2.at[ru - 1], r.r_2.at[ru - 1], at_u(pu))
            )

    parts = [(yy, lo, hi) for yy in range(4) for lo, hi in ((0, 1), (1, 2), (2, 3))]

    def back_next(n=1):
        for _ in range(n):
            if parts:
                back_part(*parts.pop(0))

    for ru in turns:
        back_next()
        relay(ru)
    back_next()
    for ru in turns:
        back_next()
        sum_v(ru)
    back_next()
    from_gs = lambda g: r.gs[:, lanes_of(g)].astype(BF)
    for t in range(13):
        for n in range(2):
            for k, part in enumerate(split3(r.gsum[n, t : t + 1, :])):
                r.pf[3 * n + k : 3 * n + k + 1, lanes_of(t)] = part
    r.pn[...] = r.pf[...].astype(BF)
    for copy in u_copies:
        copy.wait_recv()
    sends += u_copies
    for n in range(8):
        row = pl.ds(64 * n, 64)
        total = r.cur2[0, row, :].astype(F32)
        for rel in range(3):
            total = total + r.r2[rel, row, :].astype(F32)
        r.cur3[n] = total.astype(BF)
    copies = []
    for k in range(1, 8):
        q = (z + k) % 8
        copies.append(send(r.cur3.at[q], r.r3.at[k - 1], r.s_3.at[k - 1], r.r_3.at[k - 1], device(x, y, q, c)))
    sends += copies
    back_next(12)
    for copy in copies:
        copy.wait_recv()
    total = r.cur3[z].astype(F32)
    for k in range(7):
        total = total + r.r3[k].astype(F32)
    hh = r.hh
    hh[c, x, z] = total.astype(BF)
    here = hh.at[c, x, z]
    copies = []
    for k in range(1, 8):
        q = (z + k) % 8
        copies.append(send(here, here, r.s_4.at[k - 1], r.r_4.at[k - 1], device(x, y, q, c)))
    sends += copies
    unpermute(0, 8, from_gs)
    for copy in copies:
        copy.wait_recv()
    near = [(1, 6 - 3 * (x % 2) - 3 * (x // 3)), (3, 3 - 3 * (x % 2))]
    copies = [send(hh.at[c, x], hh.at[c, x], r.s_5.at[0], r.r_5.at[0], sib)]
    n = 1
    for cc in (c, 1 - c):
        for rel, pos in near:
            to = device((x + rel) % 4, y, z, cc)
            copies.append(send(hh.at[c, x, pos], hh.at[c, x, pos], r.s_5.at[n], r.r_5.at[n], to))
            copies.append(send(hh.at[c, x, 7], hh.at[c, x, 7], r.s_5.at[n + 1], r.r_5.at[n + 1], to))
            n += 2
        to = device((x + 2) % 4, y, z, cc)
        copies.append(send(hh.at[c, x, 7], hh.at[c, x, 7], r.s_5.at[n], r.r_5.at[n], to))
        n += 1
    unpermute(8, 12, from_gs)
    outs.append(write_out(r.raw2, r.ig_hbm, 1))
    r.gg_out[...] = r.og[0:1, 0:1584].reshape(1584)
    r.bg_out[...] = r.og[1:2, 0:1584].reshape(1584)
    for copy in copies:
        copy.wait_recv()
    sends += copies
    sp = (z % 2) * 8 + x * 2 + c
    b0 = (sp * 29403) // 17424 - sp // 15
    em = jnp.concatenate([hh[1, j, 7, 0:48, :] for j in range(3)], axis=0)
    for k in range(3):
        b = b0 + k
        px, pos = piece_of(b)
        tap = b % 9
        gg = b // 9
        main = jnp.concatenate([hh[0, px, pos], hh[1, px, pos]], axis=0)
        mrow = hh[0, tap // 3, 7, rows_at(16 * (tap % 3), 16), :]
        left = jnp.concatenate([main, mrow], axis=0)
        line = lax.broadcasted_iota(jnp.int32, (128, 136), 0) - (36 * gg + 4 * tap)
        unit = lax.broadcasted_iota(jnp.int32, (128, 136), 1)
        qe = jnp.where((line >= 0) & (line < 4) & (unit == 33 * line + 32), 1.0, 0.0).astype(BF)
        t1 = (dot(left, r.qm[...]) + dot(em, qe)).astype(BF)
        t2 = dot(t1, r.qo[gg], ((0,), (0,)))
        r.kgs[132 * k : 132 * k + 132, 0:GW] = t2[0:132]

    lane = lane_iota(32)
    skip = 4 * lax.broadcasted_iota(jnp.int32, (32, 128), 0)
    for k in range(13):
        rows = r.kgs[32 * k : 32 * k + 32, :]
        body = pltpu.roll(rows[:, 0:128], 0, 1, stride=4, stride_axis=0)
        rest = pltpu.roll(rows[:, 128:256], 0, 1, stride=4, stride_axis=0)
        head = jnp.where(lane >= skip, body, 0.0)
        tail = jnp.where(lane < skip, body, jnp.where(lane < skip + 4, rest, 0.0))
        r.kg[33 * k : 33 * k + 32, :] = head
        r.kg[33 * k + 32 : 33 * k + 33, :] = jnp.zeros((1, 128), F32)
        r.kg[33 * k + 1 : 33 * k + 33, :] += tail

    for copy in sends:
        copy.wait_send()
    for ay in range(4):
        for ax in range(4):
            core_copy(ay, ax).wait_send()
    for m in range(6):
        for ru in range(4):
            ring(m, ru).wait_send()
    for copy in outs:
        copy.wait()


def mega(idx, tiles, gain, bias, xt, upt):
    k = constants()
    operands = [idx, tiles, *prep_constants(), gain, bias]
    operands += [k["pg"], k["ry"], k["selm"], k["sele"], k["selb"], *fin_constants(), xt, upt]
    anywhere = pl.BlockSpec(memory_space=pl.ANY)
    return pl.pallas_call(
        mega_body,
        in_specs=[pl.BlockSpec(memory_space=pltpu.SMEM)] + [vspec()] * 9 + [anywhere] * 9,
        out_specs=[anywhere, anywhere, vspec(), vspec(), vspec()],
        out_shape=[
            struct((14, 14, 2, 1584), BF),
            struct((14, 14, 2, 1584), BF),
            struct((432, 128), F32),
            struct((1584,), F32),
            struct((1584,), F32),
        ],
        scratch_shapes=list(scratch_list().values()),
        compiler_params=pltpu.CompilerParams(
            collective_id=1, has_side_effects=True, vmem_limit_bytes=VLIM
        ),
        name="block",
    )(*operands)


def finish_body(out_a, ig_a, out_b, ig_b, one, two, sem):
    pairs = [(out_a, one, out_b), (ig_a, two, ig_b)]
    loads = [pltpu.make_async_copy(src, mid, sem.at[n]) for n, (src, mid, _) in enumerate(pairs)]
    saves = [pltpu.make_async_copy(mid, dst, sem.at[2 + n]) for n, (_, mid, dst) in enumerate(pairs)]
    for load in loads:
        load.start()
    for load, save in zip(loads, saves):
        load.wait()
        save.start()
    for save in saves:
        save.wait()


def finish(out, ig):
    anywhere = pl.BlockSpec(memory_space=pl.ANY)
    return pl.pallas_call(
        finish_body,
        in_specs=[anywhere] * 2,
        out_specs=[anywhere] * 2,
        out_shape=[struct((14, 14, 2, 1584), BF)] * 2,
        scratch_shapes=[VM((14, 14, 2, 1584), BF)] * 2 + [DMA((4,))],
        name="finish",
    )(out, ig)


def tile_rows(tile_counts, owner_order):
    ranks = jnp.arange(64, dtype=jnp.int32)
    before = (ranks[None, :] < ranks[:, None]).astype(jnp.int32)
    run_start = jnp.sum(before * tile_counts[None, :], axis=1)
    j = jnp.arange(144, dtype=jnp.int32)[:, None] - run_start[None, :]
    s = owner_order[None, :]
    y, zl, x, core = s // 16, (s // 8) % 2, (s // 2) % 4, s % 2
    vu = jnp.where(j < 2, y * 4 + x, x * 4 + y)
    spot = (j // 2) * 128 + vu * 8 + zl * 4 + core * 2 + j % 2
    held = (j >= 0) & (j < tile_counts[None, :])
    return jnp.sum(jnp.where(held, spot, 0), axis=1)


def local(block_input, upstream, kernel_tiles, tile_counts, owner_order, gain, bias):
    idx = tile_rows(tile_counts, owner_order)
    turn = lambda a: jnp.transpose(a, (1, 2, 0, 3))
    back = lambda a: jnp.transpose(a, (2, 0, 1, 3))
    out, ig, kg, gg, bg = mega(
        idx, kernel_tiles.reshape(4, 99, GW), gain, bias,
        turn(block_input), turn(upstream),
    )
    out, ig = finish(out, ig)
    sp = lax.axis_index("shard") % 16
    b0 = (sp * 29403) // 17424 - sp // 15
    kernel_grad = lax.dynamic_slice(kg.reshape(-1), (sp * 29403 - b0 * 17424,), (29403,))
    return (back(out), back(ig), kernel_grad, gg, bg)


def solution(mesh):
    return jax.shard_map(
        local,
        mesh=mesh,
        in_specs=(
            P(("dp", "shard"), None, None, None),
            P(("dp", "shard"), None, None, None),
            P("shard", None),
            P(),
            P(),
            P(),
            P(),
        ),
        out_specs=(
            P(("dp", "shard"), None, None, None),
            P(("dp", "shard"), None, None, None),
            P("shard"),
            P(),
            P(),
        ),
        check_vma=False,
    )
```

```python
import numpy as np
import jax
import jax.numpy as jnp
from jax import lax
from jax.experimental import pallas as pl
from jax.experimental.pallas import tpu as pltpu
from jax.sharding import PartitionSpec as P

GROUPS = 12
GW = 132
ROWS = 448
LANES = 1664
BF = jnp.bfloat16
F32 = jnp.float32
EPSILON = 1e-05
TOTAL = 100352
VLIM = 60 * 1024 * 1024


def extra_lane(g, a):
    return 16 * (g // 3) + 4 * (g % 3) + a


def constants():
    pg = np.zeros((GROUPS, 256, 256), np.float32)
    for g in range(GROUPS):
        for j in range(GW):
            a, l = j // 33, j % 33
            pg[g, 4 * g + j, 32 * a + l if l < 32 else 128 + extra_lane(g, a)] = 1
    ry = np.zeros((9, 128, 4, 128), np.float32)
    for g in range(GROUPS):
        for tap in range(9):
            for a in range(4):
                ry[tap, extra_lane(g, a), g // 3, 36 * (g % 3) + 4 * tap + a] = 1
    selm = np.zeros((GROUPS, 16, 128), np.float32)
    for g in range(GROUPS):
        for a in range(4):
            selm[g, 3 + a, extra_lane(g, a)] = 1
    sele = np.zeros((2, 3, 128, 12, 16), np.float32)
    selb = np.zeros((2, 3, 9, 16, 12, 16), np.float32)
    for gg in range(3):
        for u in range(36):
            q, j = u // 3, u % 3
            tap, a = u // 4, u % 4
            for kind, row in ((0, j), (1, 7 + j)):
                sele[kind, gg, 36 * gg + u, q, row] = 1
                selb[kind, gg, tap, 4 * gg + a, q, row] = 1
    bf = lambda v, *s: jnp.asarray(v.reshape(s), BF)
    return dict(
        pg=bf(pg, GROUPS, 256, 256),
        ry=bf(ry, 1152, 512),
        selm=bf(selm, 192, 128),
        sele=bf(sele, 2, 3, 128, 192),
        selb=bf(selb, 2, 3, 144, 192),
    )


def prep_constants():
    cs = np.zeros((GW, 128), np.float32)
    cse = np.zeros((GW, 112), np.float32)
    csee = np.zeros((GW, 128), np.float32)
    rs = np.zeros((112, 99), np.float32)
    rsm = np.zeros((99, 128), np.float32)
    rse = np.zeros((112, 99), np.float32)
    for a in range(4):
        for l in range(32):
            cs[33 * a + l, 32 * a + l] = 1
        cse[33 * a + 32, 99 + a] = 1
    for lane in range(128):
        csee[33 * (lane % 4) + 32, lane] = 1
    for j in range(3):
        for l in range(32):
            rs[32 * j + l, 33 * j + l] = 1
            rsm[33 * j + l, 32 * j + l] = 1
        rs[96 + j, 33 * j + 32] = 1
        rse[103 + j, 33 * j + 32] = 1
    return [jnp.asarray(v, BF) for v in (cs, cse, csee, rs, rsm, rse)]


def dot(a, b, dims=((1,), (0,))):
    return lax.dot_general(a, b, (dims, ((), ())), preferred_element_type=F32)


MESH = pl.DeviceIdType.MESH
DMA = pltpu.SemaphoreType.DMA
VM = pltpu.VMEM


def vspec():
    return pl.BlockSpec(memory_space=VM)


def struct(shape, dtype):
    return jax.ShapeDtypeStruct(shape, dtype)


def lanes_of(g, width=1):
    if isinstance(g, int):
        return pl.ds(g * 128, 128 * width)
    return pl.ds(pl.multiple_of(g * 128, 128), 128 * width)


def rows_at(start, size):
    if isinstance(start, int):
        return pl.ds(start, size)
    return pl.ds(pl.multiple_of(start, 16), size)


def lane_iota(rows):
    return lax.broadcasted_iota(jnp.int32, (rows, 128), 1)


def half_tanh(v):
    return 0.5 * jnp.tanh(0.5 * v) + 0.5


def place():
    dp = lax.axis_index("dp")
    s = lax.axis_index("shard")
    return (s // 2) % 4, s // 16, dp * 2 + (s // 8) % 2, s % 2


def device(x, y, z, c):
    return (z // 2, y * 16 + (z % 2) * 8 + x * 2 + c)


def send(src, dst, send_sem, recv_sem, to):
    copy = pltpu.make_async_remote_copy(
        src_ref=src, dst_ref=dst, send_sem=send_sem, recv_sem=recv_sem,
        device_id=to, device_id_type=MESH,
    )
    copy.start()
    return copy


def load_native(raw, xn):
    xn[...] = jnp.zeros_like(xn)
    for y in range(14):
        xn[y, 0:28, 0:1584] = raw[y].reshape(28, 1584)


def store_shifts(dst, main, lanes):
    for b in range(3):
        moved = main if b == 1 else pltpu.roll(main, (2 - 2 * b) % ROWS, 0)
        dst[b, 1:15, :, lanes] = moved.astype(BF).reshape(14, 32, 128)


def zero_borders(dst):
    zeros = jnp.zeros((3, 32, LANES), BF)
    dst[:, 0] = zeros
    dst[:, 15] = zeros


def tap_slice(src, tap, lanes, mirrored):
    a, b = tap // 3, tap % 3
    if mirrored:
        a, b = 2 - a, 2 - b
    return src[b, a : a + 14, :, lanes].reshape(ROWS, 128)


def tap_concat(src, lanes, mirrored, extra=None):
    pieces = [tap_slice(src, tap, lanes, mirrored) for tap in range(9)]
    if extra is not None:
        pieces.append(extra)
    return jnp.concatenate(pieces, axis=1)


def piece_of(b):
    s = {t: (b + 27 - t) // 27 for t in (3, 7, 10, 13, 17, 20, 24)}
    x = s[3] + s[7] + s[10] - 3 * s[13] + s[17] + s[20] + s[24]
    pos = b - 3 * s[3] - 4 * s[7] - 3 * s[10] - 3 * s[17] - 4 * s[20] - 4 * s[24]
    return x, pos


def fin_constants():
    q_m = np.zeros((128, 136), np.float32)
    q_o = np.zeros((3, 144, GW), np.float32)
    for a in range(4):
        for l in range(32):
            q_m[32 * a + l, 33 * a + l] = 1
            q_o[:, 32 * a + l, 33 * a + l] = 1
        for gg in range(3):
            q_o[gg, 128 + 4 * gg + a, 33 * a + 32] = 1
    return jnp.asarray(q_m, BF), jnp.asarray(q_o, BF)


IN_NAMES = (
    "idx", "tile", "cs", "cse", "csee", "rs", "rsm", "rse", "gain", "bias",
    "pg_h", "ry_h", "selm_h", "sele_h", "selb_h", "qm_h", "qo_h", "x_hbm", "up_hbm",
)
LOADED = ("pg", "ry", "selm", "sele", "selb", "qm", "qo")
OUT_NAMES = ("out_hbm", "ig_hbm", "kg", "gg_out", "bg_out")


def scratch_list():
    sets = dict(
        pay=VM((4, 112, 128), BF),
        gat=VM((256, 112, 128), BF),
        xb=VM((3, 16, 32, LANES), BF),
        ghb=VM((3, 16, 32, LANES), BF),
        ex=VM((ROWS, 512), BF),
        eg=VM((ROWS, 512), BF),
        bm=VM((GROUPS, 1152, 128), BF),
        ta=VM((GROUPS, 12, 16, 128), BF),
        me=VM((1152, 128), BF),
        hid=VM((ROWS, LANES), BF),
        gs=VM((ROWS, LANES), F32),
        ga=VM((ROWS, LANES), F32),
        upp=VM((ROWS, LANES), BF),
        bo=VM((ROWS, LANES), BF),
        raw=VM((14, 14, 2, 1584), BF),
        raw2=VM((14, 14, 2, 1584), BF),
        xn=VM((14, 32, LANES), BF),
        acc=VM((ROWS + 16, 128), F32),
        mec=VM((16, 1152), F32),
        bg=VM((3, 1280, 256), BF),
        kgs=VM((416, 256), F32),
        wt=VM((256, 1280), BF),
        tr=VM((128, 512), BF),
        g12t=VM((128, ROWS), BF),
        st=VM((2, 4, 4, 512, 128), BF),
        r0=VM((4, 4, 512, 128), BF),
        ra=VM((4, 256, 128), BF),
        rb=VM((4, 256, 128), BF),
        rp=VM((4, 512, 128), BF),
        rm=VM((4, 512, 128), BF),
        cur2=VM((4, 512, 128), BF),
        r2=VM((3, 512, 128), BF),
        cur3=VM((8, 64, 128), BF),
        r3=VM((7, 64, 128), BF),
        hh=VM((2, 4, 8, 64, 128), BF),
        sums=VM((2, 16, 128), F32),
        gsum=VM((2, 16, 128), F32),
        lsum=VM((2, 16, 128), F32),
        par=VM((2, 16, 128), F32),
        pf=VM((16, LANES), F32),
        pn=VM((16, LANES), BF),
        og=VM((2, LANES), F32),
        pg=VM((GROUPS, 256, 256), BF),
        ry=VM((1152, 512), BF),
        selm=VM((192, 128), BF),
        sele=VM((2, 3, 128, 192), BF),
        selb=VM((2, 3, 144, 192), BF),
        qm=VM((128, 136), BF),
        qo=VM((3, 144, GW), BF),
        s_in=DMA((2,)),
        s_k=DMA((7,)),
        s_out=DMA((2,)),
        s_sib=DMA((1,)), r_sib=DMA((1,)),
        s_z=DMA((11, 2)), r_z=DMA((11, 2)),
        s_u=DMA((2, 4)), r_u=DMA((2, 4)),
        s_v=DMA((8, 4)), r_v=DMA((8, 4)),
        s_d=DMA((33,)), r_d=DMA((33,)),
        s_c=DMA((16,)), r_c=DMA((16,)),
        s_1=DMA((6, 4)), r_1=DMA((6, 4)),
        s_2=DMA((3,)), r_2=DMA((3,)),
        s_3=DMA((7,)), r_3=DMA((7,)),
        s_4=DMA((7,)), r_4=DMA((7,)),
        s_5=DMA((11,)), r_5=DMA((11,)),
        s_a=DMA((2, 33)), r_a=DMA((2, 33)),
        buf_c=VM((2, 16, 128), F32),
        buf_p=VM((2, 16, 16, 128), F32),
        buf_z=VM((2, 2, 8, 16, 128), F32),
    )
    return sets


class Refs:
    pass


def mega_body(*refs):
    r = Refs()
    names = list(IN_NAMES) + list(OUT_NAMES) + list(scratch_list())
    for name, ref in zip(names, refs, strict=True):
        setattr(r, name, ref)
    x, y, z, c = place()
    u = x * (1 - c) + y * c
    v = y * (1 - c) + x * c
    zl = z % 2
    oz = 1 - zl
    sib = device(x, y, z, 1 - c)

    def at_u(k):
        return device(k * (1 - c) + x * c, y * (1 - c) + k * c, z, c)

    def at_v(k):
        return device(x * (1 - c) + k * c, k * (1 - c) + y * c, z, c)

    others = [sib]
    others += [device((x + k % 4) % 4, (y + k // 4) % 4, z, c) for k in range(1, 16)]
    others += [device((x + k) % 4, y, z, 1 - c) for k in range(1, 4)]
    others += [device(x, y, (z + k) % 8, cc) for k in range(1, 8) for cc in (c, 1 - c)]
    barrier = pltpu.get_barrier_semaphore()
    for d in others:
        pl.semaphore_signal(barrier, inc=1, device_id=d, device_id_type=MESH)
    in_x = pltpu.make_async_copy(r.x_hbm, r.raw, r.s_in.at[0])
    in_x.start()
    in_up = pltpu.make_async_copy(r.up_hbm, r.raw2, r.s_in.at[1])
    in_up.start()
    loads = [
        pltpu.make_async_copy(getattr(r, name + "_h"), getattr(r, name), r.s_k.at[n])
        for n, name in enumerate(LOADED)
    ]
    for load in loads:
        load.start()

    def split3(val):
        hi = val.astype(BF).astype(F32)
        mid = (val - hi).astype(BF).astype(F32)
        return hi, mid, val - hi - mid

    r.pf[...] = jnp.zeros_like(r.pf)
    for n, ref in ((0, r.gain), (3, r.bias)):
        for k, part in enumerate(split3(ref[...].reshape(1, 1584))):
            r.pf[n + k : n + k + 1, 0:1584] = part
    r.pn[...] = r.pf[...].astype(BF)
    r.lsum[...] = jnp.zeros_like(r.lsum)
    for s in range(4):
        t = r.tile[s]
        w = dot(t, r.cs[...]).astype(BF)
        we = dot(t, r.cse[...]).astype(BF)
        wee = dot(t, r.csee[...]).astype(BF)
        full = dot(r.rs[...], w) + dot(we, r.rsm[...], ((0,), (0,))) + dot(r.rse[...], wee)
        r.pay[s] = full.astype(BF)
    pl.semaphore_wait(barrier, len(others))
    sends = []

    acc = r.acc

    def first_x():
        for load in loads:
            load.wait()
        in_x.wait()
        load_native(r.raw, r.xn)
        zero_borders(r.xb)
        acc[...] = jnp.zeros_like(acc)

    def permute(lo, hi, sink):
        def step(g, carry):
            rows = jnp.concatenate(
                [r.xn[:, :, lanes_of(g, 2)].reshape(ROWS, 256), r.pn[:, lanes_of(g, 2)]], axis=0
            )
            p = dot(rows, r.pg[g])
            sink(g, p[:, :128])
            acc[...] += p[:, 128:]
            return carry

        lax.fori_loop(lo, hi, step, 0)

    def row_of(k, t):
        return (k, pl.ds(t, 1), slice(None))

    def keep_x(g, val):
        store_shifts(r.xb, val[0:ROWS], lanes_of(g))
        p = val[ROWS:]
        r.par[row_of(0, g)] = p[0:1] + p[1:2] + p[2:3]
        r.par[row_of(1, g)] = p[3:4] + p[4:5] + p[5:6]

    def keep_up(g, val):
        r.upp[:, lanes_of(g)] = val[0:ROWS].astype(BF)

    def last_x():
        keep_x(GROUPS, acc[...])
        r.ex[...] = dot(tap_concat(r.xb, lanes_of(12), False), r.ry[...]).astype(BF)

    def first_up():
        in_up.wait()
        load_native(r.raw2, r.xn)
        zero_borders(r.ghb)
        acc[...] = jnp.zeros_like(acc)

    thunks = [first_x]
    thunks += [lambda k=k: permute(3 * k, 3 * k + 3, keep_x) for k in range(4)]
    thunks += [last_x, first_up]
    thunks += [lambda k=k: permute(3 * k, 3 * k + 3, keep_up) for k in range(4)]
    thunks += [lambda: keep_up(GROUPS, acc[...])]

    def work():
        if thunks:
            thunks.pop(0)()

    gat = r.gat

    def chunk(i, j, zz):
        lin = c * 128 + ((v + i) % 4) * 32 + ((u + j) % 4) * 8 + zz * 4
        return lambda h=None: gat.at[pl.ds(lin, 4)] if h is None else gat.at[pl.ds(lin + 2 * h, 2)]

    mine = c * 128 + v * 32 + u * 8 + zl * 4 + c * 2
    other = (1 - c) * 128 + u * 32 + v * 8 + zl * 4 + c * 2
    gat[pl.ds(mine, 2)] = r.pay[pl.ds(2 * c, 2)]
    gat[pl.ds(other, 2)] = r.pay[pl.ds(2 - 2 * c, 2)]
    mine, other = gat.at[pl.ds(mine, 2)], gat.at[pl.ds(other, 2)]
    sib_copy = send(other, other, r.s_sib.at[0], r.r_sib.at[0], sib)
    own_copy = send(mine, mine, r.s_d.at[32], r.r_d.at[32], sib)
    sends += [sib_copy, own_copy]
    sib_copy.wait_recv()

    k = chunk(0, 0, zl)
    def spread_z(m, k):
        pair = [send(k(0), k(0), r.s_z.at[m, 0], r.r_z.at[m, 0], device(x, y, (z + 1) % 8, c)),
                send(k(1), k(1), r.s_z.at[m, 1], r.r_z.at[m, 1], device(x, y, (z + 7) % 8, c))]
        sends.extend(pair)
        return pair

    z0, z1 = spread_z(0, k)

    def spread(n, k, ss, rs, at, p):
        pair = [send(k(), k(), ss.at[n, 0], rs.at[n, 0], at((p + 1) % 4)),
                send(k(), k(), ss.at[n, 1], rs.at[n, 1], at((p + 3) % 4))]
        sends.extend(pair)
        return pair

    def spread_u(n, zz):
        return spread(n, chunk(0, 0, zz), r.s_u, r.r_u, at_u, u)

    def spread_v(n, k):
        return spread(n, k, r.s_v, r.r_v, at_v, v)

    def pass_on(n, k):
        sends.append(send(k(), k(), r.s_d.at[n], r.r_d.at[n], sib))

    order = [(0, zl), (0, oz), (3, zl), (1, zl), (3, oz), (1, oz), (2, zl), (2, oz)]
    ring_u, ring_v = {}, {}
    ring_u[0] = spread_u(0, zl)
    ring_v[0] = spread_v(0, chunk(0, 0, zl))
    work()
    z0.wait_recv()
    z1.wait_recv()
    ring_u[1] = spread_u(1, oz)
    ring_v[1] = spread_v(1, chunk(0, 0, oz))
    pass_on(1, chunk(0, 0, oz))
    half_u = {}
    for n, zz in ((0, zl), (1, oz)):
        work()
        ring_u[n][0].wait_recv()
        k = chunk(0, 3, zz)
        h0 = send(k(0), k(0), r.s_u.at[n, 2], r.r_u.at[n, 2], at_u((u + 1) % 4))
        ring_v[2 + 2 * n] = spread_v(2 + 2 * n, k)
        pass_on(2 + 2 * n, k)
        ring_u[n][1].wait_recv()
        k = chunk(0, 1, zz)
        h1 = send(k(1), k(1), r.s_u.at[n, 3], r.r_u.at[n, 3], at_u((u + 3) % 4))
        ring_v[3 + 2 * n] = spread_v(3 + 2 * n, k)
        pass_on(3 + 2 * n, k)
        sends += [h0, h1]
        half_u[n] = (h0, h1)
    for n, zz in ((0, zl), (1, oz)):
        work()
        half_u[n][0].wait_recv()
        half_u[n][1].wait_recv()
        k = chunk(0, 2, zz)
        ring_v[6 + n] = spread_v(6 + n, k)
        pass_on(6 + n, k)
    half_v = {}
    for n, (j, zz) in enumerate(order):
        work()
        ring_v[n][0].wait_recv()
        k = chunk(3, j, zz)
        h0 = send(k(0), k(0), r.s_v.at[n, 2], r.r_v.at[n, 2], at_v((v + 1) % 4))
        pass_on(8 + n, k)
        ring_v[n][1].wait_recv()
        k = chunk(1, j, zz)
        h1 = send(k(1), k(1), r.s_v.at[n, 3], r.r_v.at[n, 3], at_v((v + 3) % 4))
        pass_on(16 + n, k)
        sends += [h0, h1]
        half_v[n] = (h0, h1)
    for n, (j, zz) in enumerate(order):
        half_v[n][0].wait_recv()
        half_v[n][1].wait_recv()
        pass_on(24 + n, chunk(2, j, zz))
    while thunks:
        work()
    for n in range(1, 32):
        k = gat.at[pl.ds((1 - c) * 128, 4)]
        pltpu.make_async_remote_copy(
            src_ref=k, dst_ref=k, send_sem=r.s_d.at[n], recv_sem=r.r_d.at[n],
            device_id=sib, device_id_type=MESH,
        ).wait_recv()
    own_copy.wait_recv()
    for copy in sends:
        copy.wait_send()
    sends = []

    def pull(t, carry):
        g, q = t // 12, t % 12
        s = r.idx[t]
        r.bm[g, pl.ds(pl.multiple_of(q * 96, 32), 96), :] = gat[s, 0:96, :]
        r.ta[g, q] = gat[s, 96:112, :]
        return carry

    lax.fori_loop(0, 144, pull, 0)
    for q in range(12):
        m = dot(r.ta[:, q].reshape(192, 128), r.selm[...], ((0,), (0,)))
        r.me[96 * q : 96 * q + 96, :] = m[0:96].astype(BF)
    acc[...] = jnp.zeros_like(acc)
    valid = (lax.broadcasted_iota(jnp.int32, (ROWS, 128), 0) % 32) < 28

    def stat(h, t):
        h = jnp.where(valid, h.astype(F32), 0.0)
        r.lsum[row_of(0, t)] = jnp.sum(h, axis=0, keepdims=True)
        r.lsum[row_of(1, t)] = jnp.sum(h * h, axis=0, keepdims=True)

    def fstep(yy, carry):
        for gg in range(3):
            g = 3 * yy + gg
            here = (lane_iota(1152) // 4) == yy * 4 + gg
            bg = r.bg.at[gg]
            bg[0:1152, 0:128] = r.bm[g]
            bg[0:1152, 128:256] = jnp.where(here, r.me[...].astype(F32), 0.0).astype(BF)
            tails = r.ta[g].reshape(192, 128)
            bg[1152:1280, 0:128] = dot(r.sele[0, gg], tails).astype(BF)
            ee = jnp.where(here[0:128], dot(r.sele[1, gg], tails), 0.0)
            bg[1152:1280, 128:256] = ee.astype(BF)
            a = tap_concat(r.xb, lanes_of(g), False, r.ex[:, lanes_of(yy)])
            p = dot(a, bg[...])
            h = p[:, :128].astype(BF)
            r.hid[:, lanes_of(g)] = h
            stat(h, g)
            acc[0:ROWS, :] += p[:, 128:]
        return carry

    lax.fori_loop(0, 4, fstep, 0)
    h = acc[0:ROWS, :].astype(BF)
    r.hid[:, 1536:1664] = h
    stat(h, 12)

    def all_sum(k, src, dst, fill):
        def share(buf, p, base, partners):
            copies = [
                send(buf.at[p], buf.at[p], r.s_a.at[k, base + i], r.r_a.at[k, base + i], to)
                for i, to in enumerate(partners)
            ]
            sends.extend(copies)
            if fill:
                fill.pop(0)()
            for copy in copies:
                copy.wait_recv()

        def total(buf, n):
            out = buf[0]
            for i in range(1, n):
                out = out + buf[i]
            return out

        half = send(src.at[1 - c], r.buf_c.at[k], r.s_a.at[k, 0], r.r_a.at[k, 0], sib)
        half.wait_recv()
        plane, line = r.buf_p.at[k], r.buf_z.at[k]
        p = y * 4 + x
        plane[p] = src[c] + r.buf_c[k]
        over = [(p + i) % 16 for i in range(1, 16)]
        share(plane, p, 1, [device(q % 4, q // 4, z, c) for q in over])
        mine = line.at[c]
        mine[z] = total(plane, 16)
        along = [device(x, y, (z + i) % 8, c) for i in range(1, 8)]
        along += [device(x, y, (z + i) % 8, 1 - c) for i in range(8)]
        share(mine, z, 16, along)
        for n in range(2):
            dst[n] = total(line.at[n], 8)
        half.wait_send()

    def make_tr():
        tr_in = jnp.concatenate([r.me[128 * tap : 128 * tap + 128] for tap in range(9)], axis=1)
        r.tr[...] = dot(tr_in, r.ry[...]).astype(BF)
        r.wt[128:256, :] = jnp.zeros((128, 1280), BF)

    all_sum(0, r.lsum, r.sums, [make_tr])

    def tile(t, carry):
        lanes = lanes_of(t)
        avg = r.sums[row_of(0, t)] / TOTAL
        inv = lax.rsqrt(r.sums[row_of(1, t)] / TOTAL - avg * avg + EPSILON)
        gain, bias = r.par[row_of(0, t)], r.par[row_of(1, t)]
        s1 = jnp.zeros((8, 128), F32)
        s2 = jnp.zeros((8, 128), F32)
        for k in range(28):
            rows = pl.ds(16 * k, 16)
            xv = r.xb[1, 1 + k // 2, 16 * (k % 2) : 16 * (k % 2) + 16, lanes].astype(F32)
            normed = (r.hid[rows, lanes].astype(F32) - avg) * inv
            aff = gain * normed + bias
            sa = half_tanh(aff)
            act = aff * sa
            summed = xv + act
            ss = half_tanh(summed)
            out = summed * ss
            r.bo[rows, lanes] = out.astype(BF)
            gsv = r.upp[rows, lanes].astype(F32) * (ss + out * (1.0 - ss))
            gav = gsv * (sa + act * (1.0 - sa))
            r.gs[rows, lanes] = gsv
            r.ga[rows, lanes] = gav
            p = gav * normed
            s1 = s1 + (p[0:8] + p[8:16])
            s2 = s2 + (gav[0:8] + gav[8:16])
        r.lsum[row_of(0, t)] = jnp.sum(s1, axis=0, keepdims=True)
        r.lsum[row_of(1, t)] = jnp.sum(s2, axis=0, keepdims=True)
        return carry

    lax.fori_loop(0, 13, tile, 0)

    def keep_sums(lanes, whole):
        q = whole[ROWS:]
        r.og[0:1, lanes] = q[0:1] + q[1:2] + q[2:3]
        r.og[1:2, lanes] = q[3:4] + q[4:5] + q[5:6]

    def unpermute(lo, hi, src):
        def step(g, carry):
            pair = jnp.concatenate([src(g), src(GROUPS)], axis=1)
            rows = jnp.concatenate([r.pn[:, lanes_of(g)], r.pn[:, 1536:1664]], axis=1)
            p = dot(jnp.concatenate([pair, rows], axis=0), r.pg[g], ((1,), (1,)))
            whole = acc[...] + p[:, :128]
            acc[...] = p[:, 128:]
            r.xn[:, :, lanes_of(g)] = whole[0:ROWS].astype(BF).reshape(14, 32, 128)
            keep_sums(lanes_of(g), whole)
            return carry

        if lo == 0:
            acc[...] = jnp.zeros_like(acc)
        lax.fori_loop(lo, hi, step, 0)

    def write_out(raw, hbm, n):
        r.xn[:, :, 1536:1664] = acc[0:ROWS, :].astype(BF).reshape(14, 32, 128)
        keep_sums(lanes_of(12), acc[...])
        for yy in range(14):
            raw[yy] = r.xn[yy, 0:28, 0:1584].reshape(14, 2, 1584)
        copy = pltpu.make_async_copy(raw, hbm, r.s_out.at[n])
        copy.start()
        return copy

    outs = []
    from_bo = lambda g: r.bo[:, lanes_of(g)]
    all_sum(1, r.lsum, r.gsum, [
        lambda: unpermute(0, 8, from_bo),
        lambda: (unpermute(8, 12, from_bo), outs.append(write_out(r.raw, r.out_hbm, 0))),
    ])

    def gtile(t, carry):
        lanes = lanes_of(t)
        avg = r.sums[row_of(0, t)] / TOTAL
        inv = lax.rsqrt(r.sums[row_of(1, t)] / TOTAL - avg * avg + EPSILON)
        scale = r.par[row_of(0, t)] * inv
        c1 = r.gsum[row_of(1, t)] / TOTAL
        c2 = r.gsum[row_of(0, t)] / TOTAL
        normed = (r.hid[:, lanes].astype(F32) - avg) * inv
        gh = scale * (r.ga[:, lanes] - c1 - normed * c2)
        store_shifts(r.ghb, jnp.where(valid, gh, 0.0), lanes)
        return carry

    lax.fori_loop(0, 13, gtile, 0)
    r.eg[...] = dot(tap_concat(r.ghb, lanes_of(12), True), r.ry[...]).astype(BF)
    g12 = r.ghb[1, 1:15, :, 1536:1664].reshape(ROWS, 128)
    r.g12t[...] = g12.astype(F32).T.astype(BF)

    st, r0 = r.st, r.r0

    turns = (2, 1, 3, 0)
    low, high = pl.ds(0, 256), pl.ds(256, 256)

    def place_of(ay, ax, half):
        yy, xx = (y + ay) % 4, (x + ax) % 4
        return yy * (1 - half) + xx * half, xx * (1 - half) + yy * half

    def core_copy(ay, ax):
        pv, pu = place_of(ay, ax, 1 - c)
        return pltpu.make_async_remote_copy(
            src_ref=st.at[1 - c, pv, pu], dst_ref=r0.at[pv, pu],
            send_sem=r.s_c.at[4 * ay + ax], recv_sem=r.r_c.at[4 * ay + ax],
            device_id=sib, device_id_type=MESH,
        )

    def ring(m, ru):
        rv, rows, dst, way = (
            (2, low, r.ra.at[ru], 1),
            (2, high, r.rb.at[ru], 3),
            (1, high, r.rp.at[ru, high], 1),
            (1, low, r.rp.at[ru, low], 1),
            (3, low, r.rm.at[ru, low], 3),
            (3, high, r.rm.at[ru, high], 3),
        )[m]
        return pltpu.make_async_remote_copy(
            src_ref=r0.at[(v + rv) % 4, (u + ru) % 4, rows], dst_ref=dst,
            send_sem=r.s_1.at[m, ru], recv_sem=r.r_1.at[m, ru],
            device_id=at_v((v + way) % 4), device_id_type=MESH,
        )

    def launch(rv, ru):
        for m in {2: (0, 1), 1: (2,), 3: (4,), 0: ()}[rv]:
            ring(m, ru).start()

    def add_core(ay):
        for ax in turns:
            core_copy(ay, ax).wait_recv()
            pv, pu = place_of(ay, ax, c)

            def add(n, carry):
                row = pl.ds(pl.multiple_of(n * 128, 128), 128)
                total = st[c, pv, pu, row, :].astype(F32) + r0[pv, pu, row, :].astype(F32)
                r0[pv, pu, row, :] = total.astype(BF)
                return carry

            lax.fori_loop(0, 4, add, 0)
            if ax == ay:
                launch(ay, ax)
            else:
                @pl.when(c == 0)
                def _():
                    launch(ay, ax)

                @pl.when(c == 1)
                def _():
                    launch(ax, ay)

    def add_half(ru, m, buf, rv, start):
        ring(m, ru).wait_recv()
        pv, pu = (v + rv) % 4, (u + ru) % 4
        for n in range(2):
            row, own = pl.ds(128 * n, 128), pl.ds(start + 128 * n, 128)
            total = r0[pv, pu, own, :].astype(F32) + buf[ru, row, :].astype(F32)
            r0[pv, pu, own, :] = total.astype(BF)

    def relay(ru):
        add_half(ru, 0, r.ra, 1, 0)
        ring(3, ru).start()
        add_half(ru, 1, r.rb, 3, 256)
        ring(5, ru).start()

    def wstep(k):
        yy = (y + turns[k]) % 4
        acc[0:144, :] = jnp.zeros((144, 128), F32)
        r.mec[...] = jnp.zeros_like(r.mec)
        lhs12 = r.g12t[rows_at(16 * yy, 16), :]
        for gg in range(3):
            g = 3 * yy + gg
            main = r.ghb[1, 1:15, :, lanes_of(g)].reshape(ROWS, 128)
            lhs = jnp.concatenate([main.astype(F32).T.astype(BF), lhs12], axis=0)
            a = tap_concat(r.xb, lanes_of(g), False, r.ex[:, lanes_of(yy)])
            p = dot(lhs, a)
            for tap in range(9):
                px, pos = piece_of(gg * 9 + tap)
                blk = p[0:128, tap * 128 : tap * 128 + 128].astype(BF)
                st[0, yy, px, pos * 64 : pos * 64 + 64, :] = blk[0:64]
                st[1, px, yy, pos * 64 : pos * 64 + 64, :] = blk[64:128]
            rowsel = (lax.broadcasted_iota(jnp.int32, (16, 1152), 0) // 4) == gg
            r.mec[...] += jnp.where(rowsel, p[128:144, 0:1152], 0.0)
            lane = lane_iota(144)
            lanesel = (lane >= 36 * gg) & (lane < 36 * gg + 36)
            row = lax.broadcasted_iota(jnp.int32, (144, 128), 0)
            rowsel = (row < 128) | (row // 4 == 32 + gg)
            acc[0:144, :] += jnp.where(lanesel & rowsel, p[:, 1152:1280], 0.0)
        zeros = jnp.zeros((128, 128), BF)
        for px in range(3):
            for j in range(3):
                tap = 3 * px + j
                st[0, yy, px, 448 + 16 * j : 464 + 16 * j, :] = r.mec[:, 128 * tap : 128 * tap + 128].astype(BF)
            st[1, px, yy, 448:496, :] = acc[48 * px : 48 * px + 48, :].astype(BF)
            st[0, yy, px, 496:512, :] = zeros[0:16]
            st[1, px, yy, 496:512, :] = zeros[0:16]
        st[0, yy, 3, 384:512, :] = zeros
        st[1, 3, yy, 384:512, :] = zeros
        for ax in turns:
            core_copy(turns[k], ax).start()
        if k > 0:
            add_core(turns[k - 1])

    for k in range(4):
        wstep(k)
    add_core(turns[3])

    def back_part(yy, lo, hi):
        block = pl.ds(128 + 16 * yy, 16)
        wt = r.wt

        def bstep(gg, carry):
            g = 3 * yy + gg
            for tap in range(9):
                wt[0:128, 128 * tap : 128 * tap + 128] = r.bm[g, 128 * tap : 128 * tap + 128, :]
            lane = lane_iota(128)
            lanesel = (lane >= 36 * gg) & (lane < 36 * gg + 36)
            wt[0:128, 1152:1280] = jnp.where(lanesel, r.tr[:, lanes_of(yy)].astype(F32), 0.0).astype(BF)
            tails = r.ta[g].reshape(192, 128)
            bl = dot(r.selb[0, gg], tails).astype(BF)
            be = dot(r.selb[1, gg], tails)
            low = jnp.zeros((16, 128), F32)
            lane = lane_iota(16)
            for tap in range(9):
                wt[block, 128 * tap : 128 * tap + 128] = bl[16 * tap : 16 * tap + 16]
                low = jnp.where((lane // 4) == 9 * gg + tap, be[16 * tap : 16 * tap + 16], low)
            wt[block, 1152:1280] = low.astype(BF)
            a = tap_concat(r.ghb, lanes_of(g), True, r.eg[:, lanes_of(yy)])
            p = dot(a, wt[...], ((1,), (1,)))
            r.gs[:, lanes_of(g)] += p[:, :128]
            r.gs[:, 1536:1664] += p[:, 128:]
            return carry

        lax.fori_loop(lo, hi, bstep, 0)
        if hi == 3:
            wt[block, :] = jnp.zeros((16, 1280), BF)

    u_copies = []

    def sum_v(ru):
        for m in range(2, 6):
            ring(m, ru).wait_recv()
        pu = (u + ru) % 4
        for n in range(4):
            row = pl.ds(128 * n, 128)
            total = r0[v, pu, row, :].astype(F32) + r.rp[ru, row, :].astype(F32)
            r.cur2[ru, row, :] = (total + r.rm[ru, row, :].astype(F32)).astype(BF)
        if ru:
            u_copies.append(
                send(r.cur2.at[ru], r.r2.at[ru - 1], r.s_2.at[ru - 1], r.r_2.at[ru - 1], at_u(pu))
            )

    parts = [(yy, lo, hi) for yy in range(4) for lo, hi in ((0, 1), (1, 2), (2, 3))]

    def back_next(n=1):
        for _ in range(n):
            if parts:
                back_part(*parts.pop(0))

    for ru in turns:
        back_next()
        relay(ru)
    back_next()
    for ru in turns:
        back_next()
        sum_v(ru)
    back_next()
    from_gs = lambda g: r.gs[:, lanes_of(g)].astype(BF)
    for t in range(13):
        for n in range(2):
            for k, part in enumerate(split3(r.gsum[n, t : t + 1, :])):
                r.pf[3 * n + k : 3 * n + k + 1, lanes_of(t)] = part
    r.pn[...] = r.pf[...].astype(BF)
    for copy in u_copies:
        copy.wait_recv()
    sends += u_copies
    for n in range(8):
        row = pl.ds(64 * n, 64)
        total = r.cur2[0, row, :].astype(F32)
        for rel in range(3):
            total = total + r.r2[rel, row, :].astype(F32)
        r.cur3[n] = total.astype(BF)
    copies = []
    for k in range(1, 8):
        q = (z + k) % 8
        copies.append(send(r.cur3.at[q], r.r3.at[k - 1], r.s_3.at[k - 1], r.r_3.at[k - 1], device(x, y, q, c)))
    sends += copies
    back_next(12)
    for copy in copies:
        copy.wait_recv()
    total = r.cur3[z].astype(F32)
    for k in range(7):
        total = total + r.r3[k].astype(F32)
    hh = r.hh
    hh[c, x, z] = total.astype(BF)
    here = hh.at[c, x, z]
    copies = []
    for k in range(1, 8):
        q = (z + k) % 8
        copies.append(send(here, here, r.s_4.at[k - 1], r.r_4.at[k - 1], device(x, y, q, c)))
    sends += copies
    unpermute(0, 8, from_gs)
    for copy in copies:
        copy.wait_recv()
    near = [(1, 6 - 3 * (x % 2) - 3 * (x // 3)), (3, 3 - 3 * (x % 2))]
    copies = [send(hh.at[c, x], hh.at[c, x], r.s_5.at[0], r.r_5.at[0], sib)]
    n = 1
    for cc in (c, 1 - c):
        for rel, pos in near:
            to = device((x + rel) % 4, y, z, cc)
            copies.append(send(hh.at[c, x, pos], hh.at[c, x, pos], r.s_5.at[n], r.r_5.at[n], to))
            copies.append(send(hh.at[c, x, 7], hh.at[c, x, 7], r.s_5.at[n + 1], r.r_5.at[n + 1], to))
            n += 2
        to = device((x + 2) % 4, y, z, cc)
        copies.append(send(hh.at[c, x, 7], hh.at[c, x, 7], r.s_5.at[n], r.r_5.at[n], to))
        n += 1
    unpermute(8, 12, from_gs)
    outs.append(write_out(r.raw2, r.ig_hbm, 1))
    r.gg_out[...] = r.og[0:1, 0:1584].reshape(1584)
    r.bg_out[...] = r.og[1:2, 0:1584].reshape(1584)
    for copy in copies:
        copy.wait_recv()
    sends += copies
    sp = (z % 2) * 8 + x * 2 + c
    b0 = (sp * 29403) // 17424 - sp // 15
    em = jnp.concatenate([hh[1, j, 7, 0:48, :] for j in range(3)], axis=0)
    for k in range(3):
        b = b0 + k
        px, pos = piece_of(b)
        tap = b % 9
        gg = b // 9
        main = jnp.concatenate([hh[0, px, pos], hh[1, px, pos]], axis=0)
        mrow = hh[0, tap // 3, 7, rows_at(16 * (tap % 3), 16), :]
        left = jnp.concatenate([main, mrow], axis=0)
        line = lax.broadcasted_iota(jnp.int32, (128, 136), 0) - (36 * gg + 4 * tap)
        unit = lax.broadcasted_iota(jnp.int32, (128, 136), 1)
        qe = jnp.where((line >= 0) & (line < 4) & (unit == 33 * line + 32), 1.0, 0.0).astype(BF)
        t1 = (dot(left, r.qm[...]) + dot(em, qe)).astype(BF)
        t2 = dot(t1, r.qo[gg], ((0,), (0,)))
        r.kgs[132 * k : 132 * k + 132, 0:GW] = t2[0:132]

    lane = lane_iota(32)
    skip = 4 * lax.broadcasted_iota(jnp.int32, (32, 128), 0)
    for k in range(13):
        rows = r.kgs[32 * k : 32 * k + 32, :]
        body = pltpu.roll(rows[:, 0:128], 0, 1, stride=4, stride_axis=0)
        rest = pltpu.roll(rows[:, 128:256], 0, 1, stride=4, stride_axis=0)
        head = jnp.where(lane >= skip, body, 0.0)
        tail = jnp.where(lane < skip, body, jnp.where(lane < skip + 4, rest, 0.0))
        r.kg[33 * k : 33 * k + 32, :] = head
        r.kg[33 * k + 32 : 33 * k + 33, :] = jnp.zeros((1, 128), F32)
        r.kg[33 * k + 1 : 33 * k + 33, :] += tail

    for copy in sends:
        copy.wait_send()
    for ay in range(4):
        for ax in range(4):
            core_copy(ay, ax).wait_send()
    for m in range(6):
        for ru in range(4):
            ring(m, ru).wait_send()
    for copy in outs:
        copy.wait()


def mega(idx, tiles, gain, bias, xt, upt):
    k = constants()
    operands = [idx, tiles, *prep_constants(), gain, bias]
    operands += [k["pg"], k["ry"], k["selm"], k["sele"], k["selb"], *fin_constants(), xt, upt]
    anywhere = pl.BlockSpec(memory_space=pl.ANY)
    return pl.pallas_call(
        mega_body,
        in_specs=[pl.BlockSpec(memory_space=pltpu.SMEM)] + [vspec()] * 9 + [anywhere] * 9,
        out_specs=[anywhere, anywhere, vspec(), vspec(), vspec()],
        out_shape=[
            struct((14, 14, 2, 1584), BF),
            struct((14, 14, 2, 1584), BF),
            struct((432, 128), F32),
            struct((1584,), F32),
            struct((1584,), F32),
        ],
        scratch_shapes=list(scratch_list().values()),
        compiler_params=pltpu.CompilerParams(
            collective_id=1, has_side_effects=True, vmem_limit_bytes=VLIM
        ),
        name="block",
    )(*operands)


def finish_body(*refs):
    srcs, dsts, mids, sem = refs[0:4], refs[4:8], refs[8:12], refs[12]
    loads = [pltpu.make_async_copy(a, b, sem.at[0, n]) for n, (a, b) in enumerate(zip(srcs, mids))]
    saves = [pltpu.make_async_copy(a, b, sem.at[1, n]) for n, (a, b) in enumerate(zip(mids, dsts))]
    for load in loads:
        load.start()
    for load, save in zip(loads, saves):
        load.wait()
        save.start()
    for save in saves:
        save.wait()


def finish(*arrays):
    anywhere = pl.BlockSpec(memory_space=pl.ANY)
    return pl.pallas_call(
        finish_body,
        in_specs=[anywhere] * 4,
        out_specs=[anywhere] * 4,
        out_shape=[struct(a.shape, a.dtype) for a in arrays],
        scratch_shapes=[VM(a.shape, a.dtype) for a in arrays] + [DMA((2, 4))],
        name="finish",
    )(*arrays)


def tile_rows(tile_counts, owner_order):
    ranks = jnp.arange(64, dtype=jnp.int32)
    before = (ranks[None, :] < ranks[:, None]).astype(jnp.int32)
    run_start = jnp.sum(before * tile_counts[None, :], axis=1)
    j = jnp.arange(144, dtype=jnp.int32)[:, None] - run_start[None, :]
    s = owner_order[None, :]
    y, zl, x, core = s // 16, (s // 8) % 2, (s // 2) % 4, s % 2
    vu = jnp.where(j < 2, y * 4 + x, x * 4 + y)
    spot = (j // 2) * 128 + vu * 8 + zl * 4 + core * 2 + j % 2
    held = (j >= 0) & (j < tile_counts[None, :])
    return jnp.sum(jnp.where(held, spot, 0), axis=1)


def local(block_input, upstream, kernel_tiles, tile_counts, owner_order, gain, bias):
    idx = tile_rows(tile_counts, owner_order)
    turn = lambda a: jnp.transpose(a, (1, 2, 0, 3))
    back = lambda a: jnp.transpose(a, (2, 0, 1, 3))
    out, ig, kg, gg, bg = mega(
        idx, kernel_tiles.reshape(4, 99, GW), gain, bias,
        turn(block_input), turn(upstream),
    )
    out, ig, gg, bg = finish(out, ig, gg, bg)
    sp = lax.axis_index("shard") % 16
    b0 = (sp * 29403) // 17424 - sp // 15
    kernel_grad = lax.dynamic_slice(kg.reshape(-1), (sp * 29403 - b0 * 17424,), (29403,))
    return (back(out), back(ig), kernel_grad, gg, bg)


def solution(mesh):
    return jax.shard_map(
        local,
        mesh=mesh,
        in_specs=(
            P(("dp", "shard"), None, None, None),
            P(("dp", "shard"), None, None, None),
            P("shard", None),
            P(),
            P(),
            P(),
            P(),
        ),
        out_specs=(
            P(("dp", "shard"), None, None, None),
            P(("dp", "shard"), None, None, None),
            P("shard"),
            P(),
            P(),
        ),
        check_vma=False,
    )
```
